256 devices in a mesh: sys: 4 (over y), blk: 32 (over x_lo, z, core), inst: 2 (over x_hi).
Axes of the slice: x: 4 (x_hi: 2, x_lo: 2; x = x_hi * 2 + x_lo), y: 4, z: 8, core: 2. Of those that a mesh axis runs over, the one named last changes fastest.
Arguments:
- adjoint: float32 [4, 8, 5, 512, 16, 128], P('sys', 'inst', None, 'blk'), may hold values from -6 to 6
- gradient: float32 [4, 8, 5, 512, 16, 128], P('sys', 'inst', None, 'blk'), may hold values from -6 to 6
- jacobian: float32 [4, 5, 5, 512, 16, 128], P('sys', None, None, 'blk'), may hold values from -3 to 3
- coupling: float32 [4, 6, 512, 16, 128], P('sys', None, 'blk'), may hold values from 0.1 to 0.6
- pseudo_step: float32 [4, 512, 16, 128], P('sys', 'blk'), may hold values from 0.2 to 1
- receptor_cell: int32 [4, 32, 1024], P('sys', 'blk'), may hold values from 0 to 32767
- donor_owner: int32 [4, 32, 1024, 1], P('sys', 'blk'), may hold values from 0 to 127; in each aligned block of 1024 rows (0 to 1023, 1024 to 2047, ..., all dimensions but the last counted through in order) at most 16 rows name the same one
- donor_cell: int32 [4, 32, 8, 1024], P('sys', 'blk'), may hold values from 0 to 32767
- donor_weight: float32 [4, 32, 8, 1024], P('sys', 'blk'), may hold values from 0.02 to 0.25
- block_count: int32 [4, 32, 8], P('sys', 'blk'), may hold values from 64 to 128, as said below
Outputs:
- adjoint_next: float32 [4, 8, 5, 512, 16, 128], P('sys', 'inst', None, 'blk')
The draws below stay inside these ranges and needn't reach their ends.
Inputs may be any that keep to these rules, and one draw needn't show every extreme that they name: `donor_owner`: in the 1024 rows of one block no owner is named by more than 16 rows. `block_count`: the first group of rows of block 0 of system 0 is full.
All inputs are finite; a program needn't handle non-finite values.
Results may differ from the reference program's by a relative error of at most 0.00005.
Values sent between devices are 32-bit elements; how exact they have to be, the bound alone decides.
No kernel may reach another device: no remote copies, remote signals or barrier semaphores. Data moves between devices by JAX's collectives and lax.ppermute only.
A program may use at most 128 MiB of HBM per device.

```python
import math
import jax
import jax.numpy as jnp
import numpy as np
from jax import lax

FIELDS = 5
DONORS = 8
CY = 16
CZ = 128
RECEPTORS = 1024
INSTANCES = 8
SYSTEMS = 4
BLOCKS = 32
NX = 512
CELLS = 32768
OWNERS = 128
CAP = 16
RBLOCKS = 8


def draw_block_count(key, part):
    key = jax.random.fold_in(key, 7)
    counts = jax.random.randint(key, (SYSTEMS, BLOCKS, RBLOCKS), 64, 129).astype(jnp.int32)
    counts = counts.at[0, 0, 0].set(128)
    return counts.at[SYSTEMS - 1, BLOCKS - 1, RBLOCKS - 1].set(64)


def touch_ends(result, stream_key, low, top_value):
    place = [jax.random.randint(jax.random.fold_in(stream_key, axis), (), 0, length) for axis, length in enumerate(result.shape)]
    main_axis = result.shape.index(max(result.shape))
    next_to = place[:main_axis] + [(place[main_axis] + 1) % result.shape[main_axis]] + place[main_axis + 1:]
    return result.at[tuple(place)].set(low).at[tuple(next_to)].set(top_value)


def shard_levels(stream_key, shape, split, least, largest):
    def one(position, parts):
        heights = jax.random.uniform(jax.random.fold_in(jax.random.fold_in(stream_key, 6), position), (parts,), jnp.float32, least / len(split), largest / len(split))
        return jnp.repeat(jnp.exp(heights), shape[position] // parts).reshape((-1,) + (1,) * (len(shape) - position - 1))

    loudness = one(*split[0])
    for cut in split[1:]:
        loudness = loudness * one(*cut)
    return loudness


def deal_out(key, own, number, rows, count, top, bound, skew):
    order = jax.random.permutation(key, count)
    heavy_load, common = load_shares(count, rows * top, bound, skew, True), load_shares(count, rows * top, bound, skew, False)
    places = jnp.arange(count)

    def named(lengths, rotation):
        used = int((lengths > 0).sum())
        fixed = max(1, used // 4)
        moved = fixed + (places - fixed + rotation * (used - fixed)) % max(1, count - fixed)
        return jnp.zeros((count,), jnp.int32).at[order[jnp.where(places < fixed, places, moved)]].set(jnp.asarray(lengths, jnp.int32))

    lengths = jnp.where(number % 4 == 0, named(heavy_load, number // 4), named(common, number - number // 4 - 1))
    mixed = jax.random.permutation(jax.random.fold_in(own, 3), count)
    source_of, taker = mixed[0:count // 2 * 2:2], mixed[1:count // 2 * 2:2]
    slack = jnp.minimum(lengths[source_of] - 1, bound - lengths[taker]) // 2
    slack = jnp.where((source_of == order[0]) | (taker == order[0]) | (lengths[taker] == 0), 0, jnp.maximum(slack, 0))
    moved = jax.random.randint(jax.random.fold_in(own, 4), (count // 2,), 0, 1 << 20) % (slack + 1)
    lengths = lengths.at[source_of].add(-moved).at[taker].add(moved)
    members = jnp.searchsorted(jnp.cumsum(lengths), jnp.arange(rows * top), side="right").astype(jnp.int32)
    listing = members.reshape(top, rows).T
    listing = listing[jax.random.permutation(jax.random.fold_in(own, 1), rows)]
    rotation = jax.random.randint(jax.random.fold_in(own, 2), (rows, 1), 0, top)
    return jnp.take_along_axis(listing, (jnp.arange(top)[None, :] + rotation) % top, axis=1)


def load_shares(amount, total, reach, lean, full):
    loads = [(1 << 20) // math.isqrt(rank ** lean) + 1 for rank in range(1, amount + 1)]
    largest = reach if full else min(reach, max(-(-total // amount), total * loads[0] // sum(loads)))
    least = 1 if total - largest >= amount - 1 else 0
    given, surplus = [largest] + [least] * (amount - 1), total - largest - least * (amount - 1)
    while surplus > 0:
        free = [i for i in range(1, amount) if given[i] < largest] or [i for i in range(1, amount) if given[i] < reach]
        whole, left = sum([loads[i] for i in free]), surplus
        for i in free:
            addition = min(reach - given[i], max(1, left * loads[i] // whole), surplus)
            given[i] = given[i] + addition
            surplus = surplus - addition
    return np.array(given)


def gaussian(own_key, extent, scale, most, shards=(), dtype=jnp.bfloat16):
    entries = jax.random.normal(own_key, extent, jnp.float32) * scale
    if len(shards) > 0:
        entries = shard_levels(own_key, extent, shards, -0.22, 0.18) * entries
    return jnp.clip(entries, min=-most, max=most).astype(dtype)


def setup_inputs(seed: int = 0) -> dict:
    arg_keys = jax.random.split(jax.random.key(seed), 11)
    adjoint = gaussian(arg_keys[0], (SYSTEMS, INSTANCES, FIELDS, NX, CY, CZ), 1.0, 6.0, ((0, 4), (1, 2), (3, 32)), jnp.float32)
    gradient = gaussian(arg_keys[1], (SYSTEMS, INSTANCES, FIELDS, NX, CY, CZ), 1.0, 6.0, ((0, 4), (1, 2), (3, 32)), jnp.float32)
    jacobian = gaussian(arg_keys[2], (SYSTEMS, FIELDS, FIELDS, NX, CY, CZ), 0.5, 3.0, ((0, 4), (3, 32)), jnp.float32)
    coupling = jnp.clip(0.1 + 0.5 * jax.random.uniform(arg_keys[3], (SYSTEMS, 6, NX, CY, CZ), jnp.float32) ** shard_levels(arg_keys[3], (SYSTEMS, 6, NX, CY, CZ), ((0, 4), (2, 32)), -0.2, 0.2), 0.1, 0.6)
    pseudo_step = jnp.clip(0.2 + 0.8 * jax.random.uniform(arg_keys[4], (SYSTEMS, NX, CY, CZ), jnp.float32) ** shard_levels(arg_keys[4], (SYSTEMS, NX, CY, CZ), ((0, 4), (1, 32)), -0.2, 0.2), 0.2, 1.0)
    receptor_cell = touch_ends(jax.random.randint(arg_keys[5], (SYSTEMS, BLOCKS, RECEPTORS), 0, CELLS), jax.random.fold_in(arg_keys[5], 1), 0, CELLS - 1).astype(jnp.int32)
    donor_owner_keys = jax.random.split(jax.random.fold_in(arg_keys[6], 1), SYSTEMS * BLOCKS * RECEPTORS // RECEPTORS)
    donor_owner_turns = jax.random.permutation(jax.random.fold_in(arg_keys[6], 3), SYSTEMS * BLOCKS * RECEPTORS // RECEPTORS)
    donor_owner = jax.vmap(lambda own, number: deal_out(jax.random.fold_in(arg_keys[6], 2), own, number, RECEPTORS, OWNERS, 1, CAP, 2))(donor_owner_keys, donor_owner_turns).reshape((SYSTEMS, BLOCKS, RECEPTORS, 1))
    donor_cell = touch_ends(jax.random.randint(arg_keys[7], (SYSTEMS, BLOCKS, DONORS, RECEPTORS), 0, CELLS), jax.random.fold_in(arg_keys[7], 1), 0, CELLS - 1).astype(jnp.int32)
    donor_weight = jnp.clip(0.02 + 0.23 * jax.random.uniform(arg_keys[8], (SYSTEMS, BLOCKS, DONORS, RECEPTORS), jnp.float32) ** shard_levels(arg_keys[8], (SYSTEMS, BLOCKS, DONORS, RECEPTORS), ((0, 4), (1, 32)), -0.2, 0.2), 0.02, 0.25)
    block_count = draw_block_count(jax.random.fold_in(arg_keys[10], 71), 0)
    return {"adjoint": adjoint, "gradient": gradient, "jacobian": jacobian, "coupling": coupling, "pseudo_step": pseudo_step, "receptor_cell": receptor_cell, "donor_owner": donor_owner, "donor_cell": donor_cell, "donor_weight": donor_weight, "block_count": block_count}


ROTOR_RATE = 0.6


def spectral_table(number):
    indices = jnp.arange(number)
    offset = (indices[:, None] - indices[None, :]) % number
    angles = jnp.pi * offset.astype(jnp.float32) / number
    parity = 1.0 - 2.0 * (offset % 2).astype(jnp.float32)
    sines = jnp.where(offset == 0, 1.0, jnp.sin(angles))
    return jnp.where(offset == 0, 0.0, 0.5 * parity * jnp.cos(angles) / sines).astype(jnp.float32)


def reference(adjoint, gradient, jacobian, coupling, pseudo_step, receptor_cell, donor_owner, donor_cell, donor_weight, block_count):
    summed = jnp.zeros_like(adjoint)
    for field_in in range(FIELDS):
        summed = summed + jacobian[:, None, field_in] * adjoint[:, :, field_in:field_in + 1]
    padded = jnp.pad(adjoint, ((0, 0), (0, 0), (0, 0), (1, 1), (1, 1), (1, 1)))
    shifted = [padded[:, :, :, 2:, 1:-1, 1:-1], padded[:, :, :, :-2, 1:-1, 1:-1],
               padded[:, :, :, 1:-1, 2:, 1:-1], padded[:, :, :, 1:-1, :-2, 1:-1],
               padded[:, :, :, 1:-1, 1:-1, 2:], padded[:, :, :, 1:-1, 1:-1, :-2]]
    for direction in range(6):
        summed = summed - coupling[:, direction][:, None, None] * shifted[direction]
    spectra = spectral_table(INSTANCES)
    spectral = jnp.einsum('st,xsfabc->xtfabc', spectra, adjoint, precision=lax.Precision.HIGHEST)
    summed = summed + ROTOR_RATE * spectral
    channels = INSTANCES * FIELDS
    flat_rows = adjoint.reshape(SYSTEMS, channels, BLOCKS, CELLS).transpose(0, 2, 1, 3)
    picked = jnp.take_along_axis(flat_rows, receptor_cell[:, :, None, :], axis=3)
    row_ids = jnp.arange(RECEPTORS)
    living = ((row_ids % 128)[None, None, :] < block_count[:, :, row_ids // 128]).astype(jnp.float32)
    picked = picked * living[:, :, None, :]
    base_cell = donor_owner[:, :, :, 0] * CELLS
    fringe = jnp.zeros((channels, SYSTEMS * BLOCKS * CELLS), jnp.float32)
    for donor in range(DONORS):
        targets = (base_cell + donor_cell[:, :, donor, :]).reshape(-1)
        values = (donor_weight[:, :, donor, None, :] * picked).transpose(2, 0, 1, 3).reshape(channels, -1)
        fringe = fringe.at[:, targets].add(values)
    fringe = fringe.reshape(INSTANCES, FIELDS, SYSTEMS, NX, CY, CZ).transpose(2, 0, 1, 3, 4, 5)
    residual = summed + fringe - gradient
    return adjoint - pseudo_step[:, None, None] * residual
```

```python
import functools
import math

import jax
import jax.numpy as jnp
from jax import lax
from jax.experimental import pallas as pl
from jax.experimental.pallas import tpu as pltpu
from jax.sharding import Mesh, PartitionSpec as P

ROTOR_RATE = 0.6
F32 = jnp.float32
BF16 = jnp.bfloat16

FIELDS = 5
INSTANCES = 8
LOCAL = 4
CH = LOCAL * FIELDS
HI = 256
LO = 128
ROWS = 1024
CAP = 16
SLOT = 40
PIECE = CAP * SLOT // LO
FIRST = 3
ACCS = 4


def spectra_entry(offset):
    offset %= INSTANCES
    if offset == 0:
        return 0.0
    angle = math.pi * offset / INSTANCES
    return 0.5 * (-1.0) ** offset * math.cos(angle) / math.sin(angle)


def iota(shape, dim):
    return lax.broadcasted_iota(jnp.int32, shape, dim)


def split(x):
    head = x.astype(BF16)
    return head, (x - head.astype(F32)).astype(BF16)


def nt_dot(a, b):
    return lax.dot_general(a, b, (((1,), (1,)), ((), ())), preferred_element_type=F32)


def pack_kernel(meta, adj, cell, owner, donor, weight, keep, send, payload):
    spot = cell[...]
    high = spot >> 7
    low = spot & 127
    wide = 256
    for part in range(ROWS // wide):
        cols = slice(part * wide, (part + 1) * wide)
        lows = jnp.where(iota((LO, wide), 0) == low[:, cols], 1.0, 0.0).astype(BF16)
        lows = jnp.concatenate([lows, lows], axis=0)
        here = iota((HI, wide), 0) == high[:, cols]
        for channel in range(CH):
            head, tail = split(adj[channel])
            found = jnp.dot(
                jnp.concatenate([head, tail], axis=1), lows, preferred_element_type=F32
            )
            payload[channel : channel + 1, cols] = jnp.sum(
                jnp.where(here, found, 0.0), axis=0, keepdims=True
            )
    payload[CH:24, :] = jnp.zeros((24 - CH, ROWS), F32)
    payload[24:32, :] = weight[...]
    payload[32:40, :] = donor[...].astype(F32)

    name = owner[...]
    mine = meta[0]
    other = ((name >> 4) & 1) ^ mine
    name = (other << 6) | ((name >> 5) << 4) | (name & 15)
    upto = jnp.where(iota((LO, LO), 0) <= iota((LO, LO), 1), 1.0, 0.0).astype(BF16)
    ones = jnp.ones((LO, LO), BF16)
    before = jnp.zeros((LO, LO), F32)
    chosen, ranks = [], []
    for group in range(ROWS // LO):
        lanes = slice(group * LO, (group + 1) * LO)
        hit = (iota((LO, LO), 0) == name[:, lanes]) & (iota((LO, LO), 1) < meta[1 + group])
        hit = jnp.where(hit, 1.0, 0.0)
        hit16 = hit.astype(BF16)
        count = jnp.dot(hit16, upto, preferred_element_type=F32) + before
        before = before + jnp.dot(hit16, ones, preferred_element_type=F32)
        ranks.append(jnp.sum(hit * count, axis=0, keepdims=True) - 1.0)
        chosen.append(hit16)
    chosen = jnp.concatenate(chosen, axis=1)
    rank = jnp.concatenate(ranks, axis=1)
    rows = payload[...]
    placed = jnp.concatenate(
        [jnp.where(rank == float(slot), rows, 0.0) for slot in range(CAP)], axis=0
    )
    head, tail = split(placed)
    table = nt_dot(head, chosen) + nt_dot(tail, chosen)
    for piece in range(PIECE):
        block = table[piece * LO : (piece + 1) * LO].T
        keep[pl.ds(piece, 64, stride=PIECE), :] = block[:64]
        send[pl.ds(piece, 64, stride=PIECE), :] = block[64:]


def local_kernel(adj, before, after, gradient, jacobian, coupling, step, out):
    planes = 2
    rows = planes * 16
    index = pl.program_id(0)
    last = pl.num_programs(0) - 1
    base = index * planes
    y = iota((rows, LO), 0) % 16
    z = iota((rows, LO), 1)
    faces = [coupling[d].reshape(rows, LO) for d in range(6)]
    faces[2] = jnp.where(y == 15, 0.0, faces[2])
    faces[3] = jnp.where(y == 0, 0.0, faces[3])
    faces[4] = jnp.where(z == LO - 1, 0.0, faces[4])
    faces[5] = jnp.where(z == 0, 0.0, faces[5])
    tau = step[...].reshape(rows, LO)
    for field in range(FIELDS):
        blocks = [jacobian[g, field].reshape(rows, LO) for g in range(FIELDS)]
        mine = [
            adj[t * FIELDS + field, pl.ds(base, planes)].reshape(rows, LO) for t in range(LOCAL)
        ]
        for t in range(LOCAL):
            channel = t * FIELDS + field
            own = mine[t]
            total = -gradient[channel].reshape(rows, LO)
            for g in range(FIELDS):
                total = total + blocks[g] * adj[t * FIELDS + g, pl.ds(base, planes)].reshape(
                    rows, LO
                )
            next_plane = jnp.where(
                index == last, after[channel], adj[channel, jnp.minimum(base + planes, 15)]
            )
            past_plane = jnp.where(
                index == 0, before[channel], adj[channel, jnp.maximum(base - 1, 0)]
            )
            total = total - faces[0] * jnp.concatenate([own[16:], next_plane], axis=0)
            total = total - faces[1] * jnp.concatenate([past_plane, own[:16]], axis=0)
            total = total - faces[2] * pltpu.roll(own, rows - 1, 0)
            total = total - faces[3] * pltpu.roll(own, 1, 0)
            total = total - faces[4] * pltpu.roll(own, LO - 1, 1)
            total = total - faces[5] * pltpu.roll(own, 1, 1)
            for s in range(LOCAL):
                if s != t:
                    total = total + (ROTOR_RATE * spectra_entry(s - t)) * mine[s]
            out[channel] = (own - tau * total).reshape(planes, 16, LO)


def fringe_kernel(rows, partial, step, out, *scratch):
    accs = scratch[:ACCS]
    flat, expand, places, indices, products, sem = scratch[ACCS:]
    for piece in range(PIECE):
        flat[pl.ds(piece * LO, LO), :] = rows[pl.ds(piece, LO, stride=PIECE), :].T
    for slot in range(CAP):
        spot = flat[slot * SLOT + 32 : slot * SLOT + 40, :].astype(jnp.int32)
        places[slot * 8 : slot * 8 + 8, :] = ((spot >> 9) << 7) | (spot & 127)
    copy = pltpu.make_async_copy(places, indices, sem)
    copy.start()

    zeros = jnp.zeros((64, LO), F32)

    @pl.loop(0, 8192 // 64)
    def _(i):
        for acc in accs:
            acc[pl.ds(pl.multiple_of(i * 64, 64), 64), :] = zeros

    row = iota((LO, LO), 0)
    lane = iota((LO, LO), 1)
    value_row = jnp.where(row < 24, row, row - 24)
    hit = (row < 48) & (value_row == lane // 4)
    expand[:, 0:LO] = jnp.where(hit, 1.0, 0.0).astype(BF16)
    weight_row = jnp.where(row < 80, row - 48, row - 80)
    for k in range(8):
        hit = (row >= 48) & (row < 112) & (weight_row == (lane % 4) * 8 + k)
        expand[:, (k + 1) * LO : (k + 2) * LO] = jnp.where(hit, 1.0, 0.0).astype(BF16)
    copy.wait()

    @pl.loop(0, CAP)
    def _(slot):
        base = pl.multiple_of(slot * SLOT, 8)
        values = flat[pl.ds(base, 24), :]
        weights = flat[pl.ds(base + 24, 8), :]
        quarter = (flat[pl.ds(base + 32, 8), :].astype(jnp.int32) >> 7) & 3
        weights = jnp.concatenate(
            [jnp.where(quarter == q, weights, 0.0) for q in range(4)], axis=0
        )
        values_head = values.astype(BF16).astype(F32)
        weights_head = weights.astype(BF16).astype(F32)
        left = jnp.concatenate(
            [
                values_head,
                values - values_head,
                weights_head,
                weights - weights_head,
                jnp.zeros((16, LO), F32),
            ],
            axis=0,
        )
        both = jnp.dot(left.T.astype(BF16), expand[...], preferred_element_type=F32)
        for k in range(8):
            products[k] = both[:, 0:LO] * both[:, (k + 1) * LO : (k + 2) * LO]

        unroll = 8

        @pl.loop(0, LO // unroll)
        def _(chunk):
            for u in range(unroll):
                source = chunk * unroll + u
                for k in range(8):
                    acc = accs[k % ACCS]
                    place = indices[slot * 8 + k, source]
                    acc[pl.ds(place, 1), :] = (
                        acc[pl.ds(place, 1), :] + products[k, pl.ds(source, 1), :]
                    )

    @pl.loop(0, HI // 8)
    def _(i):
        turned = []
        for half in range(2):
            begin = pl.multiple_of(i * 256 + half * LO, LO)
            total = accs[0][pl.ds(begin, LO), :]
            for acc in accs[1:]:
                total = total + acc[pl.ds(begin, LO), :]
            turned.append(total.T)
        here = pl.ds(pl.multiple_of(i * 8, 8), 8)
        tau = step[here, :]
        for channel in range(CH):
            cells = slice(channel * 4, channel * 4 + 4)
            gained = jnp.concatenate([turned[0][cells], turned[1][cells]], axis=0)
            out[channel, here, :] = partial[channel, here, :] - tau * gained


def final_kernel(partial, first, rest, step, out):
    tau = step[...]
    for field in range(FIELDS):
        remote = []
        for s in range(LOCAL):
            channel = s * FIELDS + field
            remote.append(first[channel] if channel < FIRST else rest[channel - FIRST])
        for t in range(LOCAL):
            total = None
            for s in range(LOCAL):
                factor = ROTOR_RATE * spectra_entry(s - t + LOCAL)
                if s == t:
                    continue
                term = factor * remote[s]
                total = term if total is None else total + term
            channel = t * FIELDS + field
            out[channel] = partial[channel] - tau * total


def shards(
    adjoint,
    gradient,
    jacobian,
    coupling,
    pseudo_step,
    receptor_cell,
    donor_owner,
    donor_cell,
    donor_weight,
    block_count,
):
    swap = [(0, 1), (1, 0)]
    blocks = lax.axis_size("xl") * lax.axis_size("zc")
    cells = adjoint.reshape(CH, HI, LO)
    planes = adjoint.reshape(CH, 16, 16, LO)
    vmem = pl.BlockSpec(memory_space=pltpu.VMEM)
    smem = pl.BlockSpec(memory_space=pltpu.SMEM)

    first = lax.ppermute(cells[:FIRST], "inst", swap)

    meta = jnp.concatenate(
        [lax.axis_index("xl").astype(jnp.int32).reshape(1), block_count.reshape(8)]
    )
    keep, send = pl.pallas_call(
        pack_kernel,
        out_shape=[jax.ShapeDtypeStruct((64 * PIECE, LO), F32)] * 2,
        in_specs=[smem] + [vmem] * 5,
        out_specs=[vmem] * 2,
        scratch_shapes=[pltpu.VMEM((SLOT, ROWS), F32)],
        compiler_params=pltpu.CompilerParams(vmem_limit_bytes=32 * 2**20),
        name="pack",
    )(
        meta,
        cells,
        receptor_cell.reshape(1, ROWS),
        donor_owner.reshape(1, ROWS),
        donor_cell.reshape(8, ROWS),
        donor_weight.reshape(8, ROWS),
    )
    got = lax.ppermute(send, "xl", swap)

    tail, ends, _ = lax.optimization_barrier((cells[FIRST:], (planes[:, 15], planes[:, 0]), keep))
    before = lax.ppermute(ends[0], ("xl", "zc"), [(i, i + 1) for i in range(blocks - 1)])
    after = lax.ppermute(ends[1], ("xl", "zc"), [(i + 1, i) for i in range(blocks - 1)])
    rest = lax.ppermute(tail, "inst", swap)

    message = jnp.concatenate(
        [keep.reshape(64, PIECE, LO), got.reshape(64, PIECE, LO)], axis=1
    ).reshape(-1)
    arrived = lax.all_to_all(message, ("sys", "zc"), split_axis=0, concat_axis=0, tiled=True)

    steps = 8
    wide = 16 // steps
    partial = pl.pallas_call(
        local_kernel,
        grid=(steps,),
        out_shape=jax.ShapeDtypeStruct((CH, 16, 16, LO), F32),
        in_specs=[
            vmem,
            vmem,
            vmem,
            pl.BlockSpec((CH, wide, 16, LO), lambda i: (0, i, 0, 0)),
            pl.BlockSpec((FIELDS, FIELDS, wide, 16, LO), lambda i: (0, 0, i, 0, 0)),
            pl.BlockSpec((6, wide, 16, LO), lambda i: (0, i, 0, 0)),
            pl.BlockSpec((wide, 16, LO), lambda i: (i, 0, 0)),
        ],
        out_specs=pl.BlockSpec((CH, wide, 16, LO), lambda i: (0, i, 0, 0)),
        compiler_params=pltpu.CompilerParams(vmem_limit_bytes=32 * 2**20),
        cost_estimate=pl.CostEstimate(
            flops=40 * CH * HI * LO, bytes_accessed=12 * 2**20, transcendentals=0
        ),
        name="local",
    )(
        planes,
        before,
        after,
        gradient.reshape(CH, 16, 16, LO),
        jacobian.reshape(FIELDS, FIELDS, 16, 16, LO),
        coupling.reshape(6, 16, 16, LO),
        pseudo_step.reshape(16, 16, LO),
    )

    tau = pseudo_step.reshape(HI, LO)
    partial = pl.pallas_call(
        fringe_kernel,
        out_shape=jax.ShapeDtypeStruct((CH, HI, LO), F32),
        in_specs=[vmem] * 3,
        out_specs=vmem,
        scratch_shapes=[pltpu.VMEM((8192, LO), F32)] * ACCS
        + [
            pltpu.VMEM((CAP * SLOT, LO), F32),
            pltpu.VMEM((LO, 9 * LO), BF16),
            pltpu.VMEM((LO, LO), jnp.int32),
            pltpu.SMEM((LO, LO), jnp.int32),
            pltpu.VMEM((8, LO, LO), F32),
            pltpu.SemaphoreType.DMA,
        ],
        compiler_params=pltpu.CompilerParams(vmem_limit_bytes=40 * 2**20),
        name="fringe",
    )(arrived.reshape(128 * PIECE, LO), partial.reshape(CH, HI, LO), tau)

    steps = 4
    wide = HI // steps
    result = pl.pallas_call(
        final_kernel,
        grid=(steps,),
        out_shape=jax.ShapeDtypeStruct((CH, HI, LO), F32),
        in_specs=[
            pl.BlockSpec((CH, wide, LO), lambda i: (0, i, 0)),
            pl.BlockSpec((FIRST, wide, LO), lambda i: (0, i, 0)),
            pl.BlockSpec((CH - FIRST, wide, LO), lambda i: (0, i, 0)),
            pl.BlockSpec((wide, LO), lambda i: (i, 0)),
        ],
        out_specs=pl.BlockSpec((CH, wide, LO), lambda i: (0, i, 0)),
        compiler_params=pltpu.CompilerParams(vmem_limit_bytes=32 * 2**20),
        name="final",
    )(partial, first, rest, tau)
    return result.reshape(adjoint.shape)


def solution(mesh):
    fine = Mesh(mesh.devices.reshape(4, 2, 16, 2), ("sys", "xl", "zc", "inst"))
    blk = ("xl", "zc")
    return jax.shard_map(
        shards,
        mesh=fine,
        in_specs=(
            P("sys", "inst", None, blk, None, None),
            P("sys", "inst", None, blk, None, None),
            P("sys", None, None, blk, None, None),
            P("sys", None, blk, None, None),
            P("sys", blk, None, None),
            P("sys", blk, None),
            P("sys", blk, None, None),
            P("sys", blk, None, None),
            P("sys", blk, None, None),
            P("sys", blk, None),
        ),
        out_specs=P("sys", "inst", None, blk, None, None),
        check_vma=False,
    )
```

```python
import functools
import math

import jax
import jax.numpy as jnp
from jax import lax
from jax.experimental import pallas as pl
from jax.experimental.pallas import tpu as pltpu
from jax.sharding import Mesh, PartitionSpec as P

ROTOR_RATE = 0.6
F32 = jnp.float32
BF16 = jnp.bfloat16

FIELDS = 5
INSTANCES = 8
LOCAL = 4
CH = LOCAL * FIELDS
HI = 256
LO = 128
ROWS = 1024
CAP = 16
SLOT = 40
NEAR = 64
PIECE = CAP * SLOT // LO
ACCS = 4


def spectra_entry(offset):
    offset %= INSTANCES
    if offset == 0:
        return 0.0
    angle = math.pi * offset / INSTANCES
    return 0.5 * (-1.0) ** offset * math.cos(angle) / math.sin(angle)


def iota(shape, dim):
    return lax.broadcasted_iota(jnp.int32, shape, dim)


def split(x):
    head = x.astype(BF16)
    return head, (x - head.astype(F32)).astype(BF16)


def nt_dot(a, b):
    return lax.dot_general(a, b, (((1,), (1,)), ((), ())), preferred_element_type=F32)


def pick_kernel(counts, *refs):
    operands, (payload, top, bottom) = refs[:5], refs[5:8]
    held, sem = refs[8:13], refs[13]
    copies = [
        pltpu.make_async_copy(operand, place, sem.at[i])
        for i, (operand, place) in enumerate(zip(operands, held))
    ]
    for copy in copies:
        copy.start()
    adj, cell, owner, donor, weight = held
    for copy in copies:
        copy.wait()
    for channel in range(CH):
        top[channel] = adj[channel, HI - 16 :, :]
        bottom[channel] = adj[channel, :16, :]
    spot = cell[...]
    high = spot >> 7
    low = spot & 127
    wide = 256
    for part in range(ROWS // wide):
        cols = slice(part * wide, (part + 1) * wide)
        lows = jnp.where(iota((LO, wide), 0) == low[:, cols], 1.0, 0.0).astype(BF16)
        lows = jnp.concatenate([lows, lows], axis=0)
        here = iota((HI, wide), 0) == high[:, cols]
        for channel in range(CH):
            head, tail = split(adj[channel])
            found = jnp.dot(
                jnp.concatenate([head, tail], axis=1), lows, preferred_element_type=F32
            )
            payload[channel : channel + 1, cols] = jnp.sum(
                jnp.where(here, found, 0.0), axis=0, keepdims=True
            )
    for group in range(ROWS // LO):
        lanes = slice(group * LO, (group + 1) * LO)
        living = iota((1, LO), 1) < counts[group]
        payload[CH : CH + 1, lanes] = jnp.where(living, owner[:, lanes], -1).astype(F32)
    payload[CH + 1 : 24, :] = jnp.zeros((23 - CH, ROWS), F32)
    payload[24:32, :] = weight[...]
    payload[32:40, :] = donor[...].astype(F32)


def pack_kernel(half, position, payload, *refs):
    message = refs[-1]
    if half == 1:
        message[...] = refs[0][...]
    rows = payload[...]
    name = rows[CH : CH + 1].astype(jnp.int32)
    near = ((name >> 4) & 1) == position[0]
    name = jnp.where((name >= 0) & near, ((name >> 5) << 4) | (name & 15), -1)
    upto = jnp.where(iota((LO, LO), 0) <= iota((LO, LO), 1), 1.0, 0.0).astype(BF16)
    ones = jnp.ones((LO, LO), BF16)
    before = jnp.zeros((NEAR, LO), F32)
    chosen, ranks = [], []
    for group in range(ROWS // LO):
        lanes = slice(group * LO, (group + 1) * LO)
        hit = jnp.where(iota((NEAR, LO), 0) == name[:, lanes], 1.0, 0.0)
        hit16 = hit.astype(BF16)
        count = jnp.dot(hit16, upto, preferred_element_type=F32) + before
        before = before + jnp.dot(hit16, ones, preferred_element_type=F32)
        ranks.append(jnp.sum(hit * count, axis=0, keepdims=True) - 1.0)
        chosen.append(hit16)
    chosen = jnp.concatenate(chosen, axis=1)
    rank = jnp.concatenate(ranks, axis=1)
    placed = jnp.concatenate(
        [jnp.where(rank == float(slot), rows, 0.0) for slot in range(CAP)], axis=0
    )
    head, tail = split(placed)
    table = nt_dot(head, chosen) + nt_dot(tail, chosen)
    for piece in range(PIECE):
        block = table[piece * LO : (piece + 1) * LO].T
        message[pl.ds(half * PIECE + piece, NEAR, stride=2 * PIECE), :] = block
        if half == 0:
            message[pl.ds(PIECE + piece, NEAR, stride=2 * PIECE), :] = jnp.zeros((NEAR, LO), F32)


def local_kernel(adj, below, above, before, after, gradient, jacobian, coupling, step, out):
    planes = 2
    rows = planes * 16
    index = pl.program_id(0)
    last = pl.num_programs(0) - 1
    y = iota((rows, LO), 0) % 16
    z = iota((rows, LO), 1)
    faces = [coupling[d].reshape(rows, LO) for d in range(6)]
    faces[2] = jnp.where(y == 15, 0.0, faces[2])
    faces[3] = jnp.where(y == 0, 0.0, faces[3])
    faces[4] = jnp.where(z == LO - 1, 0.0, faces[4])
    faces[5] = jnp.where(z == 0, 0.0, faces[5])
    tau = step[...].reshape(rows, LO)
    for field in range(FIELDS):
        blocks = [jacobian[g, field].reshape(rows, LO) for g in range(FIELDS)]
        mine = [
            adj[t * FIELDS + field].reshape(rows, LO) for t in range(LOCAL)
        ]
        for t in range(LOCAL):
            channel = t * FIELDS + field
            own = mine[t]
            total = -gradient[channel].reshape(rows, LO)
            for g in range(FIELDS):
                total = total + blocks[g] * adj[t * FIELDS + g].reshape(rows, LO)
            next_plane = jnp.where(index == last, after[channel], above[channel, 0])
            past_plane = jnp.where(index == 0, before[channel], below[channel, 0])
            total = total - faces[0] * jnp.concatenate([own[16:], next_plane], axis=0)
            total = total - faces[1] * jnp.concatenate([past_plane, own[:16]], axis=0)
            total = total - faces[2] * pltpu.roll(own, rows - 1, 0)
            total = total - faces[3] * pltpu.roll(own, 1, 0)
            total = total - faces[4] * pltpu.roll(own, LO - 1, 1)
            total = total - faces[5] * pltpu.roll(own, 1, 1)
            for s in range(LOCAL):
                if s != t:
                    total = total + (ROTOR_RATE * spectra_entry(s - t)) * mine[s]
            out[channel] = (own - tau * total).reshape(planes, 16, LO)


def fringe_kernel(rows, partial, step, out, *scratch):
    accs = scratch[:ACCS]
    flat, expand, places, indices, products, sem = scratch[ACCS:]
    for piece in range(PIECE):
        flat[pl.ds(piece * LO, LO), :] = rows[pl.ds(piece, LO, stride=PIECE), :].T

    weights = jnp.concatenate(
        [flat[slot * SLOT + 24 : slot * SLOT + 32, :] for slot in range(CAP)], axis=0
    )
    alive = jnp.where(weights > 0.0, 1.0, 0.0)
    upto = jnp.where(iota((LO, LO), 0) <= iota((LO, LO), 1), 1.0, 0.0).astype(BF16)
    order = jnp.dot(alive.astype(BF16), upto, preferred_element_type=F32) * alive - 1.0
    order = order.astype(jnp.int32)
    places[LO : LO + 8, :] = nt_dot(jnp.ones((8, LO), BF16), alive.astype(BF16)).astype(jnp.int32)
    for slot in range(CAP):
        here = slice(slot * SLOT, (slot + 1) * SLOT)
        move = iota((LO, LO), 0) == order[slot * 8 : slot * 8 + 1]
        move = jnp.where(move, 1.0, 0.0).astype(BF16)
        old = flat[here, :]
        head = old.astype(BF16).astype(F32)
        both = nt_dot(jnp.concatenate([head, old - head], axis=0).astype(BF16), move)
        new = both[:SLOT] + both[SLOT:]
        flat[here, :] = new
        spot = new[32:40].astype(jnp.int32)
        places[slot * 8 : slot * 8 + 8, :] = ((spot >> 9) << 7) | (spot & 127)
    copy = pltpu.make_async_copy(places, indices, sem)
    copy.start()

    zeros = jnp.zeros((64, LO), F32)

    @pl.loop(0, 8192 // 64)
    def _(i):
        for acc in accs:
            acc[pl.ds(pl.multiple_of(i * 64, 64), 64), :] = zeros

    row = iota((LO, LO), 0)
    lane = iota((LO, LO), 1)
    value_row = jnp.where(row < 24, row, row - 24)
    hit = (row < 48) & (value_row == lane // 4)
    expand[:, 0:LO] = jnp.where(hit, 1.0, 0.0).astype(BF16)
    weight_row = jnp.where(row < 80, row - 48, row - 80)
    for k in range(8):
        hit = (row >= 48) & (row < 112) & (weight_row == (lane % 4) * 8 + k)
        expand[:, (k + 1) * LO : (k + 2) * LO] = jnp.where(hit, 1.0, 0.0).astype(BF16)
    copy.wait()

    @pl.loop(0, CAP)
    def _(slot):
        base = pl.multiple_of(slot * SLOT, 8)
        values = flat[pl.ds(base, 24), :]
        weights = flat[pl.ds(base + 24, 8), :]
        quarter = (flat[pl.ds(base + 32, 8), :].astype(jnp.int32) >> 7) & 3
        weights = jnp.concatenate(
            [jnp.where(quarter == q, weights, 0.0) for q in range(4)], axis=0
        )
        values_head = values.astype(BF16).astype(F32)
        weights_head = weights.astype(BF16).astype(F32)
        left = jnp.concatenate(
            [
                values_head,
                values - values_head,
                weights_head,
                weights - weights_head,
                jnp.zeros((16, LO), F32),
            ],
            axis=0,
        )
        both = jnp.dot(left.T.astype(BF16), expand[...], preferred_element_type=F32)
        for k in range(8):
            products[k] = both[:, 0:LO] * both[:, (k + 1) * LO : (k + 2) * LO]

        unroll = 8

        @pl.loop(0, (indices[LO, slot * 8] + (unroll - 1)) // unroll)
        def _(chunk):
            for u in range(unroll):
                source = chunk * unroll + u
                for k in range(8):
                    acc = accs[k % ACCS]
                    place = indices[slot * 8 + k, source]
                    acc[pl.ds(place, 1), :] = (
                        acc[pl.ds(place, 1), :] + products[k, pl.ds(source, 1), :]
                    )

    @pl.loop(0, HI // 8)
    def _(i):
        turned = []
        for half in range(2):
            begin = pl.multiple_of(i * 256 + half * LO, LO)
            total = accs[0][pl.ds(begin, LO), :]
            for acc in accs[1:]:
                total = total + acc[pl.ds(begin, LO), :]
            turned.append(total.T)
        here = pl.ds(pl.multiple_of(i * 8, 8), 8)
        tau = step[here, :]
        for channel in range(CH):
            cells = slice(channel * 4, channel * 4 + 4)
            gained = jnp.concatenate([turned[0][cells], turned[1][cells]], axis=0)
            out[channel, here, :] = partial[channel, here, :] - tau * gained


def final_kernel(partial, remote, step, out, ready, sem):
    steps = 8
    wide = HI // steps

    def copy_of(i):
        here = pl.ds(pl.multiple_of(i * wide, wide), wide)
        return pltpu.make_async_copy(ready.at[:, here, :], out.at[:, here, :], sem.at[i])

    @pl.loop(0, steps)
    def _(i):
        here = pl.ds(pl.multiple_of(i * wide, wide), wide)
        tau = step[here, :]
        for field in range(FIELDS):
            others = [remote[s * FIELDS + field, here, :] for s in range(LOCAL)]
            for t in range(LOCAL):
                total = None
                for s in range(LOCAL):
                    if s == t:
                        continue
                    term = (ROTOR_RATE * spectra_entry(s - t + LOCAL)) * others[s]
                    total = term if total is None else total + term
                channel = t * FIELDS + field
                ready[channel, here, :] = partial[channel, here, :] - tau * total
        copy_of(i).start()

    for i in range(steps):
        copy_of(i).wait()


def shards(
    adjoint,
    gradient,
    jacobian,
    coupling,
    pseudo_step,
    receptor_cell,
    donor_owner,
    donor_cell,
    donor_weight,
    block_count,
):
    swap = [(0, 1), (1, 0)]
    blocks = lax.axis_size("xl") * lax.axis_size("zc")
    cells = adjoint.reshape(CH, HI, LO)
    planes = adjoint.reshape(CH, 16, 16, LO)
    vmem = pl.BlockSpec(memory_space=pltpu.VMEM)
    smem = pl.BlockSpec(memory_space=pltpu.SMEM)

    payload, top, bottom = pl.pallas_call(
        pick_kernel,
        out_shape=[
            jax.ShapeDtypeStruct((SLOT, ROWS), F32),
            jax.ShapeDtypeStruct((CH, 16, LO), F32),
            jax.ShapeDtypeStruct((CH, 16, LO), F32),
        ],
        in_specs=[smem] + [pl.BlockSpec(memory_space=pl.ANY)] * 5,
        out_specs=[vmem] * 3,
        scratch_shapes=[
            pltpu.VMEM((CH, HI, LO), F32),
            pltpu.VMEM((1, ROWS), jnp.int32),
            pltpu.VMEM((1, ROWS), jnp.int32),
            pltpu.VMEM((8, ROWS), jnp.int32),
            pltpu.VMEM((8, ROWS), F32),
            pltpu.SemaphoreType.DMA((5,)),
        ],
        compiler_params=pltpu.CompilerParams(vmem_limit_bytes=56 * 2**20),
        name="pick",
    )(
        block_count.reshape(8),
        cells,
        receptor_cell.reshape(1, ROWS),
        donor_owner.reshape(1, ROWS),
        donor_cell.reshape(8, ROWS),
        donor_weight.reshape(8, ROWS),
    )
    got = lax.ppermute(payload, "xl", swap)
    before = lax.ppermute(top, ("xl", "zc"), [(i, i + 1) for i in range(blocks - 1)])
    after = lax.ppermute(bottom, ("xl", "zc"), [(i + 1, i) for i in range(blocks - 1)])
    whole, got, before, after = lax.optimization_barrier((cells, got, before, after))
    rest = lax.ppermute(whole, "inst", swap)

    position = lax.axis_index("xl").astype(jnp.int32).reshape(1)
    message_shape = jax.ShapeDtypeStruct((NEAR * 2 * PIECE, LO), F32)
    message = pl.pallas_call(
        functools.partial(pack_kernel, 0),
        out_shape=message_shape,
        in_specs=[smem, vmem],
        out_specs=vmem,
        compiler_params=pltpu.CompilerParams(vmem_limit_bytes=32 * 2**20),
        name="pack_own",
    )(position, payload)

    message = pl.pallas_call(
        functools.partial(pack_kernel, 1),
        out_shape=message_shape,
        in_specs=[smem, vmem, vmem],
        out_specs=vmem,
        compiler_params=pltpu.CompilerParams(vmem_limit_bytes=32 * 2**20),
        name="pack_other",
    )(position, got, message)
    message, gradient = lax.optimization_barrier((message, gradient))
    arrived = lax.all_to_all(
        message.reshape(-1), ("sys", "zc"), split_axis=0, concat_axis=0, tiled=True
    )

    steps = 8
    wide = 16 // steps
    partial = pl.pallas_call(
        local_kernel,
        grid=(steps,),
        out_shape=jax.ShapeDtypeStruct((CH, 16, 16, LO), F32),
        in_specs=[
            pl.BlockSpec((CH, wide, 16, LO), lambda i: (0, i, 0, 0)),
            pl.BlockSpec((CH, 1, 16, LO), lambda i: (0, jnp.maximum(wide * i - 1, 0), 0, 0)),
            pl.BlockSpec((CH, 1, 16, LO), lambda i: (0, jnp.minimum(wide * i + wide, 15), 0, 0)),
            vmem,
            vmem,
            pl.BlockSpec((CH, wide, 16, LO), lambda i: (0, i, 0, 0)),
            pl.BlockSpec((FIELDS, FIELDS, wide, 16, LO), lambda i: (0, 0, i, 0, 0)),
            pl.BlockSpec((6, wide, 16, LO), lambda i: (0, i, 0, 0)),
            pl.BlockSpec((wide, 16, LO), lambda i: (i, 0, 0)),
        ],
        out_specs=pl.BlockSpec((CH, wide, 16, LO), lambda i: (0, i, 0, 0)),
        compiler_params=pltpu.CompilerParams(vmem_limit_bytes=56 * 2**20),
        cost_estimate=pl.CostEstimate(
            flops=40 * CH * HI * LO, bytes_accessed=12 * 2**20, transcendentals=0
        ),
        name="local",
    )(
        planes,
        planes,
        planes,
        before,
        after,
        gradient.reshape(CH, 16, 16, LO),
        jacobian.reshape(FIELDS, FIELDS, 16, 16, LO),
        coupling.reshape(6, 16, 16, LO),
        pseudo_step.reshape(16, 16, LO),
    )

    arrived, partial = lax.optimization_barrier((arrived, partial))
    tau = pseudo_step.reshape(HI, LO)
    partial = pl.pallas_call(
        fringe_kernel,
        out_shape=jax.ShapeDtypeStruct((CH, HI, LO), F32),
        in_specs=[vmem] * 3,
        out_specs=vmem,
        scratch_shapes=[pltpu.VMEM((8192, LO), F32)] * ACCS
        + [
            pltpu.VMEM((CAP * SLOT, LO), F32),
            pltpu.VMEM((LO, 9 * LO), BF16),
            pltpu.VMEM((LO + 8, LO), jnp.int32),
            pltpu.SMEM((LO + 8, LO), jnp.int32),
            pltpu.VMEM((8, LO, LO), F32),
            pltpu.SemaphoreType.DMA,
        ],
        compiler_params=pltpu.CompilerParams(vmem_limit_bytes=40 * 2**20),
        name="fringe",
    )(arrived.reshape(128 * PIECE, LO), partial.reshape(CH, HI, LO), tau)

    result = pl.pallas_call(
        final_kernel,
        out_shape=jax.ShapeDtypeStruct((CH, HI, LO), F32),
        in_specs=[vmem] * 3,
        out_specs=pl.BlockSpec(memory_space=pl.ANY),
        scratch_shapes=[pltpu.VMEM((CH, HI, LO), F32), pltpu.SemaphoreType.DMA((8,))],
        compiler_params=pltpu.CompilerParams(vmem_limit_bytes=40 * 2**20),
        name="final",
    )(partial, rest, tau)
    return result.reshape(adjoint.shape)


def solution(mesh):
    fine = Mesh(mesh.devices.reshape(4, 2, 16, 2), ("sys", "xl", "zc", "inst"))
    blk = ("xl", "zc")
    return jax.shard_map(
        shards,
        mesh=fine,
        in_specs=(
            P("sys", "inst", None, blk, None, None),
            P("sys", "inst", None, blk, None, None),
            P("sys", None, None, blk, None, None),
            P("sys", None, blk, None, None),
            P("sys", blk, None, None),
            P("sys", blk, None),
            P("sys", blk, None, None),
            P("sys", blk, None, None),
            P("sys", blk, None, None),
            P("sys", blk, None),
        ),
        out_specs=P("sys", "inst", None, blk, None, None),
        check_vma=False,
    )
```

```python
import math

import jax
import jax.numpy as jnp
from jax import lax
from jax.experimental import pallas as pl
from jax.experimental.pallas import tpu as pltpu
from jax.sharding import Mesh, PartitionSpec as P

ROTOR_RATE = 0.6
F32 = jnp.float32
BF16 = jnp.bfloat16

FIELDS = 5
INSTANCES = 8
LOCAL = 4
CH = LOCAL * FIELDS
HI = 256
LO = 128
ROWS = 1024
CAP = 16
SLOT = 40
NEAR = 64
PIECE = CAP * SLOT // LO
FIRST = 2
ACCS = 4


def spectra_entry(offset):
    offset %= INSTANCES
    if offset == 0:
        return 0.0
    angle = math.pi * offset / INSTANCES
    return 0.5 * (-1.0) ** offset * math.cos(angle) / math.sin(angle)


def iota(shape, dim):
    return lax.broadcasted_iota(jnp.int32, shape, dim)


def split(x):
    head = x.astype(BF16)
    return head, (x - head.astype(F32)).astype(BF16)


def takes(microseconds):
    return pl.CostEstimate(flops=0, bytes_accessed=microseconds * 3_700_000, transcendentals=0)


def nt_dot(a, b):
    return lax.dot_general(a, b, (((1,), (1,)), ((), ())), preferred_element_type=F32)


def pick_kernel(counts, *refs):
    (cells, *small), (payload, top, bottom) = refs[:5], refs[5:8]
    adj, cell, owner, donor, weight, sem, small_sem = refs[8:]

    def chunk_copy(i):
        here = pl.ds(i * LOCAL, LOCAL)
        return pltpu.make_async_copy(cells.at[here], adj.at[here], sem.at[i])

    copies = [
        pltpu.make_async_copy(operand, place, small_sem.at[i])
        for i, (operand, place) in enumerate(zip(small, (cell, owner, donor, weight)))
    ]
    for copy in copies:
        copy.start()
    for i in range(FIELDS):
        chunk_copy(i).start()
    for copy in copies:
        copy.wait()
    spot = cell[...]
    high = spot >> 7
    low = spot & 127
    wide = 256
    for part in range(ROWS // wide):
        cols = slice(part * wide, (part + 1) * wide)
        lows = jnp.where(iota((LO, wide), 0) == low[:, cols], 1.0, 0.0).astype(BF16)
        lows = jnp.concatenate([lows, lows], axis=0)
        here = iota((HI, wide), 0) == high[:, cols]

        @pl.loop(0, FIELDS)
        def _(chunk):
            if part == 0:
                chunk_copy(chunk).wait()
            for i in range(LOCAL):
                channel = chunk * LOCAL + i
                head, tail = split(adj[channel])
                found = jnp.dot(
                    jnp.concatenate([head, tail], axis=1), lows, preferred_element_type=F32
                )
                payload[pl.ds(channel, 1), cols] = jnp.sum(
                    jnp.where(here, found, 0.0), axis=0, keepdims=True
                )

    for group in range(ROWS // LO):
        lanes = slice(group * LO, (group + 1) * LO)
        living = iota((1, LO), 1) < counts[group]
        payload[CH : CH + 1, lanes] = jnp.where(living, owner[:, lanes], -1).astype(F32)
    payload[CH + 1 : 24, :] = jnp.zeros((23 - CH, ROWS), F32)
    payload[24:32, :] = weight[...]
    payload[32:40, :] = donor[...].astype(F32)
    for channel in range(CH):
        top[channel] = adj[channel, HI - 16 :, :]
        bottom[channel] = adj[channel, :16, :]


def pack_kernel(position, own, got, message):
    upto = jnp.where(iota((LO, LO), 0) <= iota((LO, LO), 1), 1.0, 0.0).astype(BF16)
    ones = jnp.ones((LO, LO), BF16)
    for half, payload in enumerate((own, got)):
        rows = payload[...]
        name = rows[CH : CH + 1].astype(jnp.int32)
        near = ((name >> 4) & 1) == position[0]
        name = jnp.where((name >= 0) & near, ((name >> 5) << 4) | (name & 15), -1)
        before = jnp.zeros((NEAR, LO), F32)
        chosen, ranks = [], []
        for group in range(ROWS // LO):
            lanes = slice(group * LO, (group + 1) * LO)
            hit = jnp.where(iota((NEAR, LO), 0) == name[:, lanes], 1.0, 0.0)
            hit16 = hit.astype(BF16)
            count = jnp.dot(hit16, upto, preferred_element_type=F32) + before
            before = before + jnp.dot(hit16, ones, preferred_element_type=F32)
            ranks.append(jnp.sum(hit * count, axis=0, keepdims=True) - 1.0)
            chosen.append(hit16)
        chosen = jnp.concatenate(chosen, axis=1)
        rank = jnp.concatenate(ranks, axis=1)
        placed = jnp.concatenate(
            [jnp.where(rank == float(slot), rows, 0.0) for slot in range(CAP)], axis=0
        )
        head, tail = split(placed)
        table = nt_dot(head, chosen) + nt_dot(tail, chosen)
        for piece in range(PIECE):
            block = table[piece * LO : (piece + 1) * LO].T
            message[pl.ds(half * PIECE + piece, NEAR, stride=2 * PIECE), :] = block


def local_kernel(adj, below, above, gradient, jacobian, coupling, step, out, edge):
    planes = step.shape[0]
    rows = planes * 16
    index = pl.program_id(0)
    last = pl.num_programs(0) - 1
    y = iota((rows, LO), 0) % 16
    z = iota((rows, LO), 1)
    faces = [coupling[d].reshape(rows, LO) for d in range(6)]
    faces[2] = jnp.where(y == 15, 0.0, faces[2])
    faces[3] = jnp.where(y == 0, 0.0, faces[3])
    faces[4] = jnp.where(z == LO - 1, 0.0, faces[4])
    faces[5] = jnp.where(z == 0, 0.0, faces[5])
    tau = step[...].reshape(rows, LO)

    @pl.when(index == 0)
    def _():
        edge[0] = (tau * faces[1])[:16]

    @pl.when(index == last)
    def _():
        edge[1] = (tau * faces[0])[-16:]

    for field in range(FIELDS):
        blocks = [jacobian[g, field].reshape(rows, LO) for g in range(FIELDS)]
        mine = [
            adj[t * FIELDS + field].reshape(rows, LO) for t in range(LOCAL)
        ]
        for t in range(LOCAL):
            channel = t * FIELDS + field
            own = mine[t]
            total = -gradient[channel].reshape(rows, LO)
            for g in range(FIELDS):
                total = total + blocks[g] * adj[t * FIELDS + g].reshape(rows, LO)
            next_plane = jnp.where(index == last, 0.0, above[channel, 0])
            past_plane = jnp.where(index == 0, 0.0, below[channel, 0])
            total = total - faces[0] * jnp.concatenate([own[16:], next_plane], axis=0)
            total = total - faces[1] * jnp.concatenate([past_plane, own[:-16]], axis=0)
            total = total - faces[2] * pltpu.roll(own, rows - 1, 0)
            total = total - faces[3] * pltpu.roll(own, 1, 0)
            total = total - faces[4] * pltpu.roll(own, LO - 1, 1)
            total = total - faces[5] * pltpu.roll(own, 1, 1)
            for s in range(LOCAL):
                if s != t:
                    total = total + (ROTOR_RATE * spectra_entry(s - t)) * mine[s]
            out[channel] = (own - tau * total).reshape(planes, 16, LO)


def fringe_kernel(rows, partial, step, out, *scratch):
    accs = scratch[:ACCS]
    flat, expand, order, places, indices, products, held, sem, held_sem = scratch[ACCS:]
    fetch = pltpu.make_async_copy(partial, held, held_sem)
    fetch.start()
    for piece in range(PIECE):
        flat[pl.ds(piece * LO, LO), :] = rows[pl.ds(piece, LO, stride=PIECE), :].T

    weights = jnp.concatenate(
        [flat[slot * SLOT + 24 : slot * SLOT + 32, :] for slot in range(CAP)], axis=0
    )
    alive = jnp.where(weights > 0.0, 1.0, 0.0)
    upto = jnp.where(iota((LO, LO), 0) <= iota((LO, LO), 1), 1.0, 0.0).astype(BF16)
    rank = jnp.dot(alive.astype(BF16), upto, preferred_element_type=F32) * alive - 1.0
    order[...] = rank.astype(jnp.int32)
    places[LO : LO + 8, :] = nt_dot(jnp.ones((8, LO), BF16), alive.astype(BF16)).astype(jnp.int32)

    def move_of(slot):
        target = order[pl.ds(pl.multiple_of(slot * 8, 8), 1), :]
        return jnp.where(iota((LO, LO), 0) == target, 1.0, 0.0).astype(BF16)

    @pl.loop(0, CAP // 4)
    def _(four):
        for i in range(4):
            slot = four * 4 + i
            spot = flat[pl.ds(pl.multiple_of(slot * SLOT, 8) + 32, 8), :]
            head = spot.astype(BF16).astype(F32)
            both = jnp.concatenate([head, spot - head], axis=0).astype(BF16)
            both = nt_dot(both, move_of(slot))
            spot = (both[:8] + both[8:]).astype(jnp.int32)
            places[pl.ds(pl.multiple_of(slot * 8, 8), 8), :] = ((spot >> 9) << 7) | (spot & 127)

    copy = pltpu.make_async_copy(places, indices, sem)
    copy.start()

    row = iota((LO, LO), 0)
    lane = iota((LO, LO), 1)
    value_row = jnp.where(row < 24, row, row - 24)
    hit = (row < 48) & (value_row == lane // 4)
    expand[:, 0:LO] = jnp.where(hit, 1.0, 0.0).astype(BF16)
    weight_row = jnp.where(row < 80, row - 48, row - 80)
    for k in range(8):
        hit = (row >= 48) & (row < 112) & (weight_row == (lane % 4) * 8 + k)
        expand[:, (k + 1) * LO : (k + 2) * LO] = jnp.where(hit, 1.0, 0.0).astype(BF16)

    @pl.loop(0, CAP // 4)
    def _(four):
        for i in range(4):
            slot = four * 4 + i
            base = pl.multiple_of(slot * SLOT, 8)
            values = flat[pl.ds(base, 24), :]
            weights = flat[pl.ds(base + 24, 8), :]
            quarter = (flat[pl.ds(base + 32, 8), :].astype(jnp.int32) >> 7) & 3
            weights = jnp.concatenate(
                [jnp.where(quarter == q, weights, 0.0) for q in range(4)], axis=0
            )
            values_head = values.astype(BF16).astype(F32)
            weights_head = weights.astype(BF16).astype(F32)
            left = jnp.concatenate(
                [
                    values_head,
                    values - values_head,
                    weights_head,
                    weights - weights_head,
                    jnp.zeros((16, LO), F32),
                ],
                axis=0,
            )
            turned = nt_dot(move_of(slot), left.astype(BF16)).astype(BF16)
            both = jnp.dot(turned, expand[...], preferred_element_type=F32)
            here = pl.ds(pl.multiple_of(slot * LO, LO), LO)
            for k in range(8):
                products[k, here, :] = both[:, 0:LO] * both[:, (k + 1) * LO : (k + 2) * LO]

    zeros = jnp.zeros((64, LO), F32)

    @pl.loop(0, 8192 // 64)
    def _(i):
        for acc in accs:
            acc[pl.ds(pl.multiple_of(i * 64, 64), 64), :] = zeros

    copy.wait()

    @pl.loop(0, CAP)
    def _(slot):
        unroll = 8

        @pl.loop(0, (indices[LO, slot * 8] + (unroll - 1)) // unroll)
        def _(chunk):
            for u in range(unroll):
                source = chunk * unroll + u
                for k in range(8):
                    acc = accs[k % ACCS]
                    place = indices[slot * 8 + k, source]
                    acc[pl.ds(place, 1), :] = (
                        acc[pl.ds(place, 1), :] + products[k, pl.ds(slot * LO + source, 1), :]
                    )

    fetch.wait()

    @pl.loop(0, HI // 8, unroll=4)
    def _(i):
        turned = []
        for half in range(2):
            begin = pl.multiple_of(i * 256 + half * LO, LO)
            total = accs[0][pl.ds(begin, LO), :]
            for acc in accs[1:]:
                total = total + acc[pl.ds(begin, LO), :]
            turned.append(total.T)
        here = pl.ds(pl.multiple_of(i * 8, 8), 8)
        tau = step[here, :]
        for channel in range(CH):
            cells = slice(channel * 4, channel * 4 + 4)
            gained = jnp.concatenate([turned[0][cells], turned[1][cells]], axis=0)
            out[channel, here, :] = held[channel, here, :] - tau * gained


def final_kernel(partial, first, rest, step, before, after, edge, out, ready, sem):
    steps = 8
    wide = HI // steps

    def copy_of(i):
        here = pl.ds(pl.multiple_of(i * wide, wide), wide)
        return pltpu.make_async_copy(ready.at[:, here, :], out.at[:, here, :], sem.at[i])

    def block(i):
        here = pl.ds(pl.multiple_of(i * wide, wide), wide)
        tau = step[here, :]
        for field in range(FIELDS):
            channels = [s * FIELDS + field for s in range(LOCAL)]
            others = [
                first[c, here, :] if c < FIRST else rest[c - FIRST, here, :] for c in channels
            ]
            for t in range(LOCAL):
                total = None
                for s in range(LOCAL):
                    if s == t:
                        continue
                    term = (ROTOR_RATE * spectra_entry(s - t + LOCAL)) * others[s]
                    total = term if total is None else total + term
                channel = channels[t]
                ready[channel, here, :] = partial[channel, here, :] - tau * total

    @pl.loop(0, steps)
    def _(i):
        block(i)

        @pl.when(i == 0)
        def _():
            for channel in range(CH):
                ready[channel, :16, :] += edge[0] * before[channel]

        @pl.when(i == steps - 1)
        def _():
            for channel in range(CH):
                ready[channel, HI - 16 :, :] += edge[1] * after[channel]

        copy_of(i).start()

    for i in range(steps):
        copy_of(i).wait()


def shards(
    adjoint,
    gradient,
    jacobian,
    coupling,
    pseudo_step,
    receptor_cell,
    donor_owner,
    donor_cell,
    donor_weight,
    block_count,
):
    swap = [(0, 1), (1, 0)]
    blocks = lax.axis_size("xl") * lax.axis_size("zc")
    cells = adjoint.reshape(CH, HI, LO)
    planes = adjoint.reshape(CH, 16, 16, LO)
    vmem = pl.BlockSpec(memory_space=pltpu.VMEM)
    smem = pl.BlockSpec(memory_space=pltpu.SMEM)

    first = lax.ppermute(cells[:FIRST], "inst", swap)
    payload, top, bottom = pl.pallas_call(
        pick_kernel,
        out_shape=[
            jax.ShapeDtypeStruct((SLOT, ROWS), F32),
            jax.ShapeDtypeStruct((CH, 16, LO), F32),
            jax.ShapeDtypeStruct((CH, 16, LO), F32),
        ],
        in_specs=[smem] + [pl.BlockSpec(memory_space=pl.ANY)] * 5,
        out_specs=[vmem] * 3,
        scratch_shapes=[
            pltpu.VMEM((CH, HI, LO), F32),
            pltpu.VMEM((1, ROWS), jnp.int32),
            pltpu.VMEM((1, ROWS), jnp.int32),
            pltpu.VMEM((8, ROWS), jnp.int32),
            pltpu.VMEM((8, ROWS), F32),
            pltpu.SemaphoreType.DMA((FIELDS,)),
            pltpu.SemaphoreType.DMA((4,)),
        ],
        compiler_params=pltpu.CompilerParams(vmem_limit_bytes=56 * 2**20),
        cost_estimate=takes(5),
        name="pick",
    )(
        block_count.reshape(8),
        cells,
        receptor_cell.reshape(1, ROWS),
        donor_owner.reshape(1, ROWS),
        donor_cell.reshape(8, ROWS),
        donor_weight.reshape(8, ROWS),
    )
    payload, first = lax.optimization_barrier((payload, first))
    got = lax.ppermute(payload, "xl", swap)
    rest, got = lax.optimization_barrier((cells[FIRST:], got))
    rest = lax.ppermute(rest, "inst", swap)

    message = pl.pallas_call(
        pack_kernel,
        out_shape=jax.ShapeDtypeStruct((NEAR * 2 * PIECE, LO), F32),
        in_specs=[smem, vmem, vmem],
        out_specs=vmem,
        compiler_params=pltpu.CompilerParams(vmem_limit_bytes=32 * 2**20),
        cost_estimate=takes(3),
        name="pack",
    )(lax.axis_index("xl").astype(jnp.int32).reshape(1), payload, got)
    message, gradient, top, bottom = lax.optimization_barrier((message, gradient, top, bottom))
    arrived = lax.all_to_all(
        message.reshape(-1), ("sys", "zc"), split_axis=0, concat_axis=0, tiled=True
    )
    before = lax.ppermute(top, ("xl", "zc"), [(i, i + 1) for i in range(blocks - 1)])
    after = lax.ppermute(bottom, ("xl", "zc"), [(i + 1, i) for i in range(blocks - 1)])

    steps = 4
    wide = 16 // steps
    partial, edge = pl.pallas_call(
        local_kernel,
        grid=(steps,),
        out_shape=[
            jax.ShapeDtypeStruct((CH, 16, 16, LO), F32),
            jax.ShapeDtypeStruct((2, 16, LO), F32),
        ],
        in_specs=[
            pl.BlockSpec((CH, wide, 16, LO), lambda i: (0, i, 0, 0)),
            pl.BlockSpec((CH, 1, 16, LO), lambda i: (0, jnp.maximum(wide * i - 1, 0), 0, 0)),
            pl.BlockSpec((CH, 1, 16, LO), lambda i: (0, jnp.minimum(wide * i + wide, 15), 0, 0)),
            pl.BlockSpec((CH, wide, 16, LO), lambda i: (0, i, 0, 0)),
            pl.BlockSpec((FIELDS, FIELDS, wide, 16, LO), lambda i: (0, 0, i, 0, 0)),
            pl.BlockSpec((6, wide, 16, LO), lambda i: (0, i, 0, 0)),
            pl.BlockSpec((wide, 16, LO), lambda i: (i, 0, 0)),
        ],
        out_specs=[
            pl.BlockSpec((CH, wide, 16, LO), lambda i: (0, i, 0, 0)),
            pl.BlockSpec((2, 16, LO), lambda i: (0, 0, 0)),
        ],
        compiler_params=pltpu.CompilerParams(vmem_limit_bytes=56 * 2**20),
        cost_estimate=takes(6),
        name="local",
    )(
        planes,
        planes,
        planes,
        gradient.reshape(CH, 16, 16, LO),
        jacobian.reshape(FIELDS, FIELDS, 16, 16, LO),
        coupling.reshape(6, 16, 16, LO),
        pseudo_step.reshape(16, 16, LO),
    )

    arrived, partial = lax.optimization_barrier((arrived, partial))
    tau = pseudo_step.reshape(HI, LO)
    partial = pl.pallas_call(
        fringe_kernel,
        out_shape=jax.ShapeDtypeStruct((CH, HI, LO), F32),
        in_specs=[vmem, pl.BlockSpec(memory_space=pl.ANY), vmem],
        out_specs=vmem,
        scratch_shapes=[pltpu.VMEM((8192, LO), F32)] * ACCS
        + [
            pltpu.VMEM((CAP * SLOT, LO), F32),
            pltpu.VMEM((LO, 9 * LO), BF16),
            pltpu.VMEM((LO, LO), jnp.int32),
            pltpu.VMEM((LO + 8, LO), jnp.int32),
            pltpu.SMEM((LO + 8, LO), jnp.int32),
            pltpu.VMEM((8, CAP * LO, LO), F32),
            pltpu.VMEM((CH, HI, LO), F32),
            pltpu.SemaphoreType.DMA,
            pltpu.SemaphoreType.DMA,
        ],
        compiler_params=pltpu.CompilerParams(vmem_limit_bytes=58 * 2**20),
        cost_estimate=takes(25),
        name="fringe",
    )(arrived.reshape(128 * PIECE, LO), partial.reshape(CH, HI, LO), tau)

    result = pl.pallas_call(
        final_kernel,
        out_shape=jax.ShapeDtypeStruct((CH, HI, LO), F32),
        in_specs=[vmem] * 7,
        out_specs=pl.BlockSpec(memory_space=pl.ANY),
        scratch_shapes=[pltpu.VMEM((CH, HI, LO), F32), pltpu.SemaphoreType.DMA((8,))],
        compiler_params=pltpu.CompilerParams(vmem_limit_bytes=40 * 2**20),
        cost_estimate=takes(2),
        name="final",
    )(partial, first, rest, tau, before, after, edge)
    return result.reshape(adjoint.shape)


def solution(mesh):
    fine = Mesh(mesh.devices.reshape(4, 2, 16, 2), ("sys", "xl", "zc", "inst"))
    blk = ("xl", "zc")
    return jax.shard_map(
        shards,
        mesh=fine,
        in_specs=(
            P("sys", "inst", None, blk, None, None),
            P("sys", "inst", None, blk, None, None),
            P("sys", None, None, blk, None, None),
            P("sys", None, blk, None, None),
            P("sys", blk, None, None),
            P("sys", blk, None),
            P("sys", blk, None, None),
            P("sys", blk, None, None),
            P("sys", blk, None, None),
            P("sys", blk, None),
        ),
        out_specs=P("sys", "inst", None, blk, None, None),
        check_vma=False,
    )
```

```python
import math

import jax
import jax.numpy as jnp
from jax import lax
from jax.experimental import pallas as pl
from jax.experimental.pallas import tpu as pltpu
from jax.sharding import Mesh, PartitionSpec as P

ROTOR_RATE = 0.6
F32 = jnp.float32
BF16 = jnp.bfloat16

FIELDS = 5
INSTANCES = 8
LOCAL = 4
CH = LOCAL * FIELDS
HI = 256
LO = 128
ROWS = 1024
CAP = 16
SLOT = 40
NEAR = 64
PIECE = CAP * SLOT // LO
FIRST = 2
ACCS = 8


def spectra_entry(offset):
    offset %= INSTANCES
    if offset == 0:
        return 0.0
    angle = math.pi * offset / INSTANCES
    return 0.5 * (-1.0) ** offset * math.cos(angle) / math.sin(angle)


def iota(shape, dim):
    return lax.broadcasted_iota(jnp.int32, shape, dim)


def split(x):
    head = x.astype(BF16)
    return head, (x - head.astype(F32)).astype(BF16)


def takes(microseconds):
    return pl.CostEstimate(flops=0, bytes_accessed=microseconds * 3_700_000, transcendentals=0)


def nt_dot(a, b):
    return lax.dot_general(a, b, (((1,), (1,)), ((), ())), preferred_element_type=F32)


def pick_kernel(counts, *refs):
    (cells, *small), (payload, top, bottom) = refs[:5], refs[5:8]
    adj, cell, owner, donor, weight, sem, small_sem = refs[8:]

    def chunk_copy(i):
        here = pl.ds(i * LOCAL, LOCAL)
        return pltpu.make_async_copy(cells.at[here], adj.at[here], sem.at[i])

    copies = [
        pltpu.make_async_copy(operand, place, small_sem.at[i])
        for i, (operand, place) in enumerate(zip(small, (cell, owner, donor, weight)))
    ]
    for copy in copies:
        copy.start()
    for i in range(FIELDS):
        chunk_copy(i).start()
    for copy in copies:
        copy.wait()
    spot = cell[...]
    high = spot >> 7
    low = spot & 127
    wide = 256
    for part in range(ROWS // wide):
        cols = slice(part * wide, (part + 1) * wide)
        lows = jnp.where(iota((LO, wide), 0) == low[:, cols], 1.0, 0.0).astype(BF16)
        lows = jnp.concatenate([lows, lows], axis=0)
        here = iota((HI, wide), 0) == high[:, cols]
        for channel in range(CH):
            if part == 0 and channel % LOCAL == 0:
                chunk_copy(channel // LOCAL).wait()
            head, tail = split(adj[channel])
            found = jnp.dot(
                jnp.concatenate([head, tail], axis=1), lows, preferred_element_type=F32
            )
            payload[channel : channel + 1, cols] = jnp.sum(
                jnp.where(here, found, 0.0), axis=0, keepdims=True
            )
    for group in range(ROWS // LO):
        lanes = slice(group * LO, (group + 1) * LO)
        living = iota((1, LO), 1) < counts[group]
        payload[CH : CH + 1, lanes] = jnp.where(living, owner[:, lanes], -1).astype(F32)
    payload[CH + 1 : 24, :] = jnp.zeros((23 - CH, ROWS), F32)
    payload[24:32, :] = weight[...]
    payload[32:40, :] = donor[...].astype(F32)
    for channel in range(CH):
        top[channel] = adj[channel, HI - 16 :, :]
        bottom[channel] = adj[channel, :16, :]


def pack_kernel(position, own, got, message):
    upto = jnp.where(iota((LO, LO), 0) <= iota((LO, LO), 1), 1.0, 0.0).astype(BF16)
    ones = jnp.ones((LO, LO), BF16)
    for half, payload in enumerate((own, got)):
        rows = payload[...]
        name = rows[CH : CH + 1].astype(jnp.int32)
        near = ((name >> 4) & 1) == position[0]
        name = jnp.where((name >= 0) & near, ((name >> 5) << 4) | (name & 15), -1)
        before = jnp.zeros((NEAR, LO), F32)
        chosen, ranks = [], []
        for group in range(ROWS // LO):
            lanes = slice(group * LO, (group + 1) * LO)
            hit = jnp.where(iota((NEAR, LO), 0) == name[:, lanes], 1.0, 0.0)
            hit16 = hit.astype(BF16)
            count = jnp.dot(hit16, upto, preferred_element_type=F32) + before
            before = before + jnp.dot(hit16, ones, preferred_element_type=F32)
            ranks.append(jnp.sum(hit * count, axis=0, keepdims=True) - 1.0)
            chosen.append(hit16)
        chosen = jnp.concatenate(chosen, axis=1)
        rank = jnp.concatenate(ranks, axis=1)
        placed = jnp.concatenate(
            [jnp.where(rank == float(slot), rows, 0.0) for slot in range(CAP)], axis=0
        )
        head, tail = split(placed)
        table = nt_dot(head, chosen) + nt_dot(tail, chosen)
        for piece in range(PIECE):
            block = table[piece * LO : (piece + 1) * LO].T
            message[pl.ds(half * PIECE + piece, NEAR, stride=2 * PIECE), :] = block


def local_kernel(adj, below, above, gradient, jacobian, coupling, step, out, edge):
    planes = step.shape[0]
    rows = planes * 16
    index = pl.program_id(0)
    last = pl.num_programs(0) - 1
    y = iota((rows, LO), 0) % 16
    z = iota((rows, LO), 1)
    faces = [coupling[d].reshape(rows, LO) for d in range(6)]
    faces[2] = jnp.where(y == 15, 0.0, faces[2])
    faces[3] = jnp.where(y == 0, 0.0, faces[3])
    faces[4] = jnp.where(z == LO - 1, 0.0, faces[4])
    faces[5] = jnp.where(z == 0, 0.0, faces[5])
    tau = step[...].reshape(rows, LO)

    @pl.when(index == 0)
    def _():
        edge[0] = (tau * faces[1])[:16]

    @pl.when(index == last)
    def _():
        edge[1] = (tau * faces[0])[-16:]

    for field in range(FIELDS):
        blocks = [jacobian[g, field].reshape(rows, LO) for g in range(FIELDS)]
        mine = [
            adj[t * FIELDS + field].reshape(rows, LO) for t in range(LOCAL)
        ]
        for t in range(LOCAL):
            channel = t * FIELDS + field
            own = mine[t]
            total = -gradient[channel].reshape(rows, LO)
            for g in range(FIELDS):
                total = total + blocks[g] * adj[t * FIELDS + g].reshape(rows, LO)
            next_plane = jnp.where(index == last, 0.0, above[channel, 0])
            past_plane = jnp.where(index == 0, 0.0, below[channel, 0])
            total = total - faces[0] * jnp.concatenate([own[16:], next_plane], axis=0)
            total = total - faces[1] * jnp.concatenate([past_plane, own[:-16]], axis=0)
            total = total - faces[2] * pltpu.roll(own, rows - 1, 0)
            total = total - faces[3] * pltpu.roll(own, 1, 0)
            total = total - faces[4] * pltpu.roll(own, LO - 1, 1)
            total = total - faces[5] * pltpu.roll(own, 1, 1)
            for s in range(LOCAL):
                if s != t:
                    total = total + (ROTOR_RATE * spectra_entry(s - t)) * mine[s]
            out[channel] = (own - tau * total).reshape(planes, 16, LO)


def fringe_kernel(rows, partial, step, out, *scratch):
    accs = scratch[:ACCS]
    flat, expand, order, places, indices, products, held, sem, held_sem = scratch[ACCS:]
    fetch = pltpu.make_async_copy(partial, held, held_sem)
    fetch.start()
    for piece in range(PIECE):
        flat[pl.ds(piece * LO, LO), :] = rows[pl.ds(piece, LO, stride=PIECE), :].T

    weights = jnp.concatenate(
        [flat[slot * SLOT + 24 : slot * SLOT + 32, :] for slot in range(CAP)], axis=0
    )
    alive = jnp.where(weights > 0.0, 1.0, 0.0)
    upto = jnp.where(iota((LO, LO), 0) <= iota((LO, LO), 1), 1.0, 0.0).astype(BF16)
    rank = jnp.dot(alive.astype(BF16), upto, preferred_element_type=F32) * alive - 1.0
    order[...] = rank.astype(jnp.int32)
    places[LO : LO + 8, :] = nt_dot(jnp.ones((8, LO), BF16), alive.astype(BF16)).astype(jnp.int32)

    def move_of(slot):
        target = order[pl.ds(pl.multiple_of(slot * 8, 8), 1), :]
        return jnp.where(iota((LO, LO), 0) == target, 1.0, 0.0).astype(BF16)

    @pl.loop(0, CAP // 4)
    def _(four):
        for i in range(4):
            slot = four * 4 + i
            spot = flat[pl.ds(pl.multiple_of(slot * SLOT, 8) + 32, 8), :]
            head = spot.astype(BF16).astype(F32)
            both = jnp.concatenate([head, spot - head], axis=0).astype(BF16)
            both = nt_dot(both, move_of(slot))
            spot = (both[:8] + both[8:]).astype(jnp.int32)
            places[pl.ds(pl.multiple_of(slot * 8, 8), 8), :] = ((spot >> 9) << 7) | (spot & 127)

    copy = pltpu.make_async_copy(places, indices, sem)
    copy.start()

    row = iota((LO, LO), 0)
    lane = iota((LO, LO), 1)
    value_row = jnp.where(row < 24, row, row - 24)
    hit = (row < 48) & (value_row == lane // 4)
    expand[:, 0:LO] = jnp.where(hit, 1.0, 0.0).astype(BF16)
    weight_row = jnp.where(row < 80, row - 48, row - 80)
    for k in range(8):
        hit = (row >= 48) & (row < 112) & (weight_row == (lane % 4) * 8 + k)
        expand[:, (k + 1) * LO : (k + 2) * LO] = jnp.where(hit, 1.0, 0.0).astype(BF16)

    @pl.loop(0, CAP // 4)
    def _(four):
        for i in range(4):
            slot = four * 4 + i
            base = pl.multiple_of(slot * SLOT, 8)
            values = flat[pl.ds(base, 24), :]
            weights = flat[pl.ds(base + 24, 8), :]
            quarter = (flat[pl.ds(base + 32, 8), :].astype(jnp.int32) >> 7) & 3
            weights = jnp.concatenate(
                [jnp.where(quarter == q, weights, 0.0) for q in range(4)], axis=0
            )
            values_head = values.astype(BF16).astype(F32)
            weights_head = weights.astype(BF16).astype(F32)
            left = jnp.concatenate(
                [
                    values_head,
                    values - values_head,
                    weights_head,
                    weights - weights_head,
                    jnp.zeros((16, LO), F32),
                ],
                axis=0,
            )
            turned = nt_dot(move_of(slot), left.astype(BF16)).astype(BF16)
            both = jnp.dot(turned, expand[...], preferred_element_type=F32)
            here = pl.ds(pl.multiple_of(slot * LO, LO), LO)
            for k in range(8):
                products[k, here, :] = both[:, 0:LO] * both[:, (k + 1) * LO : (k + 2) * LO]

    zeros = jnp.zeros((64, LO), F32)

    @pl.loop(0, 8192 // 64)
    def _(i):
        for acc in accs:
            acc[pl.ds(pl.multiple_of(i * 64, 64), 64), :] = zeros

    copy.wait()
    listed = indices.reshape((LO + 8) * LO)

    @pl.loop(0, CAP)
    def _(slot):
        unroll = 8

        @pl.loop(0, (listed[LO * LO + slot * 8] + (unroll - 1)) // unroll)
        def _(chunk):
            for u in range(unroll):
                source = chunk * unroll + u
                for k in range(8):
                    acc = accs[k % ACCS]
                    place = listed[slot * 8 * LO + chunk * unroll + (k * LO + u)]
                    acc[pl.ds(place, 1), :] = (
                        acc[pl.ds(place, 1), :] + products[k, pl.ds(slot * LO + source, 1), :]
                    )

    fetch.wait()

    @pl.loop(0, HI // 8, unroll=4)
    def _(i):
        turned = []
        for half in range(2):
            begin = pl.multiple_of(i * 256 + half * LO, LO)
            total = accs[0][pl.ds(begin, LO), :]
            for acc in accs[1:]:
                total = total + acc[pl.ds(begin, LO), :]
            turned.append(total.T)
        here = pl.ds(pl.multiple_of(i * 8, 8), 8)
        tau = step[here, :]
        for channel in range(CH):
            cells = slice(channel * 4, channel * 4 + 4)
            gained = jnp.concatenate([turned[0][cells], turned[1][cells]], axis=0)
            out[channel, here, :] = held[channel, here, :] - tau * gained


def final_kernel(partial, first, rest, step, before, after, edge, out, ready, sem):
    steps = 8
    wide = HI // steps

    def copy_of(i):
        here = pl.ds(pl.multiple_of(i * wide, wide), wide)
        return pltpu.make_async_copy(ready.at[:, here, :], out.at[:, here, :], sem.at[i])

    def block(i):
        here = pl.ds(pl.multiple_of(i * wide, wide), wide)
        tau = step[here, :]
        for field in range(FIELDS):
            channels = [s * FIELDS + field for s in range(LOCAL)]
            others = [
                first[c, here, :] if c < FIRST else rest[c - FIRST, here, :] for c in channels
            ]
            for t in range(LOCAL):
                total = None
                for s in range(LOCAL):
                    if s == t:
                        continue
                    term = (ROTOR_RATE * spectra_entry(s - t + LOCAL)) * others[s]
                    total = term if total is None else total + term
                channel = channels[t]
                ready[channel, here, :] = partial[channel, here, :] - tau * total

    @pl.loop(0, steps)
    def _(i):
        block(i)

        @pl.when(i == 0)
        def _():
            for channel in range(CH):
                ready[channel, :16, :] += edge[0] * before[channel]

        @pl.when(i == steps - 1)
        def _():
            for channel in range(CH):
                ready[channel, HI - 16 :, :] += edge[1] * after[channel]

        copy_of(i).start()

    for i in range(steps):
        copy_of(i).wait()


def shards(
    adjoint,
    gradient,
    jacobian,
    coupling,
    pseudo_step,
    receptor_cell,
    donor_owner,
    donor_cell,
    donor_weight,
    block_count,
):
    swap = [(0, 1), (1, 0)]
    blocks = lax.axis_size("xl") * lax.axis_size("zc")
    cells = adjoint.reshape(CH, HI, LO)
    planes = adjoint.reshape(CH, 16, 16, LO)
    vmem = pl.BlockSpec(memory_space=pltpu.VMEM)
    smem = pl.BlockSpec(memory_space=pltpu.SMEM)
    hbm = pl.BlockSpec(memory_space=pltpu.HBM)

    first = lax.ppermute(cells[:FIRST], "inst", swap)
    payload, top, bottom = pl.pallas_call(
        pick_kernel,
        out_shape=[
            jax.ShapeDtypeStruct((SLOT, ROWS), F32),
            jax.ShapeDtypeStruct((CH, 16, LO), F32),
            jax.ShapeDtypeStruct((CH, 16, LO), F32),
        ],
        in_specs=[smem] + [hbm] * 5,
        out_specs=[vmem] * 3,
        scratch_shapes=[
            pltpu.VMEM((CH, HI, LO), F32),
            pltpu.VMEM((1, ROWS), jnp.int32),
            pltpu.VMEM((1, ROWS), jnp.int32),
            pltpu.VMEM((8, ROWS), jnp.int32),
            pltpu.VMEM((8, ROWS), F32),
            pltpu.SemaphoreType.DMA((FIELDS,)),
            pltpu.SemaphoreType.DMA((4,)),
        ],
        compiler_params=pltpu.CompilerParams(vmem_limit_bytes=56 * 2**20),
        cost_estimate=takes(5),
        name="pick",
    )(
        block_count.reshape(8),
        cells,
        receptor_cell.reshape(1, ROWS),
        donor_owner.reshape(1, ROWS),
        donor_cell.reshape(8, ROWS),
        donor_weight.reshape(8, ROWS),
    )
    payload, first = lax.optimization_barrier((payload, first))
    got = lax.ppermute(payload, "xl", swap)
    rest, got = lax.optimization_barrier((cells[FIRST:], got))
    rest = lax.ppermute(rest, "inst", swap)

    message = pl.pallas_call(
        pack_kernel,
        out_shape=jax.ShapeDtypeStruct((NEAR * 2 * PIECE, LO), F32),
        in_specs=[smem, vmem, vmem],
        out_specs=vmem,
        compiler_params=pltpu.CompilerParams(vmem_limit_bytes=32 * 2**20),
        cost_estimate=takes(3),
        name="pack",
    )(lax.axis_index("xl").astype(jnp.int32).reshape(1), payload, got)
    message, gradient, top, bottom = lax.optimization_barrier((message, gradient, top, bottom))
    arrived = lax.all_to_all(
        message.reshape(-1), ("sys", "zc"), split_axis=0, concat_axis=0, tiled=True
    )
    before = lax.ppermute(top, ("xl", "zc"), [(i, i + 1) for i in range(blocks - 1)])
    after = lax.ppermute(bottom, ("xl", "zc"), [(i + 1, i) for i in range(blocks - 1)])

    steps = 4
    wide = 16 // steps
    partial, edge = pl.pallas_call(
        local_kernel,
        grid=(steps,),
        out_shape=[
            jax.ShapeDtypeStruct((CH, 16, 16, LO), F32),
            jax.ShapeDtypeStruct((2, 16, LO), F32),
        ],
        in_specs=[
            pl.BlockSpec((CH, wide, 16, LO), lambda i: (0, i, 0, 0)),
            pl.BlockSpec((CH, 1, 16, LO), lambda i: (0, jnp.maximum(wide * i - 1, 0), 0, 0)),
            pl.BlockSpec((CH, 1, 16, LO), lambda i: (0, jnp.minimum(wide * i + wide, 15), 0, 0)),
            pl.BlockSpec((CH, wide, 16, LO), lambda i: (0, i, 0, 0)),
            pl.BlockSpec((FIELDS, FIELDS, wide, 16, LO), lambda i: (0, 0, i, 0, 0)),
            pl.BlockSpec((6, wide, 16, LO), lambda i: (0, i, 0, 0)),
            pl.BlockSpec((wide, 16, LO), lambda i: (i, 0, 0)),
        ],
        out_specs=[
            pl.BlockSpec((CH, wide, 16, LO), lambda i: (0, i, 0, 0)),
            pl.BlockSpec((2, 16, LO), lambda i: (0, 0, 0)),
        ],
        compiler_params=pltpu.CompilerParams(vmem_limit_bytes=56 * 2**20),
        cost_estimate=takes(6),
        name="local",
    )(
        planes,
        planes,
        planes,
        gradient.reshape(CH, 16, 16, LO),
        jacobian.reshape(FIELDS, FIELDS, 16, 16, LO),
        coupling.reshape(6, 16, 16, LO),
        pseudo_step.reshape(16, 16, LO),
    )

    arrived, partial = lax.optimization_barrier((arrived, partial))
    tau = pseudo_step.reshape(HI, LO)
    partial = pl.pallas_call(
        fringe_kernel,
        out_shape=jax.ShapeDtypeStruct((CH, HI, LO), F32),
        in_specs=[vmem, hbm, vmem],
        out_specs=vmem,
        scratch_shapes=[pltpu.VMEM((8192, LO), F32)] * ACCS
        + [
            pltpu.VMEM((CAP * SLOT, LO), F32),
            pltpu.VMEM((LO, 9 * LO), BF16),
            pltpu.VMEM((LO, LO), jnp.int32),
            pltpu.VMEM((LO + 8, LO), jnp.int32),
            pltpu.SMEM((LO + 8, LO), jnp.int32),
            pltpu.VMEM((8, CAP * LO, LO), F32),
            pltpu.VMEM((CH, HI, LO), F32),
            pltpu.SemaphoreType.DMA,
            pltpu.SemaphoreType.DMA,
        ],
        compiler_params=pltpu.CompilerParams(vmem_limit_bytes=50 * 2**20),
        cost_estimate=takes(25),
        name="fringe",
    )(arrived.reshape(128 * PIECE, LO), partial.reshape(CH, HI, LO), tau)

    result = pl.pallas_call(
        final_kernel,
        out_shape=jax.ShapeDtypeStruct((CH, HI, LO), F32),
        in_specs=[vmem] * 7,
        out_specs=pl.BlockSpec(memory_space=pl.ANY),
        scratch_shapes=[pltpu.VMEM((CH, HI, LO), F32), pltpu.SemaphoreType.DMA((8,))],
        compiler_params=pltpu.CompilerParams(vmem_limit_bytes=40 * 2**20),
        cost_estimate=takes(2),
        name="final",
    )(partial, first, rest, tau, before, after, edge)
    return result.reshape(adjoint.shape)


def solution(mesh):
    fine = Mesh(mesh.devices.reshape(4, 2, 16, 2), ("sys", "xl", "zc", "inst"))
    blk = ("xl", "zc")
    return jax.shard_map(
        shards,
        mesh=fine,
        in_specs=(
            P("sys", "inst", None, blk, None, None),
            P("sys", "inst", None, blk, None, None),
            P("sys", None, None, blk, None, None),
            P("sys", None, blk, None, None),
            P("sys", blk, None, None),
            P("sys", blk, None),
            P("sys", blk, None, None),
            P("sys", blk, None, None),
            P("sys", blk, None, None),
            P("sys", blk, None),
        ),
        out_specs=P("sys", "inst", None, blk, None, None),
        check_vma=False,
    )
```

```python
import math

import jax
import jax.numpy as jnp
from jax import lax
from jax.experimental import pallas as pl
from jax.experimental.pallas import tpu as pltpu
from jax.sharding import Mesh, PartitionSpec as P

ROTOR_RATE = 0.6
F32 = jnp.float32
BF16 = jnp.bfloat16

FIELDS = 5
INSTANCES = 8
LOCAL = 4
CH = LOCAL * FIELDS
HI = 256
LO = 128
ROWS = 1024
CAP = 16
SLOT = 40
NEAR = 64
PIECE = CAP * SLOT // LO
FIRST = 3
ACCS = 8


def spectra_entry(offset):
    offset %= INSTANCES
    if offset == 0:
        return 0.0
    angle = math.pi * offset / INSTANCES
    return 0.5 * (-1.0) ** offset * math.cos(angle) / math.sin(angle)


def iota(shape, dim):
    return lax.broadcasted_iota(jnp.int32, shape, dim)


def split(x):
    head = x.astype(BF16)
    return head, (x - head.astype(F32)).astype(BF16)


def takes(microseconds):
    return pl.CostEstimate(flops=0, bytes_accessed=microseconds * 3_700_000, transcendentals=0)


def nt_dot(a, b):
    return lax.dot_general(a, b, (((1,), (1,)), ((), ())), preferred_element_type=F32)


def pick_kernel(counts, *refs):
    (cells, *small), (payload, top, bottom) = refs[:5], refs[5:8]
    adj, cell, owner, donor, weight, sem, small_sem = refs[8:]

    def chunk_copy(i):
        here = pl.ds(i * LOCAL, LOCAL)
        return pltpu.make_async_copy(cells.at[here], adj.at[here], sem.at[i])

    copies = [
        pltpu.make_async_copy(operand, place, small_sem.at[i])
        for i, (operand, place) in enumerate(zip(small, (cell, owner, donor, weight)))
    ]
    for copy in copies:
        copy.start()
    for i in range(FIELDS):
        chunk_copy(i).start()
    for copy in copies:
        copy.wait()
    for i in range(FIELDS):
        chunk_copy(i).wait()
    spot = cell[...]
    high = (spot >> 7) & 127
    low = ((spot >> 14) << 7) | (spot & 127)
    lefts = []
    for channel in range(CH):
        whole = adj[channel]
        head, tail = split(jnp.concatenate([whole[:LO], whole[LO:]], axis=1))
        lefts.append(jnp.concatenate([head, tail], axis=1))
    left = jnp.concatenate(lefts, axis=0)
    wide = 256
    for part in range(ROWS // wide):
        cols = slice(part * wide, (part + 1) * wide)
        lows = jnp.where(iota((2 * LO, wide), 0) == low[:, cols], 1.0, 0.0).astype(BF16)
        lows = jnp.concatenate([lows, lows], axis=0)
        here = iota((LO, wide), 0) == high[:, cols]
        found = jnp.dot(left, lows, preferred_element_type=F32)
        for channel in range(CH):
            payload[channel : channel + 1, cols] = jnp.sum(
                jnp.where(here, found[channel * LO : (channel + 1) * LO], 0.0),
                axis=0,
                keepdims=True,
            )
    for group in range(ROWS // LO):
        lanes = slice(group * LO, (group + 1) * LO)
        living = iota((1, LO), 1) < counts[group]
        payload[CH : CH + 1, lanes] = jnp.where(living, owner[:, lanes], -1).astype(F32)
    payload[CH + 1 : 24, :] = jnp.zeros((23 - CH, ROWS), F32)
    payload[24:32, :] = weight[...]
    payload[32:40, :] = donor[...].astype(F32)
    for channel in range(CH):
        top[channel] = adj[channel, HI - 16 :, :]
        bottom[channel] = adj[channel, :16, :]


def pack_kernel(position, own, got, message):
    upto = jnp.where(iota((LO, LO), 0) <= iota((LO, LO), 1), 1.0, 0.0).astype(BF16)
    ones = jnp.ones((LO, LO), BF16)
    for half, payload in enumerate((own, got)):
        rows = payload[...]
        name = rows[CH : CH + 1].astype(jnp.int32)
        near = ((name >> 4) & 1) == position[0]
        name = jnp.where((name >= 0) & near, ((name >> 5) << 4) | (name & 15), -1)
        before = jnp.zeros((NEAR, LO), F32)
        chosen, ranks = [], []
        for group in range(ROWS // LO):
            lanes = slice(group * LO, (group + 1) * LO)
            hit = jnp.where(iota((NEAR, LO), 0) == name[:, lanes], 1.0, 0.0)
            hit16 = hit.astype(BF16)
            count = jnp.dot(hit16, upto, preferred_element_type=F32) + before
            before = before + jnp.dot(hit16, ones, preferred_element_type=F32)
            ranks.append(jnp.sum(hit * count, axis=0, keepdims=True) - 1.0)
            chosen.append(hit16)
        chosen = jnp.concatenate(chosen, axis=1)
        rank = jnp.concatenate(ranks, axis=1)
        placed = jnp.concatenate(
            [jnp.where(rank == float(slot), rows, 0.0) for slot in range(CAP)], axis=0
        )
        head, tail = split(placed)
        table = nt_dot(head, chosen) + nt_dot(tail, chosen)
        for piece in range(PIECE):
            block = table[piece * LO : (piece + 1) * LO].T
            message[pl.ds(half * PIECE + piece, NEAR, stride=2 * PIECE), :] = block


def local_kernel(adj, below, above, gradient, jacobian, coupling, step, out, edge):
    planes = step.shape[0]
    rows = planes * 16
    index = pl.program_id(0)
    last = pl.num_programs(0) - 1
    y = iota((rows, LO), 0) % 16
    z = iota((rows, LO), 1)
    faces = [coupling[d].reshape(rows, LO) for d in range(6)]
    faces[2] = jnp.where(y == 15, 0.0, faces[2])
    faces[3] = jnp.where(y == 0, 0.0, faces[3])
    faces[4] = jnp.where(z == LO - 1, 0.0, faces[4])
    faces[5] = jnp.where(z == 0, 0.0, faces[5])
    tau = step[...].reshape(rows, LO)

    @pl.when(index == 0)
    def _():
        edge[0] = (tau * faces[1])[:16]

    @pl.when(index == last)
    def _():
        edge[1] = (tau * faces[0])[-16:]

    for field in range(FIELDS):
        blocks = [jacobian[g, field].reshape(rows, LO) for g in range(FIELDS)]
        mine = [
            adj[t * FIELDS + field].reshape(rows, LO) for t in range(LOCAL)
        ]
        for t in range(LOCAL):
            channel = t * FIELDS + field
            own = mine[t]
            total = -gradient[channel].reshape(rows, LO)
            for g in range(FIELDS):
                total = total + blocks[g] * adj[t * FIELDS + g].reshape(rows, LO)
            next_plane = jnp.where(index == last, 0.0, above[channel, 0])
            past_plane = jnp.where(index == 0, 0.0, below[channel, 0])
            total = total - faces[0] * jnp.concatenate([own[16:], next_plane], axis=0)
            total = total - faces[1] * jnp.concatenate([past_plane, own[:-16]], axis=0)
            total = total - faces[2] * pltpu.roll(own, rows - 1, 0)
            total = total - faces[3] * pltpu.roll(own, 1, 0)
            total = total - faces[4] * pltpu.roll(own, LO - 1, 1)
            total = total - faces[5] * pltpu.roll(own, 1, 1)
            for s in range(LOCAL):
                if s != t:
                    total = total + (ROTOR_RATE * spectra_entry(s - t)) * mine[s]
            out[channel] = (own - tau * total).reshape(planes, 16, LO)


def fringe_kernel(rows, partial, step, out, *scratch):
    accs = scratch[:ACCS]
    flat, expand, order, places, indices, products, held, sem, held_sem = scratch[ACCS:]
    fetch = pltpu.make_async_copy(partial, held, held_sem)
    fetch.start()
    for piece in range(PIECE):
        flat[pl.ds(piece * LO, LO), :] = rows[pl.ds(piece, LO, stride=PIECE), :].T

    weights = jnp.concatenate(
        [flat[slot * SLOT + 24 : slot * SLOT + 32, :] for slot in range(CAP)], axis=0
    )
    alive = jnp.where(weights > 0.0, 1.0, 0.0)
    upto = jnp.where(iota((LO, LO), 0) <= iota((LO, LO), 1), 1.0, 0.0).astype(BF16)
    rank = jnp.dot(alive.astype(BF16), upto, preferred_element_type=F32) * alive - 1.0
    order[...] = rank.astype(jnp.int32)
    places[LO : LO + 8, :] = nt_dot(jnp.ones((8, LO), BF16), alive.astype(BF16)).astype(jnp.int32)

    def move_of(slot):
        target = order[pl.ds(pl.multiple_of(slot * 8, 8), 1), :]
        return jnp.where(iota((LO, LO), 0) == target, 1.0, 0.0).astype(BF16)

    @pl.loop(0, CAP // 4)
    def _(four):
        for i in range(4):
            slot = four * 4 + i
            spot = flat[pl.ds(pl.multiple_of(slot * SLOT, 8) + 32, 8), :]
            head = spot.astype(BF16).astype(F32)
            both = jnp.concatenate([head, spot - head], axis=0).astype(BF16)
            both = nt_dot(both, move_of(slot))
            spot = (both[:8] + both[8:]).astype(jnp.int32)
            places[pl.ds(pl.multiple_of(slot * 8, 8), 8), :] = ((spot >> 9) << 7) | (spot & 127)

    copy = pltpu.make_async_copy(places, indices, sem)
    copy.start()

    row = iota((LO, LO), 0)
    lane = iota((LO, LO), 1)
    value_row = jnp.where(row < 24, row, row - 24)
    hit = (row < 48) & (value_row == lane // 4)
    expand[:, 0:LO] = jnp.where(hit, 1.0, 0.0).astype(BF16)
    weight_row = jnp.where(row < 80, row - 48, row - 80)
    for k in range(8):
        hit = (row >= 48) & (row < 112) & (weight_row == (lane % 4) * 8 + k)
        expand[:, (k + 1) * LO : (k + 2) * LO] = jnp.where(hit, 1.0, 0.0).astype(BF16)

    @pl.loop(0, CAP // 4)
    def _(four):
        for i in range(4):
            slot = four * 4 + i
            base = pl.multiple_of(slot * SLOT, 8)
            values = flat[pl.ds(base, 24), :]
            weights = flat[pl.ds(base + 24, 8), :]
            quarter = (flat[pl.ds(base + 32, 8), :].astype(jnp.int32) >> 7) & 3
            weights = jnp.concatenate(
                [jnp.where(quarter == q, weights, 0.0) for q in range(4)], axis=0
            )
            values_head = values.astype(BF16).astype(F32)
            weights_head = weights.astype(BF16).astype(F32)
            left = jnp.concatenate(
                [
                    values_head,
                    values - values_head,
                    weights_head,
                    weights - weights_head,
                    jnp.zeros((16, LO), F32),
                ],
                axis=0,
            )
            turned = nt_dot(move_of(slot), left.astype(BF16)).astype(BF16)
            both = jnp.dot(turned, expand[...], preferred_element_type=F32)
            here = pl.ds(pl.multiple_of(slot * LO, LO), LO)
            for k in range(8):
                products[k, here, :] = both[:, 0:LO] * both[:, (k + 1) * LO : (k + 2) * LO]

    zeros = jnp.zeros((64, LO), F32)

    @pl.loop(0, 8192 // 64)
    def _(i):
        for acc in accs:
            acc[pl.ds(pl.multiple_of(i * 64, 64), 64), :] = zeros

    copy.wait()
    listed = indices.reshape((LO + 8) * LO)

    @pl.loop(0, CAP)
    def _(slot):
        unroll = 8

        @pl.loop(0, (listed[LO * LO + slot * 8] + (unroll - 1)) // unroll)
        def _(chunk):
            for u in range(unroll):
                source = chunk * unroll + u
                for k in range(8):
                    acc = accs[k % ACCS]
                    place = listed[slot * 8 * LO + chunk * unroll + (k * LO + u)]
                    acc[pl.ds(place, 1), :] = (
                        acc[pl.ds(place, 1), :] + products[k, pl.ds(slot * LO + source, 1), :]
                    )

    fetch.wait()

    @pl.loop(0, HI // 8, unroll=4)
    def _(i):
        turned = []
        for half in range(2):
            begin = pl.multiple_of(i * 256 + half * LO, LO)
            total = accs[0][pl.ds(begin, LO), :]
            for acc in accs[1:]:
                total = total + acc[pl.ds(begin, LO), :]
            turned.append(total.T)
        here = pl.ds(pl.multiple_of(i * 8, 8), 8)
        tau = step[here, :]
        for channel in range(CH):
            cells = slice(channel * 4, channel * 4 + 4)
            gained = jnp.concatenate([turned[0][cells], turned[1][cells]], axis=0)
            out[channel, here, :] = held[channel, here, :] - tau * gained


def final_kernel(partial, first, rest, step, before, after, edge, out, ready, sem):
    steps = 8
    wide = HI // steps

    def copy_of(i):
        here = pl.ds(pl.multiple_of(i * wide, wide), wide)
        return pltpu.make_async_copy(ready.at[:, here, :], out.at[:, here, :], sem.at[i])

    def block(i):
        here = pl.ds(pl.multiple_of(i * wide, wide), wide)
        tau = step[here, :]
        for field in range(FIELDS):
            channels = [s * FIELDS + field for s in range(LOCAL)]
            others = [
                first[c, here, :] if c < FIRST else rest[c - FIRST, here, :] for c in channels
            ]
            for t in range(LOCAL):
                total = None
                for s in range(LOCAL):
                    if s == t:
                        continue
                    term = (ROTOR_RATE * spectra_entry(s - t + LOCAL)) * others[s]
                    total = term if total is None else total + term
                channel = channels[t]
                ready[channel, here, :] = partial[channel, here, :] - tau * total

    @pl.loop(0, steps)
    def _(i):
        block(i)

        @pl.when(i == 0)
        def _():
            for channel in range(CH):
                ready[channel, :16, :] += edge[0] * before[channel]

        @pl.when(i == steps - 1)
        def _():
            for channel in range(CH):
                ready[channel, HI - 16 :, :] += edge[1] * after[channel]

        copy_of(i).start()

    for i in range(steps):
        copy_of(i).wait()


def shards(
    adjoint,
    gradient,
    jacobian,
    coupling,
    pseudo_step,
    receptor_cell,
    donor_owner,
    donor_cell,
    donor_weight,
    block_count,
):
    swap = [(0, 1), (1, 0)]
    blocks = lax.axis_size("xl") * lax.axis_size("zc")
    cells = adjoint.reshape(CH, HI, LO)
    planes = adjoint.reshape(CH, 16, 16, LO)
    vmem = pl.BlockSpec(memory_space=pltpu.VMEM)
    smem = pl.BlockSpec(memory_space=pltpu.SMEM)
    hbm = pl.BlockSpec(memory_space=pltpu.HBM)

    first = lax.ppermute(cells[:FIRST], "inst", swap)
    payload, top, bottom = pl.pallas_call(
        pick_kernel,
        out_shape=[
            jax.ShapeDtypeStruct((SLOT, ROWS), F32),
            jax.ShapeDtypeStruct((CH, 16, LO), F32),
            jax.ShapeDtypeStruct((CH, 16, LO), F32),
        ],
        in_specs=[smem] + [hbm] * 5,
        out_specs=[vmem] * 3,
        scratch_shapes=[
            pltpu.VMEM((CH, HI, LO), F32),
            pltpu.VMEM((1, ROWS), jnp.int32),
            pltpu.VMEM((1, ROWS), jnp.int32),
            pltpu.VMEM((8, ROWS), jnp.int32),
            pltpu.VMEM((8, ROWS), F32),
            pltpu.SemaphoreType.DMA((FIELDS,)),
            pltpu.SemaphoreType.DMA((4,)),
        ],
        compiler_params=pltpu.CompilerParams(vmem_limit_bytes=56 * 2**20),
        cost_estimate=takes(5),
        name="pick",
    )(
        block_count.reshape(8),
        cells,
        receptor_cell.reshape(1, ROWS),
        donor_owner.reshape(1, ROWS),
        donor_cell.reshape(8, ROWS),
        donor_weight.reshape(8, ROWS),
    )
    got = lax.ppermute(payload, "xl", swap)
    rest, got, first = lax.optimization_barrier((cells[FIRST:], got, first))
    rest = lax.ppermute(rest, "inst", swap)

    message = pl.pallas_call(
        pack_kernel,
        out_shape=jax.ShapeDtypeStruct((NEAR * 2 * PIECE, LO), F32),
        in_specs=[smem, vmem, vmem],
        out_specs=vmem,
        compiler_params=pltpu.CompilerParams(vmem_limit_bytes=32 * 2**20),
        cost_estimate=takes(3),
        name="pack",
    )(lax.axis_index("xl").astype(jnp.int32).reshape(1), payload, got)
    message, gradient, top, bottom = lax.optimization_barrier((message, gradient, top, bottom))
    arrived = lax.all_to_all(
        message.reshape(-1), ("sys", "zc"), split_axis=0, concat_axis=0, tiled=True
    )
    before = lax.ppermute(top, ("xl", "zc"), [(i, i + 1) for i in range(blocks - 1)])
    after = lax.ppermute(bottom, ("xl", "zc"), [(i + 1, i) for i in range(blocks - 1)])

    steps = 4
    wide = 16 // steps
    partial, edge = pl.pallas_call(
        local_kernel,
        grid=(steps,),
        out_shape=[
            jax.ShapeDtypeStruct((CH, 16, 16, LO), F32),
            jax.ShapeDtypeStruct((2, 16, LO), F32),
        ],
        in_specs=[
            pl.BlockSpec((CH, wide, 16, LO), lambda i: (0, i, 0, 0)),
            pl.BlockSpec((CH, 1, 16, LO), lambda i: (0, jnp.maximum(wide * i - 1, 0), 0, 0)),
            pl.BlockSpec((CH, 1, 16, LO), lambda i: (0, jnp.minimum(wide * i + wide, 15), 0, 0)),
            pl.BlockSpec((CH, wide, 16, LO), lambda i: (0, i, 0, 0)),
            pl.BlockSpec((FIELDS, FIELDS, wide, 16, LO), lambda i: (0, 0, i, 0, 0)),
            pl.BlockSpec((6, wide, 16, LO), lambda i: (0, i, 0, 0)),
            pl.BlockSpec((wide, 16, LO), lambda i: (i, 0, 0)),
        ],
        out_specs=[
            pl.BlockSpec((CH, wide, 16, LO), lambda i: (0, i, 0, 0)),
            pl.BlockSpec((2, 16, LO), lambda i: (0, 0, 0)),
        ],
        compiler_params=pltpu.CompilerParams(vmem_limit_bytes=56 * 2**20),
        cost_estimate=takes(6),
        name="local",
    )(
        planes,
        planes,
        planes,
        gradient.reshape(CH, 16, 16, LO),
        jacobian.reshape(FIELDS, FIELDS, 16, 16, LO),
        coupling.reshape(6, 16, 16, LO),
        pseudo_step.reshape(16, 16, LO),
    )

    arrived, partial = lax.optimization_barrier((arrived, partial))
    tau = pseudo_step.reshape(HI, LO)
    partial = pl.pallas_call(
        fringe_kernel,
        out_shape=jax.ShapeDtypeStruct((CH, HI, LO), F32),
        in_specs=[vmem, hbm, vmem],
        out_specs=vmem,
        scratch_shapes=[pltpu.VMEM((8192, LO), F32)] * ACCS
        + [
            pltpu.VMEM((CAP * SLOT, LO), F32),
            pltpu.VMEM((LO, 9 * LO), BF16),
            pltpu.VMEM((LO, LO), jnp.int32),
            pltpu.VMEM((LO + 8, LO), jnp.int32),
            pltpu.SMEM((LO + 8, LO), jnp.int32),
            pltpu.VMEM((8, CAP * LO, LO), F32),
            pltpu.VMEM((CH, HI, LO), F32),
            pltpu.SemaphoreType.DMA,
            pltpu.SemaphoreType.DMA,
        ],
        compiler_params=pltpu.CompilerParams(vmem_limit_bytes=50 * 2**20),
        cost_estimate=takes(25),
        name="fringe",
    )(arrived.reshape(128 * PIECE, LO), partial.reshape(CH, HI, LO), tau)

    result = pl.pallas_call(
        final_kernel,
        out_shape=jax.ShapeDtypeStruct((CH, HI, LO), F32),
        in_specs=[vmem] * 7,
        out_specs=pl.BlockSpec(memory_space=pl.ANY),
        scratch_shapes=[pltpu.VMEM((CH, HI, LO), F32), pltpu.SemaphoreType.DMA((8,))],
        compiler_params=pltpu.CompilerParams(vmem_limit_bytes=40 * 2**20),
        cost_estimate=takes(2),
        name="final",
    )(partial, first, rest, tau, before, after, edge)
    return result.reshape(adjoint.shape)


def solution(mesh):
    fine = Mesh(mesh.devices.reshape(4, 2, 16, 2), ("sys", "xl", "zc", "inst"))
    blk = ("xl", "zc")
    return jax.shard_map(
        shards,
        mesh=fine,
        in_specs=(
            P("sys", "inst", None, blk, None, None),
            P("sys", "inst", None, blk, None, None),
            P("sys", None, None, blk, None, None),
            P("sys", None, blk, None, None),
            P("sys", blk, None, None),
            P("sys", blk, None),
            P("sys", blk, None, None),
            P("sys", blk, None, None),
            P("sys", blk, None, None),
            P("sys", blk, None),
        ),
        out_specs=P("sys", "inst", None, blk, None, None),
        check_vma=False,
    )
```

```python
import math

import jax
import jax.numpy as jnp
from jax import lax
from jax.experimental import pallas as pl
from jax.experimental.pallas import tpu as pltpu
from jax.sharding import Mesh, PartitionSpec as P

ROTOR_RATE = 0.6
F32 = jnp.float32
BF16 = jnp.bfloat16

FIELDS = 5
INSTANCES = 8
LOCAL = 4
CH = LOCAL * FIELDS
HI = 256
LO = 128
ROWS = 1024
CAP = 16
SLOT = 40
NEAR = 64
PIECE = CAP * SLOT // LO
FIRST = 3
ACCS = 8


def spectra_entry(offset):
    offset %= INSTANCES
    if offset == 0:
        return 0.0
    angle = math.pi * offset / INSTANCES
    return 0.5 * (-1.0) ** offset * math.cos(angle) / math.sin(angle)


def iota(shape, dim):
    return lax.broadcasted_iota(jnp.int32, shape, dim)


def split(x):
    head = x.astype(BF16)
    return head, (x - head.astype(F32)).astype(BF16)


def takes(microseconds):
    return pl.CostEstimate(flops=0, bytes_accessed=microseconds * 3_700_000, transcendentals=0)


def nt_dot(a, b):
    return lax.dot_general(a, b, (((1,), (1,)), ((), ())), preferred_element_type=F32)


def pick_kernel(counts, *refs):
    (cells, *small), (payload, top, bottom) = refs[:5], refs[5:8]
    adj, cell, owner, donor, weight, sem, small_sem = refs[8:]

    def chunk_copy(i):
        here = pl.ds(i * LOCAL, LOCAL)
        return pltpu.make_async_copy(cells.at[here], adj.at[here], sem.at[i])

    copies = [
        pltpu.make_async_copy(operand, place, small_sem.at[i])
        for i, (operand, place) in enumerate(zip(small, (cell, owner, donor, weight)))
    ]
    for copy in copies:
        copy.start()
    for i in range(FIELDS):
        chunk_copy(i).start()
    for copy in copies:
        copy.wait()
    for i in range(FIELDS):
        chunk_copy(i).wait()
    spot = cell[...]
    high = (spot >> 7) & 127
    low = ((spot >> 14) << 7) | (spot & 127)
    lefts = []
    for channel in range(CH):
        whole = adj[channel]
        head, tail = split(jnp.concatenate([whole[:LO], whole[LO:]], axis=1))
        lefts.append(jnp.concatenate([head, tail], axis=1))
    left = jnp.concatenate(lefts, axis=0)
    wide = 256
    for part in range(ROWS // wide):
        cols = slice(part * wide, (part + 1) * wide)
        lows = jnp.where(iota((2 * LO, wide), 0) == low[:, cols], 1.0, 0.0).astype(BF16)
        lows = jnp.concatenate([lows, lows], axis=0)
        here = iota((LO, wide), 0) == high[:, cols]
        found = jnp.dot(left, lows, preferred_element_type=F32)
        for channel in range(CH):
            payload[channel : channel + 1, cols] = jnp.sum(
                jnp.where(here, found[channel * LO : (channel + 1) * LO], 0.0),
                axis=0,
                keepdims=True,
            )
    for group in range(ROWS // LO):
        lanes = slice(group * LO, (group + 1) * LO)
        living = iota((1, LO), 1) < counts[group]
        payload[CH : CH + 1, lanes] = jnp.where(living, owner[:, lanes], -1).astype(F32)
    payload[CH + 1 : 24, :] = jnp.zeros((23 - CH, ROWS), F32)
    payload[24:32, :] = weight[...]
    payload[32:40, :] = donor[...].astype(F32)
    for channel in range(CH):
        top[channel] = adj[channel, HI - 16 :, :]
        bottom[channel] = adj[channel, :16, :]


def pack_kernel(position, own, got, message):
    upto = jnp.where(iota((LO, LO), 0) <= iota((LO, LO), 1), 1.0, 0.0).astype(BF16)
    ones = jnp.ones((LO, LO), BF16)
    for half, payload in enumerate((own, got)):
        rows = payload[...]
        name = rows[CH : CH + 1].astype(jnp.int32)
        near = ((name >> 4) & 1) == position[0]
        name = jnp.where((name >= 0) & near, ((name >> 5) << 4) | (name & 15), -1)
        before = jnp.zeros((NEAR, LO), F32)
        chosen, ranks = [], []
        for group in range(ROWS // LO):
            lanes = slice(group * LO, (group + 1) * LO)
            hit = jnp.where(iota((NEAR, LO), 0) == name[:, lanes], 1.0, 0.0)
            hit16 = hit.astype(BF16)
            count = jnp.dot(hit16, upto, preferred_element_type=F32) + before
            before = before + jnp.dot(hit16, ones, preferred_element_type=F32)
            ranks.append(jnp.sum(hit * count, axis=0, keepdims=True) - 1.0)
            chosen.append(hit16)
        chosen = jnp.concatenate(chosen, axis=1)
        rank = jnp.concatenate(ranks, axis=1)
        placed = jnp.concatenate(
            [jnp.where(rank == float(slot), rows, 0.0) for slot in range(CAP)], axis=0
        )
        head, tail = split(placed)
        table = nt_dot(head, chosen) + nt_dot(tail, chosen)
        for piece in range(PIECE):
            block = table[piece * LO : (piece + 1) * LO].T
            message[pl.ds(half * PIECE + piece, NEAR, stride=2 * PIECE), :] = block


def local_kernel(adj, below, above, gradient, jacobian, coupling, step, out, edge):
    planes = step.shape[0]
    rows = planes * 16
    index = pl.program_id(0)
    last = pl.num_programs(0) - 1
    y = iota((rows, LO), 0) % 16
    z = iota((rows, LO), 1)
    faces = [coupling[d].reshape(rows, LO) for d in range(6)]
    faces[2] = jnp.where(y == 15, 0.0, faces[2])
    faces[3] = jnp.where(y == 0, 0.0, faces[3])
    faces[4] = jnp.where(z == LO - 1, 0.0, faces[4])
    faces[5] = jnp.where(z == 0, 0.0, faces[5])
    tau = step[...].reshape(rows, LO)

    @pl.when(index == 0)
    def _():
        edge[0] = (tau * faces[1])[:16]

    @pl.when(index == last)
    def _():
        edge[1] = (tau * faces[0])[-16:]

    for field in range(FIELDS):
        blocks = [jacobian[g, field].reshape(rows, LO) for g in range(FIELDS)]
        mine = [
            adj[t * FIELDS + field].reshape(rows, LO) for t in range(LOCAL)
        ]
        for t in range(LOCAL):
            channel = t * FIELDS + field
            own = mine[t]
            total = -gradient[channel].reshape(rows, LO)
            for g in range(FIELDS):
                total = total + blocks[g] * adj[t * FIELDS + g].reshape(rows, LO)
            next_plane = jnp.where(index == last, 0.0, above[channel, 0])
            past_plane = jnp.where(index == 0, 0.0, below[channel, 0])
            total = total - faces[0] * jnp.concatenate([own[16:], next_plane], axis=0)
            total = total - faces[1] * jnp.concatenate([past_plane, own[:-16]], axis=0)
            total = total - faces[2] * pltpu.roll(own, rows - 1, 0)
            total = total - faces[3] * pltpu.roll(own, 1, 0)
            total = total - faces[4] * pltpu.roll(own, LO - 1, 1)
            total = total - faces[5] * pltpu.roll(own, 1, 1)
            for s in range(LOCAL):
                if s != t:
                    total = total + (ROTOR_RATE * spectra_entry(s - t)) * mine[s]
            out[channel] = (own - tau * total).reshape(planes, 16, LO)


def fringe_kernel(rows, partial, step, out, *scratch):
    accs = scratch[:ACCS]
    flat, expand, order, places, indices, products, held, sem, held_sem = scratch[ACCS:]
    fetch = pltpu.make_async_copy(partial, held, held_sem)
    fetch.start()
    for piece in range(PIECE):
        flat[pl.ds(piece * LO, LO), :] = rows[pl.ds(piece, LO, stride=PIECE), :].T

    weights = jnp.concatenate(
        [flat[slot * SLOT + 24 : slot * SLOT + 32, :] for slot in range(CAP)], axis=0
    )
    alive = jnp.where(weights > 0.0, 1.0, 0.0)
    upto = jnp.where(iota((LO, LO), 0) <= iota((LO, LO), 1), 1.0, 0.0).astype(BF16)
    rank = jnp.dot(alive.astype(BF16), upto, preferred_element_type=F32) * alive - 1.0
    order[...] = rank.astype(jnp.int32)
    places[LO : LO + 8, :] = nt_dot(jnp.ones((8, LO), BF16), alive.astype(BF16)).astype(jnp.int32)

    def move_of(slot):
        target = order[pl.ds(pl.multiple_of(slot * 8, 8), 1), :]
        return jnp.where(iota((LO, LO), 0) == target, 1.0, 0.0).astype(BF16)

    @pl.loop(0, CAP // 4)
    def _(four):
        for i in range(4):
            slot = four * 4 + i
            spot = flat[pl.ds(pl.multiple_of(slot * SLOT, 8) + 32, 8), :]
            head = spot.astype(BF16).astype(F32)
            both = jnp.concatenate([head, spot - head], axis=0).astype(BF16)
            both = nt_dot(both, move_of(slot))
            spot = (both[:8] + both[8:]).astype(jnp.int32)
            places[pl.ds(pl.multiple_of(slot * 8, 8), 8), :] = ((spot >> 9) << 7) | (spot & 127)

    copy = pltpu.make_async_copy(places, indices, sem)
    copy.start()

    row = iota((LO, LO), 0)
    lane = iota((LO, LO), 1)
    value_row = jnp.where(row < 24, row, row - 24)
    hit = (row < 48) & (value_row == lane // 4)
    expand[:, 0:LO] = jnp.where(hit, 1.0, 0.0).astype(BF16)
    weight_row = jnp.where(row < 80, row - 48, row - 80)
    for k in range(8):
        hit = (row >= 48) & (row < 112) & (weight_row == (lane % 4) * 8 + k)
        expand[:, (k + 1) * LO : (k + 2) * LO] = jnp.where(hit, 1.0, 0.0).astype(BF16)

    @pl.loop(0, CAP // 4)
    def _(four):
        for i in range(4):
            slot = four * 4 + i
            base = pl.multiple_of(slot * SLOT, 8)
            values = flat[pl.ds(base, 24), :]
            weights = flat[pl.ds(base + 24, 8), :]
            quarter = (flat[pl.ds(base + 32, 8), :].astype(jnp.int32) >> 7) & 3
            weights = jnp.concatenate(
                [jnp.where(quarter == q, weights, 0.0) for q in range(4)], axis=0
            )
            values_head = values.astype(BF16).astype(F32)
            weights_head = weights.astype(BF16).astype(F32)
            left = jnp.concatenate(
                [
                    values_head,
                    values - values_head,
                    weights_head,
                    weights - weights_head,
                    jnp.zeros((16, LO), F32),
                ],
                axis=0,
            )
            turned = nt_dot(move_of(slot), left.astype(BF16)).astype(BF16)
            both = jnp.dot(turned, expand[...], preferred_element_type=F32)
            here = pl.ds(pl.multiple_of(slot * LO, LO), LO)
            for k in range(8):
                products[k, here, :] = both[:, 0:LO] * both[:, (k + 1) * LO : (k + 2) * LO]

    zeros = jnp.zeros((64, LO), F32)

    @pl.loop(0, 8192 // 64)
    def _(i):
        for acc in accs:
            acc[pl.ds(pl.multiple_of(i * 64, 64), 64), :] = zeros

    copy.wait()
    listed = indices.reshape((LO + 8) * LO)

    @pl.loop(0, CAP)
    def _(slot):
        unroll = 8

        @pl.loop(0, (listed[LO * LO + slot * 8] + (unroll - 1)) // unroll)
        def _(chunk):
            for u in range(unroll):
                source = chunk * unroll + u
                for k in range(8):
                    acc = accs[k % ACCS]
                    place = listed[slot * 8 * LO + chunk * unroll + (k * LO + u)]
                    acc[pl.ds(place, 1), :] = (
                        acc[pl.ds(place, 1), :] + products[k, pl.ds(slot * LO + source, 1), :]
                    )

    fetch.wait()

    @pl.loop(0, HI // 8, unroll=4)
    def _(i):
        turned = []
        for half in range(2):
            begin = pl.multiple_of(i * 256 + half * LO, LO)
            total = accs[0][pl.ds(begin, LO), :]
            for acc in accs[1:]:
                total = total + acc[pl.ds(begin, LO), :]
            turned.append(total.T)
        here = pl.ds(pl.multiple_of(i * 8, 8), 8)
        tau = step[here, :]
        for channel in range(CH):
            cells = slice(channel * 4, channel * 4 + 4)
            gained = jnp.concatenate([turned[0][cells], turned[1][cells]], axis=0)
            out[channel, here, :] = held[channel, here, :] - tau * gained


def final_kernel(
    partial, first, rest, step, before, after, crossed_up, crossed_down, edge, out, ready, sem
):
    steps = 8
    wide = HI // steps

    def copy_of(i):
        here = pl.ds(pl.multiple_of(i * wide, wide), wide)
        return pltpu.make_async_copy(ready.at[:, here, :], out.at[:, here, :], sem.at[i])

    def block(i):
        here = pl.ds(pl.multiple_of(i * wide, wide), wide)
        tau = step[here, :]
        for field in range(FIELDS):
            channels = [s * FIELDS + field for s in range(LOCAL)]
            others = [
                first[c, here, :] if c < FIRST else rest[c - FIRST, here, :] for c in channels
            ]
            for t in range(LOCAL):
                total = None
                for s in range(LOCAL):
                    if s == t:
                        continue
                    term = (ROTOR_RATE * spectra_entry(s - t + LOCAL)) * others[s]
                    total = term if total is None else total + term
                channel = channels[t]
                ready[channel, here, :] = partial[channel, here, :] - tau * total

    @pl.loop(0, steps)
    def _(i):
        block(i)

        @pl.when(i == 0)
        def _():
            for channel in range(CH):
                ready[channel, :16, :] += edge[0] * (before[channel] + crossed_up[channel])

        @pl.when(i == steps - 1)
        def _():
            for channel in range(CH):
                ready[channel, HI - 16 :, :] += edge[1] * (after[channel] + crossed_down[channel])

        copy_of(i).start()

    for i in range(steps):
        copy_of(i).wait()


def shards(
    adjoint,
    gradient,
    jacobian,
    coupling,
    pseudo_step,
    receptor_cell,
    donor_owner,
    donor_cell,
    donor_weight,
    block_count,
):
    swap = [(0, 1), (1, 0)]
    cells = adjoint.reshape(CH, HI, LO)
    planes = adjoint.reshape(CH, 16, 16, LO)
    vmem = pl.BlockSpec(memory_space=pltpu.VMEM)
    smem = pl.BlockSpec(memory_space=pltpu.SMEM)
    hbm = pl.BlockSpec(memory_space=pltpu.HBM)

    first = lax.ppermute(cells[:FIRST], "inst", swap)
    payload, top, bottom = pl.pallas_call(
        pick_kernel,
        out_shape=[
            jax.ShapeDtypeStruct((SLOT, ROWS), F32),
            jax.ShapeDtypeStruct((CH, 16, LO), F32),
            jax.ShapeDtypeStruct((CH, 16, LO), F32),
        ],
        in_specs=[smem] + [hbm] * 5,
        out_specs=[vmem] * 3,
        scratch_shapes=[
            pltpu.VMEM((CH, HI, LO), F32),
            pltpu.VMEM((1, ROWS), jnp.int32),
            pltpu.VMEM((1, ROWS), jnp.int32),
            pltpu.VMEM((8, ROWS), jnp.int32),
            pltpu.VMEM((8, ROWS), F32),
            pltpu.SemaphoreType.DMA((FIELDS,)),
            pltpu.SemaphoreType.DMA((4,)),
        ],
        compiler_params=pltpu.CompilerParams(vmem_limit_bytes=56 * 2**20),
        cost_estimate=takes(5),
        name="pick",
    )(
        block_count.reshape(8),
        cells,
        receptor_cell.reshape(1, ROWS),
        donor_owner.reshape(1, ROWS),
        donor_cell.reshape(8, ROWS),
        donor_weight.reshape(8, ROWS),
    )
    got = lax.ppermute(payload, "xl", swap)
    half = lax.axis_size("zc")
    crossed = (
        lax.ppermute(top, ("xl", "zc"), [(half - 1, half)]),
        lax.ppermute(bottom, ("xl", "zc"), [(half, half - 1)]),
    )
    rest, got, first, crossed = lax.optimization_barrier((cells[FIRST:], got, first, crossed))
    rest = lax.ppermute(rest, "inst", swap)

    message = pl.pallas_call(
        pack_kernel,
        out_shape=jax.ShapeDtypeStruct((NEAR * 2 * PIECE, LO), F32),
        in_specs=[smem, vmem, vmem],
        out_specs=vmem,
        compiler_params=pltpu.CompilerParams(vmem_limit_bytes=32 * 2**20),
        cost_estimate=takes(3),
        name="pack",
    )(lax.axis_index("xl").astype(jnp.int32).reshape(1), payload, got)
    message, gradient, top, bottom = lax.optimization_barrier((message, gradient, top, bottom))
    arrived = lax.all_to_all(
        message.reshape(-1), ("sys", "zc"), split_axis=0, concat_axis=0, tiled=True
    )
    inside = [i for i in range(2 * half - 1) if i != half - 1]
    before = lax.ppermute(top, ("xl", "zc"), [(i, i + 1) for i in inside])
    after = lax.ppermute(bottom, ("xl", "zc"), [(i + 1, i) for i in inside])

    steps = 4
    wide = 16 // steps
    partial, edge = pl.pallas_call(
        local_kernel,
        grid=(steps,),
        out_shape=[
            jax.ShapeDtypeStruct((CH, 16, 16, LO), F32),
            jax.ShapeDtypeStruct((2, 16, LO), F32),
        ],
        in_specs=[
            pl.BlockSpec((CH, wide, 16, LO), lambda i: (0, i, 0, 0)),
            pl.BlockSpec((CH, 1, 16, LO), lambda i: (0, jnp.maximum(wide * i - 1, 0), 0, 0)),
            pl.BlockSpec((CH, 1, 16, LO), lambda i: (0, jnp.minimum(wide * i + wide, 15), 0, 0)),
            pl.BlockSpec((CH, wide, 16, LO), lambda i: (0, i, 0, 0)),
            pl.BlockSpec((FIELDS, FIELDS, wide, 16, LO), lambda i: (0, 0, i, 0, 0)),
            pl.BlockSpec((6, wide, 16, LO), lambda i: (0, i, 0, 0)),
            pl.BlockSpec((wide, 16, LO), lambda i: (i, 0, 0)),
        ],
        out_specs=[
            pl.BlockSpec((CH, wide, 16, LO), lambda i: (0, i, 0, 0)),
            pl.BlockSpec((2, 16, LO), lambda i: (0, 0, 0)),
        ],
        compiler_params=pltpu.CompilerParams(vmem_limit_bytes=56 * 2**20),
        cost_estimate=takes(6),
        name="local",
    )(
        planes,
        planes,
        planes,
        gradient.reshape(CH, 16, 16, LO),
        jacobian.reshape(FIELDS, FIELDS, 16, 16, LO),
        coupling.reshape(6, 16, 16, LO),
        pseudo_step.reshape(16, 16, LO),
    )

    arrived, partial = lax.optimization_barrier((arrived, partial))
    tau = pseudo_step.reshape(HI, LO)
    partial = pl.pallas_call(
        fringe_kernel,
        out_shape=jax.ShapeDtypeStruct((CH, HI, LO), F32),
        in_specs=[vmem, hbm, vmem],
        out_specs=vmem,
        scratch_shapes=[pltpu.VMEM((8192, LO), F32)] * ACCS
        + [
            pltpu.VMEM((CAP * SLOT, LO), F32),
            pltpu.VMEM((LO, 9 * LO), BF16),
            pltpu.VMEM((LO, LO), jnp.int32),
            pltpu.VMEM((LO + 8, LO), jnp.int32),
            pltpu.SMEM((LO + 8, LO), jnp.int32),
            pltpu.VMEM((8, CAP * LO, LO), F32),
            pltpu.VMEM((CH, HI, LO), F32),
            pltpu.SemaphoreType.DMA,
            pltpu.SemaphoreType.DMA,
        ],
        compiler_params=pltpu.CompilerParams(vmem_limit_bytes=50 * 2**20),
        cost_estimate=takes(25),
        name="fringe",
    )(arrived.reshape(128 * PIECE, LO), partial.reshape(CH, HI, LO), tau)

    result = pl.pallas_call(
        final_kernel,
        out_shape=jax.ShapeDtypeStruct((CH, HI, LO), F32),
        in_specs=[vmem] * 9,
        out_specs=pl.BlockSpec(memory_space=pl.ANY),
        scratch_shapes=[pltpu.VMEM((CH, HI, LO), F32), pltpu.SemaphoreType.DMA((8,))],
        compiler_params=pltpu.CompilerParams(vmem_limit_bytes=40 * 2**20),
        cost_estimate=takes(2),
        name="final",
    )(partial, first, rest, tau, before, after, *crossed, edge)
    return result.reshape(adjoint.shape)


def solution(mesh):
    fine = Mesh(mesh.devices.reshape(4, 2, 16, 2), ("sys", "xl", "zc", "inst"))
    blk = ("xl", "zc")
    return jax.shard_map(
        shards,
        mesh=fine,
        in_specs=(
            P("sys", "inst", None, blk, None, None),
            P("sys", "inst", None, blk, None, None),
            P("sys", None, None, blk, None, None),
            P("sys", None, blk, None, None),
            P("sys", blk, None, None),
            P("sys", blk, None),
            P("sys", blk, None, None),
            P("sys", blk, None, None),
            P("sys", blk, None, None),
            P("sys", blk, None),
        ),
        out_specs=P("sys", "inst", None, blk, None, None),
        check_vma=False,
    )
```

```python
import math

import jax
import jax.numpy as jnp
from jax import lax
from jax.experimental import pallas as pl
from jax.experimental.pallas import tpu as pltpu
from jax.sharding import Mesh, PartitionSpec as P

ROTOR_RATE = 0.6
F32 = jnp.float32
BF16 = jnp.bfloat16

FIELDS = 5
INSTANCES = 8
LOCAL = 4
CH = LOCAL * FIELDS
HI = 256
LO = 128
ROWS = 1024
CAP = 16
SLOT = 40
NEAR = 64
PIECE = CAP * SLOT // LO
FIRST = 10
ACCS = 8


def spectra_entry(offset):
    offset %= INSTANCES
    if offset == 0:
        return 0.0
    angle = math.pi * offset / INSTANCES
    return 0.5 * (-1.0) ** offset * math.cos(angle) / math.sin(angle)


def iota(shape, dim):
    return lax.broadcasted_iota(jnp.int32, shape, dim)


def split(x):
    head = x.astype(BF16)
    return head, (x - head.astype(F32)).astype(BF16)


def takes(microseconds):
    return pl.CostEstimate(flops=0, bytes_accessed=microseconds * 3_700_000, transcendentals=0)


def nt_dot(a, b):
    return lax.dot_general(a, b, (((1,), (1,)), ((), ())), preferred_element_type=F32)


def pick_kernel(counts, *refs):
    (cells, *small), (payload, top, bottom) = refs[:5], refs[5:8]
    adj, cell, owner, donor, weight, sem, small_sem = refs[8:]

    def chunk_copy(i):
        here = pl.ds(i * LOCAL, LOCAL)
        return pltpu.make_async_copy(cells.at[here], adj.at[here], sem.at[i])

    copies = [
        pltpu.make_async_copy(operand, place, small_sem.at[i])
        for i, (operand, place) in enumerate(zip(small, (cell, owner, donor, weight)))
    ]
    for copy in copies:
        copy.start()
    for i in range(FIELDS):
        chunk_copy(i).start()
    for copy in copies:
        copy.wait()
    for i in range(FIELDS):
        chunk_copy(i).wait()
    spot = cell[...]
    high = (spot >> 7) & 127
    low = ((spot >> 14) << 7) | (spot & 127)
    lefts = []
    for channel in range(CH):
        whole = adj[channel]
        head, tail = split(jnp.concatenate([whole[:LO], whole[LO:]], axis=1))
        lefts.append(jnp.concatenate([head, tail], axis=1))
    left = jnp.concatenate(lefts, axis=0)
    wide = 256
    for part in range(ROWS // wide):
        cols = slice(part * wide, (part + 1) * wide)
        lows = jnp.where(iota((2 * LO, wide), 0) == low[:, cols], 1.0, 0.0).astype(BF16)
        lows = jnp.concatenate([lows, lows], axis=0)
        here = iota((LO, wide), 0) == high[:, cols]
        found = jnp.dot(left, lows, preferred_element_type=F32)
        for channel in range(CH):
            payload[channel : channel + 1, cols] = jnp.sum(
                jnp.where(here, found[channel * LO : (channel + 1) * LO], 0.0),
                axis=0,
                keepdims=True,
            )
    for group in range(ROWS // LO):
        lanes = slice(group * LO, (group + 1) * LO)
        living = iota((1, LO), 1) < counts[group]
        payload[CH : CH + 1, lanes] = jnp.where(living, owner[:, lanes], -1).astype(F32)
    payload[CH + 1 : 24, :] = jnp.zeros((23 - CH, ROWS), F32)
    payload[24:32, :] = weight[...]
    payload[32:40, :] = donor[...].astype(F32)
    for channel in range(CH):
        top[channel] = adj[channel, HI - 16 :, :]
        bottom[channel] = adj[channel, :16, :]


def pack_kernel(position, own, got, message):
    upto = jnp.where(iota((LO, LO), 0) <= iota((LO, LO), 1), 1.0, 0.0).astype(BF16)
    ones = jnp.ones((LO, LO), BF16)
    for half, payload in enumerate((own, got)):
        rows = payload[...]
        name = rows[CH : CH + 1].astype(jnp.int32)
        near = ((name >> 4) & 1) == position[0]
        name = jnp.where((name >= 0) & near, ((name >> 5) << 4) | (name & 15), -1)
        before = jnp.zeros((NEAR, LO), F32)
        chosen, ranks = [], []
        for group in range(ROWS // LO):
            lanes = slice(group * LO, (group + 1) * LO)
            hit = jnp.where(iota((NEAR, LO), 0) == name[:, lanes], 1.0, 0.0)
            hit16 = hit.astype(BF16)
            count = jnp.dot(hit16, upto, preferred_element_type=F32) + before
            before = before + jnp.dot(hit16, ones, preferred_element_type=F32)
            ranks.append(jnp.sum(hit * count, axis=0, keepdims=True) - 1.0)
            chosen.append(hit16)
        chosen = jnp.concatenate(chosen, axis=1)
        rank = jnp.concatenate(ranks, axis=1)
        placed = jnp.concatenate(
            [jnp.where(rank == float(slot), rows, 0.0) for slot in range(CAP)], axis=0
        )
        head, tail = split(placed)
        table = nt_dot(head, chosen) + nt_dot(tail, chosen)
        for piece in range(PIECE):
            block = table[piece * LO : (piece + 1) * LO].T
            message[pl.ds(half * PIECE + piece, NEAR, stride=2 * PIECE), :] = block


def local_kernel(adj, below, above, gradient, jacobian, coupling, step, out, edge):
    planes = step.shape[0]
    rows = planes * 16
    index = pl.program_id(0)
    last = pl.num_programs(0) - 1
    y = iota((rows, LO), 0) % 16
    z = iota((rows, LO), 1)
    faces = [coupling[d].reshape(rows, LO) for d in range(6)]
    faces[2] = jnp.where(y == 15, 0.0, faces[2])
    faces[3] = jnp.where(y == 0, 0.0, faces[3])
    faces[4] = jnp.where(z == LO - 1, 0.0, faces[4])
    faces[5] = jnp.where(z == 0, 0.0, faces[5])
    tau = step[...].reshape(rows, LO)

    @pl.when(index == 0)
    def _():
        edge[0] = (tau * faces[1])[:16]

    @pl.when(index == last)
    def _():
        edge[1] = (tau * faces[0])[-16:]

    for field in range(FIELDS):
        blocks = [jacobian[g, field].reshape(rows, LO) for g in range(FIELDS)]
        mine = [
            adj[t * FIELDS + field].reshape(rows, LO) for t in range(LOCAL)
        ]
        for t in range(LOCAL):
            channel = t * FIELDS + field
            own = mine[t]
            total = -gradient[channel].reshape(rows, LO)
            for g in range(FIELDS):
                total = total + blocks[g] * adj[t * FIELDS + g].reshape(rows, LO)
            next_plane = jnp.where(index == last, 0.0, above[channel, 0])
            past_plane = jnp.where(index == 0, 0.0, below[channel, 0])
            total = total - faces[0] * jnp.concatenate([own[16:], next_plane], axis=0)
            total = total - faces[1] * jnp.concatenate([past_plane, own[:-16]], axis=0)
            total = total - faces[2] * pltpu.roll(own, rows - 1, 0)
            total = total - faces[3] * pltpu.roll(own, 1, 0)
            total = total - faces[4] * pltpu.roll(own, LO - 1, 1)
            total = total - faces[5] * pltpu.roll(own, 1, 1)
            for s in range(LOCAL):
                if s != t:
                    total = total + (ROTOR_RATE * spectra_entry(s - t)) * mine[s]
            out[channel] = (own - tau * total).reshape(planes, 16, LO)


def fringe_kernel(rows, partial, step, out, *scratch):
    accs = scratch[:ACCS]
    flat, expand, order, places, indices, products, held, sem, held_sem, out_sem = scratch[ACCS:]
    fetch = pltpu.make_async_copy(partial, held, held_sem)
    fetch.start()
    for piece in range(PIECE):
        flat[pl.ds(piece * LO, LO), :] = rows[pl.ds(piece, LO, stride=PIECE), :].T

    weights = jnp.concatenate(
        [flat[slot * SLOT + 24 : slot * SLOT + 32, :] for slot in range(CAP)], axis=0
    )
    alive = jnp.where(weights > 0.0, 1.0, 0.0)
    upto = jnp.where(iota((LO, LO), 0) <= iota((LO, LO), 1), 1.0, 0.0).astype(BF16)
    rank = jnp.dot(alive.astype(BF16), upto, preferred_element_type=F32) * alive - 1.0
    order[...] = rank.astype(jnp.int32)
    places[LO : LO + 8, :] = nt_dot(jnp.ones((8, LO), BF16), alive.astype(BF16)).astype(jnp.int32)

    def move_of(slot):
        target = order[pl.ds(pl.multiple_of(slot * 8, 8), 1), :]
        return jnp.where(iota((LO, LO), 0) == target, 1.0, 0.0).astype(BF16)

    @pl.loop(0, CAP // 4)
    def _(four):
        for i in range(4):
            slot = four * 4 + i
            spot = flat[pl.ds(pl.multiple_of(slot * SLOT, 8) + 32, 8), :]
            head = spot.astype(BF16).astype(F32)
            both = jnp.concatenate([head, spot - head], axis=0).astype(BF16)
            both = nt_dot(both, move_of(slot))
            spot = (both[:8] + both[8:]).astype(jnp.int32)
            places[pl.ds(pl.multiple_of(slot * 8, 8), 8), :] = ((spot >> 9) << 7) | (spot & 127)

    copy = pltpu.make_async_copy(places, indices, sem)
    copy.start()

    row = iota((LO, LO), 0)
    lane = iota((LO, LO), 1)
    value_row = jnp.where(row < 24, row, row - 24)
    hit = (row < 48) & (value_row == lane // 4)
    expand[:, 0:LO] = jnp.where(hit, 1.0, 0.0).astype(BF16)
    weight_row = jnp.where(row < 80, row - 48, row - 80)
    for k in range(8):
        hit = (row >= 48) & (row < 112) & (weight_row == (lane % 4) * 8 + k)
        expand[:, (k + 1) * LO : (k + 2) * LO] = jnp.where(hit, 1.0, 0.0).astype(BF16)

    @pl.loop(0, CAP // 4)
    def _(four):
        for i in range(4):
            slot = four * 4 + i
            base = pl.multiple_of(slot * SLOT, 8)
            values = flat[pl.ds(base, 24), :]
            weights = flat[pl.ds(base + 24, 8), :]
            quarter = (flat[pl.ds(base + 32, 8), :].astype(jnp.int32) >> 7) & 3
            weights = jnp.concatenate(
                [jnp.where(quarter == q, weights, 0.0) for q in range(4)], axis=0
            )
            values_head = values.astype(BF16).astype(F32)
            weights_head = weights.astype(BF16).astype(F32)
            left = jnp.concatenate(
                [
                    values_head,
                    values - values_head,
                    weights_head,
                    weights - weights_head,
                    jnp.zeros((16, LO), F32),
                ],
                axis=0,
            )
            turned = nt_dot(move_of(slot), left.astype(BF16)).astype(BF16)
            both = jnp.dot(turned, expand[...], preferred_element_type=F32)
            here = pl.ds(pl.multiple_of(slot * LO, LO), LO)
            for k in range(8):
                products[k, here, :] = both[:, 0:LO] * both[:, (k + 1) * LO : (k + 2) * LO]

    zeros = jnp.zeros((64, LO), F32)

    @pl.loop(0, 8192 // 64)
    def _(i):
        for acc in accs:
            acc[pl.ds(pl.multiple_of(i * 64, 64), 64), :] = zeros

    copy.wait()
    listed = indices.reshape((LO + 8) * LO)

    @pl.loop(0, CAP)
    def _(slot):
        unroll = 8

        @pl.loop(0, (listed[LO * LO + slot * 8] + (unroll - 1)) // unroll)
        def _(chunk):
            for u in range(unroll):
                source = chunk * unroll + u
                for k in range(8):
                    acc = accs[k % ACCS]
                    place = listed[slot * 8 * LO + chunk * unroll + (k * LO + u)]
                    acc[pl.ds(place, 1), :] = (
                        acc[pl.ds(place, 1), :] + products[k, pl.ds(slot * LO + source, 1), :]
                    )

    fetch.wait()

    steps = 8
    wide = HI // steps

    def copy_of(i):
        here = pl.ds(pl.multiple_of(i * wide, wide), wide)
        return pltpu.make_async_copy(held.at[:, here, :], out.at[:, here, :], out_sem.at[i])

    @pl.loop(0, steps)
    def _(step_index):
        for part in range(wide // 8):
            i = step_index * (wide // 8) + part
            turned = []
            for half in range(2):
                begin = pl.multiple_of(i * 256 + half * LO, LO)
                total = accs[0][pl.ds(begin, LO), :]
                for acc in accs[1:]:
                    total = total + acc[pl.ds(begin, LO), :]
                turned.append(total.T)
            here = pl.ds(pl.multiple_of(i * 8, 8), 8)
            tau = step[here, :]
            for channel in range(CH):
                cells = slice(channel * 4, channel * 4 + 4)
                gained = jnp.concatenate([turned[0][cells], turned[1][cells]], axis=0)
                held[channel, here, :] = held[channel, here, :] - tau * gained
        copy_of(step_index).start()

    for i in range(steps):
        copy_of(i).wait()


def final_kernel(group, step, edge, *refs):
    (source, gathered, permuted, below, above, out), refs = refs[:6], refs[6:]
    first, rest, before, after, ready, sem, first_sem, rest_sem, own_sem, face_sem = refs
    steps = 8
    wide = HI // steps

    def copy_of(i):
        here = pl.ds(pl.multiple_of(i * wide, wide), wide)
        return pltpu.make_async_copy(ready.at[:, here, :], out.at[:, here, :], sem.at[i])

    def fetch_of(i):
        here = pl.ds(pl.multiple_of(i * wide, wide), wide)
        other = gathered.at[1 - group[0], :, here, :]
        return (
            pltpu.make_async_copy(other, first.at[:, here, :], first_sem.at[i]),
            pltpu.make_async_copy(permuted.at[:, here, :], rest.at[:, here, :], rest_sem.at[i]),
            pltpu.make_async_copy(source.at[:, here, :], ready.at[:, here, :], own_sem.at[i]),
        )

    faces = (
        pltpu.make_async_copy(below, before, face_sem.at[0]),
        pltpu.make_async_copy(above, after, face_sem.at[1]),
    )
    for i in range(steps):
        for copy in fetch_of(i):
            copy.start()
        if i == 0:
            for copy in faces:
                copy.start()
    for copy in faces:
        copy.wait()

    def block(i):
        here = pl.ds(pl.multiple_of(i * wide, wide), wide)
        for copy in fetch_of(i):
            copy.wait()
        tau = step[here, :]
        for field in range(FIELDS):
            channels = [s * FIELDS + field for s in range(LOCAL)]
            others = [
                first[c, here, :] if c < FIRST else rest[c - FIRST, here, :] for c in channels
            ]
            for t in range(LOCAL):
                total = None
                for s in range(LOCAL):
                    if s == t:
                        continue
                    term = (ROTOR_RATE * spectra_entry(s - t + LOCAL)) * others[s]
                    total = term if total is None else total + term
                channel = channels[t]
                ready[channel, here, :] = ready[channel, here, :] - tau * total

    @pl.loop(0, steps)
    def _(i):
        block(i)

        @pl.when(i == 0)
        def _():
            for channel in range(CH):
                ready[channel, :16, :] += edge[0] * before[channel]

        @pl.when(i == steps - 1)
        def _():
            for channel in range(CH):
                ready[channel, HI - 16 :, :] += edge[1] * after[channel]

        copy_of(i).start()

    for i in range(steps):
        copy_of(i).wait()


def shards(
    adjoint,
    gradient,
    jacobian,
    coupling,
    pseudo_step,
    receptor_cell,
    donor_owner,
    donor_cell,
    donor_weight,
    block_count,
):
    swap = [(0, 1), (1, 0)]
    blocks = lax.axis_size("xl") * lax.axis_size("zc")
    cells = adjoint.reshape(CH, HI, LO)
    planes = adjoint.reshape(CH, 16, 16, LO)
    vmem = pl.BlockSpec(memory_space=pltpu.VMEM)
    smem = pl.BlockSpec(memory_space=pltpu.SMEM)
    hbm = pl.BlockSpec(memory_space=pltpu.HBM)

    first = lax.all_gather(cells[:FIRST], "inst")
    payload, top, bottom = pl.pallas_call(
        pick_kernel,
        out_shape=[
            jax.ShapeDtypeStruct((SLOT, ROWS), F32),
            jax.ShapeDtypeStruct((CH, 16, LO), F32),
            jax.ShapeDtypeStruct((CH, 16, LO), F32),
        ],
        in_specs=[smem] + [hbm] * 5,
        out_specs=[vmem] * 3,
        scratch_shapes=[
            pltpu.VMEM((CH, HI, LO), F32),
            pltpu.VMEM((1, ROWS), jnp.int32),
            pltpu.VMEM((1, ROWS), jnp.int32),
            pltpu.VMEM((8, ROWS), jnp.int32),
            pltpu.VMEM((8, ROWS), F32),
            pltpu.SemaphoreType.DMA((FIELDS,)),
            pltpu.SemaphoreType.DMA((4,)),
        ],
        compiler_params=pltpu.CompilerParams(vmem_limit_bytes=56 * 2**20),
        cost_estimate=takes(5),
        name="pick",
    )(
        block_count.reshape(8),
        cells,
        receptor_cell.reshape(1, ROWS),
        donor_owner.reshape(1, ROWS),
        donor_cell.reshape(8, ROWS),
        donor_weight.reshape(8, ROWS),
    )
    got = lax.ppermute(payload, "xl", swap)
    rest, got = lax.optimization_barrier((cells[FIRST:], got))
    rest = lax.ppermute(rest, "inst", swap)

    message = pl.pallas_call(
        pack_kernel,
        out_shape=jax.ShapeDtypeStruct((NEAR * 2 * PIECE, LO), F32),
        in_specs=[smem, vmem, vmem],
        out_specs=vmem,
        compiler_params=pltpu.CompilerParams(vmem_limit_bytes=32 * 2**20),
        cost_estimate=takes(3),
        name="pack",
    )(lax.axis_index("xl").astype(jnp.int32).reshape(1), payload, got)
    message, gradient, top, bottom = lax.optimization_barrier((message, gradient, top, bottom))
    arrived = lax.all_to_all(
        message.reshape(-1), ("sys", "zc"), split_axis=0, concat_axis=0, tiled=True
    )
    before = lax.ppermute(top, ("xl", "zc"), [(i, i + 1) for i in range(blocks - 1)])
    after = lax.ppermute(bottom, ("xl", "zc"), [(i + 1, i) for i in range(blocks - 1)])

    steps = 4
    wide = 16 // steps
    partial, edge = pl.pallas_call(
        local_kernel,
        grid=(steps,),
        out_shape=[
            jax.ShapeDtypeStruct((CH, 16, 16, LO), F32),
            jax.ShapeDtypeStruct((2, 16, LO), F32),
        ],
        in_specs=[
            pl.BlockSpec((CH, wide, 16, LO), lambda i: (0, i, 0, 0)),
            pl.BlockSpec((CH, 1, 16, LO), lambda i: (0, jnp.maximum(wide * i - 1, 0), 0, 0)),
            pl.BlockSpec((CH, 1, 16, LO), lambda i: (0, jnp.minimum(wide * i + wide, 15), 0, 0)),
            pl.BlockSpec((CH, wide, 16, LO), lambda i: (0, i, 0, 0)),
            pl.BlockSpec((FIELDS, FIELDS, wide, 16, LO), lambda i: (0, 0, i, 0, 0)),
            pl.BlockSpec((6, wide, 16, LO), lambda i: (0, i, 0, 0)),
            pl.BlockSpec((wide, 16, LO), lambda i: (i, 0, 0)),
        ],
        out_specs=[
            pl.BlockSpec((CH, wide, 16, LO), lambda i: (0, i, 0, 0)),
            pl.BlockSpec((2, 16, LO), lambda i: (0, 0, 0)),
        ],
        compiler_params=pltpu.CompilerParams(vmem_limit_bytes=56 * 2**20),
        cost_estimate=takes(6),
        name="local",
    )(
        planes,
        planes,
        planes,
        gradient.reshape(CH, 16, 16, LO),
        jacobian.reshape(FIELDS, FIELDS, 16, 16, LO),
        coupling.reshape(6, 16, 16, LO),
        pseudo_step.reshape(16, 16, LO),
    )

    arrived, partial = lax.optimization_barrier((arrived, partial))
    tau = pseudo_step.reshape(HI, LO)
    partial = pl.pallas_call(
        fringe_kernel,
        out_shape=jax.ShapeDtypeStruct((CH, HI, LO), F32),
        in_specs=[vmem, hbm, vmem],
        out_specs=hbm,
        scratch_shapes=[pltpu.VMEM((8192, LO), F32)] * ACCS
        + [
            pltpu.VMEM((CAP * SLOT, LO), F32),
            pltpu.VMEM((LO, 9 * LO), BF16),
            pltpu.VMEM((LO, LO), jnp.int32),
            pltpu.VMEM((LO + 8, LO), jnp.int32),
            pltpu.SMEM((LO + 8, LO), jnp.int32),
            pltpu.VMEM((8, CAP * LO, LO), F32),
            pltpu.VMEM((CH, HI, LO), F32),
            pltpu.SemaphoreType.DMA,
            pltpu.SemaphoreType.DMA,
            pltpu.SemaphoreType.DMA((8,)),
        ],
        compiler_params=pltpu.CompilerParams(vmem_limit_bytes=50 * 2**20),
        cost_estimate=takes(25),
        name="fringe",
    )(arrived.reshape(128 * PIECE, LO), partial.reshape(CH, HI, LO), tau)

    result = pl.pallas_call(
        final_kernel,
        out_shape=jax.ShapeDtypeStruct((CH, HI, LO), F32),
        in_specs=[smem] + [vmem] * 2 + [pl.BlockSpec(memory_space=pl.ANY)] * 5,
        out_specs=pl.BlockSpec(memory_space=pl.ANY),
        scratch_shapes=[
            pltpu.VMEM((FIRST, HI, LO), F32),
            pltpu.VMEM((CH - FIRST, HI, LO), F32),
            pltpu.VMEM((CH, 16, LO), F32),
            pltpu.VMEM((CH, 16, LO), F32),
            pltpu.VMEM((CH, HI, LO), F32),
            pltpu.SemaphoreType.DMA((8,)),
            pltpu.SemaphoreType.DMA((8,)),
            pltpu.SemaphoreType.DMA((8,)),
            pltpu.SemaphoreType.DMA((8,)),
            pltpu.SemaphoreType.DMA((2,)),
        ],
        compiler_params=pltpu.CompilerParams(vmem_limit_bytes=51 * 2**20),
        cost_estimate=takes(2),
        name="final",
    )(
        lax.axis_index("inst").astype(jnp.int32).reshape(1),
        tau,
        edge,
        partial,
        first,
        rest,
        before,
        after,
    )
    return result.reshape(adjoint.shape)


def solution(mesh):
    fine = Mesh(mesh.devices.reshape(4, 2, 16, 2), ("sys", "xl", "zc", "inst"))
    blk = ("xl", "zc")
    return jax.shard_map(
        shards,
        mesh=fine,
        in_specs=(
            P("sys", "inst", None, blk, None, None),
            P("sys", "inst", None, blk, None, None),
            P("sys", None, None, blk, None, None),
            P("sys", None, blk, None, None),
            P("sys", blk, None, None),
            P("sys", blk, None),
            P("sys", blk, None, None),
            P("sys", blk, None, None),
            P("sys", blk, None, None),
            P("sys", blk, None),
        ),
        out_specs=P("sys", "inst", None, blk, None, None),
        check_vma=False,
    )
```

```python
import math

import jax
import jax.numpy as jnp
from jax import lax
from jax.experimental import pallas as pl
from jax.experimental.pallas import tpu as pltpu
from jax.sharding import Mesh, PartitionSpec as P

ROTOR_RATE = 0.6
F32 = jnp.float32
BF16 = jnp.bfloat16

FIELDS = 5
INSTANCES = 8
LOCAL = 4
CH = LOCAL * FIELDS
HI = 256
LO = 128
ROWS = 1024
CAP = 16
SLOT = 40
NEAR = 64
PIECE = CAP * SLOT // LO
FIRST = 3
ACCS = 8


def spectra_entry(offset):
    offset %= INSTANCES
    if offset == 0:
        return 0.0
    angle = math.pi * offset / INSTANCES
    return 0.5 * (-1.0) ** offset * math.cos(angle) / math.sin(angle)


def iota(shape, dim):
    return lax.broadcasted_iota(jnp.int32, shape, dim)


def split(x):
    head = x.astype(BF16)
    return head, (x - head.astype(F32)).astype(BF16)


def takes(microseconds):
    return pl.CostEstimate(flops=0, bytes_accessed=microseconds * 3_700_000, transcendentals=0)


def nt_dot(a, b):
    return lax.dot_general(a, b, (((1,), (1,)), ((), ())), preferred_element_type=F32)


def pick_kernel(counts, *refs):
    (cells, *small), (payload, top, bottom) = refs[:5], refs[5:8]
    adj, cell, owner, donor, weight, sem, small_sem = refs[8:]

    def chunk_copy(i):
        here = pl.ds(i * LOCAL, LOCAL)
        return pltpu.make_async_copy(cells.at[here], adj.at[here], sem.at[i])

    copies = [
        pltpu.make_async_copy(operand, place, small_sem.at[i])
        for i, (operand, place) in enumerate(zip(small, (cell, owner, donor, weight)))
    ]
    for copy in copies:
        copy.start()
    for i in range(FIELDS):
        chunk_copy(i).start()
    for copy in copies:
        copy.wait()
    for i in range(FIELDS):
        chunk_copy(i).wait()
    spot = cell[...]
    high = (spot >> 7) & 127
    low = ((spot >> 14) << 7) | (spot & 127)
    lefts = []
    for channel in range(CH):
        whole = adj[channel]
        head, tail = split(jnp.concatenate([whole[:LO], whole[LO:]], axis=1))
        lefts.append(jnp.concatenate([head, tail], axis=1))
    left = jnp.concatenate(lefts, axis=0)
    wide = 256
    for part in range(ROWS // wide):
        cols = slice(part * wide, (part + 1) * wide)
        lows = jnp.where(iota((2 * LO, wide), 0) == low[:, cols], 1.0, 0.0).astype(BF16)
        lows = jnp.concatenate([lows, lows], axis=0)
        here = iota((LO, wide), 0) == high[:, cols]
        found = jnp.dot(left, lows, preferred_element_type=F32)
        for channel in range(CH):
            payload[channel : channel + 1, cols] = jnp.sum(
                jnp.where(here, found[channel * LO : (channel + 1) * LO], 0.0),
                axis=0,
                keepdims=True,
            )
    for group in range(ROWS // LO):
        lanes = slice(group * LO, (group + 1) * LO)
        living = iota((1, LO), 1) < counts[group]
        payload[CH : CH + 1, lanes] = jnp.where(living, owner[:, lanes], -1).astype(F32)
    payload[CH + 1 : 24, :] = jnp.zeros((23 - CH, ROWS), F32)
    payload[24:32, :] = weight[...]
    payload[32:40, :] = donor[...].astype(F32)
    for channel in range(CH):
        top[channel] = adj[channel, HI - 16 :, :]
        bottom[channel] = adj[channel, :16, :]


def pack_kernel(position, own, got, message):
    upto = jnp.where(iota((LO, LO), 0) <= iota((LO, LO), 1), 1.0, 0.0).astype(BF16)
    ones = jnp.ones((LO, LO), BF16)
    for half, payload in enumerate((own, got)):
        rows = payload[...]
        name = rows[CH : CH + 1].astype(jnp.int32)
        near = ((name >> 4) & 1) == position[0]
        name = jnp.where((name >= 0) & near, ((name >> 5) << 4) | (name & 15), -1)
        before = jnp.zeros((NEAR, LO), F32)
        chosen, ranks = [], []
        for group in range(ROWS // LO):
            lanes = slice(group * LO, (group + 1) * LO)
            hit = jnp.where(iota((NEAR, LO), 0) == name[:, lanes], 1.0, 0.0)
            hit16 = hit.astype(BF16)
            count = jnp.dot(hit16, upto, preferred_element_type=F32) + before
            before = before + jnp.dot(hit16, ones, preferred_element_type=F32)
            ranks.append(jnp.sum(hit * count, axis=0, keepdims=True) - 1.0)
            chosen.append(hit16)
        chosen = jnp.concatenate(chosen, axis=1)
        rank = jnp.concatenate(ranks, axis=1)
        placed = jnp.concatenate(
            [jnp.where(rank == float(slot), rows, 0.0) for slot in range(CAP)], axis=0
        )
        head, tail = split(placed)
        table = nt_dot(head, chosen) + nt_dot(tail, chosen)
        for piece in range(PIECE):
            block = table[piece * LO : (piece + 1) * LO].T
            message[pl.ds(half * PIECE + piece, NEAR, stride=2 * PIECE), :] = block


def local_kernel(adj, below, above, gradient, jacobian, coupling, step, out, edge):
    planes = step.shape[0]
    rows = planes * 16
    index = pl.program_id(0)
    last = pl.num_programs(0) - 1
    y = iota((rows, LO), 0) % 16
    z = iota((rows, LO), 1)
    faces = [coupling[d].reshape(rows, LO) for d in range(6)]
    faces[2] = jnp.where(y == 15, 0.0, faces[2])
    faces[3] = jnp.where(y == 0, 0.0, faces[3])
    faces[4] = jnp.where(z == LO - 1, 0.0, faces[4])
    faces[5] = jnp.where(z == 0, 0.0, faces[5])
    tau = step[...].reshape(rows, LO)

    @pl.when(index == 0)
    def _():
        edge[0] = (tau * faces[1])[:16]

    @pl.when(index == last)
    def _():
        edge[1] = (tau * faces[0])[-16:]

    for field in range(FIELDS):
        blocks = [jacobian[g, field].reshape(rows, LO) for g in range(FIELDS)]
        mine = [
            adj[t * FIELDS + field].reshape(rows, LO) for t in range(LOCAL)
        ]
        for t in range(LOCAL):
            channel = t * FIELDS + field
            own = mine[t]
            total = -gradient[channel].reshape(rows, LO)
            for g in range(FIELDS):
                total = total + blocks[g] * adj[t * FIELDS + g].reshape(rows, LO)
            next_plane = jnp.where(index == last, 0.0, above[channel, 0])
            past_plane = jnp.where(index == 0, 0.0, below[channel, 0])
            total = total - faces[0] * jnp.concatenate([own[16:], next_plane], axis=0)
            total = total - faces[1] * jnp.concatenate([past_plane, own[:-16]], axis=0)
            total = total - faces[2] * pltpu.roll(own, rows - 1, 0)
            total = total - faces[3] * pltpu.roll(own, 1, 0)
            total = total - faces[4] * pltpu.roll(own, LO - 1, 1)
            total = total - faces[5] * pltpu.roll(own, 1, 1)
            for s in range(LOCAL):
                if s != t:
                    total = total + (ROTOR_RATE * spectra_entry(s - t)) * mine[s]
            out[channel] = (own - tau * total).reshape(planes, 16, LO)


def fringe_kernel(rows, partial, step, out, *scratch):
    accs = scratch[:ACCS]
    flat, expand, order, places, indices, products, held, sem, held_sem = scratch[ACCS:]
    fetch = pltpu.make_async_copy(partial, held, held_sem)
    fetch.start()
    for piece in range(PIECE):
        flat[pl.ds(piece * LO, LO), :] = rows[pl.ds(piece, LO, stride=PIECE), :].T

    weights = jnp.concatenate(
        [flat[slot * SLOT + 24 : slot * SLOT + 32, :] for slot in range(CAP)], axis=0
    )
    alive = jnp.where(weights > 0.0, 1.0, 0.0)
    upto = jnp.where(iota((LO, LO), 0) <= iota((LO, LO), 1), 1.0, 0.0).astype(BF16)
    rank = jnp.dot(alive.astype(BF16), upto, preferred_element_type=F32) * alive - 1.0
    order[...] = rank.astype(jnp.int32)
    places[LO : LO + 8, :] = nt_dot(jnp.ones((8, LO), BF16), alive.astype(BF16)).astype(jnp.int32)

    def move_of(slot):
        target = order[pl.ds(pl.multiple_of(slot * 8, 8), 1), :]
        return jnp.where(iota((LO, LO), 0) == target, 1.0, 0.0).astype(BF16)

    @pl.loop(0, CAP // 4)
    def _(four):
        for i in range(4):
            slot = four * 4 + i
            spot = flat[pl.ds(pl.multiple_of(slot * SLOT, 8) + 32, 8), :]
            head = spot.astype(BF16).astype(F32)
            both = jnp.concatenate([head, spot - head], axis=0).astype(BF16)
            both = nt_dot(both, move_of(slot))
            spot = (both[:8] + both[8:]).astype(jnp.int32)
            places[pl.ds(pl.multiple_of(slot * 8, 8), 8), :] = ((spot >> 9) << 7) | (spot & 127)

    copy = pltpu.make_async_copy(places, indices, sem)
    copy.start()

    row = iota((LO, LO), 0)
    lane = iota((LO, LO), 1)
    value_row = jnp.where(row < 24, row, row - 24)
    hit = (row < 48) & (value_row == lane // 4)
    expand[:, 0:LO] = jnp.where(hit, 1.0, 0.0).astype(BF16)
    weight_row = jnp.where(row < 80, row - 48, row - 80)
    for k in range(8):
        hit = (row >= 48) & (row < 112) & (weight_row == (lane % 4) * 8 + k)
        expand[:, (k + 1) * LO : (k + 2) * LO] = jnp.where(hit, 1.0, 0.0).astype(BF16)

    @pl.loop(0, CAP // 4)
    def _(four):
        for i in range(4):
            slot = four * 4 + i
            base = pl.multiple_of(slot * SLOT, 8)
            values = flat[pl.ds(base, 24), :]
            weights = flat[pl.ds(base + 24, 8), :]
            quarter = (flat[pl.ds(base + 32, 8), :].astype(jnp.int32) >> 7) & 3
            weights = jnp.concatenate(
                [jnp.where(quarter == q, weights, 0.0) for q in range(4)], axis=0
            )
            values_head = values.astype(BF16).astype(F32)
            weights_head = weights.astype(BF16).astype(F32)
            left = jnp.concatenate(
                [
                    values_head,
                    values - values_head,
                    weights_head,
                    weights - weights_head,
                    jnp.zeros((16, LO), F32),
                ],
                axis=0,
            )
            turned = nt_dot(move_of(slot), left.astype(BF16)).astype(BF16)
            both = jnp.dot(turned, expand[...], preferred_element_type=F32)
            here = pl.ds(pl.multiple_of(slot * LO, LO), LO)
            for k in range(8):
                products[k, here, :] = both[:, 0:LO] * both[:, (k + 1) * LO : (k + 2) * LO]

    zeros = jnp.zeros((64, LO), F32)

    @pl.loop(0, 8192 // 64)
    def _(i):
        for acc in accs:
            acc[pl.ds(pl.multiple_of(i * 64, 64), 64), :] = zeros

    copy.wait()
    listed = indices.reshape((LO + 8) * LO)

    @pl.loop(0, CAP)
    def _(slot):
        unroll = 8

        @pl.loop(0, (listed[LO * LO + slot * 8] + (unroll - 1)) // unroll)
        def _(chunk):
            for u in range(unroll):
                source = chunk * unroll + u
                for k in range(8):
                    acc = accs[k % ACCS]
                    place = listed[slot * 8 * LO + chunk * unroll + (k * LO + u)]
                    acc[pl.ds(place, 1), :] = (
                        acc[pl.ds(place, 1), :] + products[k, pl.ds(slot * LO + source, 1), :]
                    )

    fetch.wait()

    @pl.loop(0, HI // 8, unroll=4)
    def _(i):
        turned = []
        for half in range(2):
            begin = pl.multiple_of(i * 256 + half * LO, LO)
            total = accs[0][pl.ds(begin, LO), :]
            for acc in accs[1:]:
                total = total + acc[pl.ds(begin, LO), :]
            turned.append(total.T)
        here = pl.ds(pl.multiple_of(i * 8, 8), 8)
        tau = step[here, :]
        for channel in range(CH):
            cells = slice(channel * 4, channel * 4 + 4)
            gained = jnp.concatenate([turned[0][cells], turned[1][cells]], axis=0)
            out[channel, here, :] = held[channel, here, :] - tau * gained


def final_kernel(partial, first, rest, step, before, after, edge, out, ready, sem):
    steps = 8
    wide = HI // steps

    def copy_of(i):
        here = pl.ds(pl.multiple_of(i * wide, wide), wide)
        return pltpu.make_async_copy(ready.at[:, here, :], out.at[:, here, :], sem.at[i])

    def block(i):
        here = pl.ds(pl.multiple_of(i * wide, wide), wide)
        tau = step[here, :]
        for field in range(FIELDS):
            channels = [s * FIELDS + field for s in range(LOCAL)]
            others = [
                first[c, here, :] if c < FIRST else rest[c - FIRST, here, :] for c in channels
            ]
            for t in range(LOCAL):
                total = None
                for s in range(LOCAL):
                    if s == t:
                        continue
                    term = (ROTOR_RATE * spectra_entry(s - t + LOCAL)) * others[s]
                    total = term if total is None else total + term
                channel = channels[t]
                ready[channel, here, :] = partial[channel, here, :] - tau * total

    @pl.loop(0, steps, unroll=2)
    def _(i):
        block(i)

        @pl.when(i == 0)
        def _():
            for channel in range(CH):
                ready[channel, :16, :] += edge[0] * before[channel]

        @pl.when(i == steps - 1)
        def _():
            for channel in range(CH):
                ready[channel, HI - 16 :, :] += edge[1] * after[channel]

        copy_of(i).start()

    for i in range(steps):
        copy_of(i).wait()


def shards(
    adjoint,
    gradient,
    jacobian,
    coupling,
    pseudo_step,
    receptor_cell,
    donor_owner,
    donor_cell,
    donor_weight,
    block_count,
):
    swap = [(0, 1), (1, 0)]
    blocks = lax.axis_size("xl") * lax.axis_size("zc")
    cells = adjoint.reshape(CH, HI, LO)
    planes = adjoint.reshape(CH, 16, 16, LO)
    vmem = pl.BlockSpec(memory_space=pltpu.VMEM)
    smem = pl.BlockSpec(memory_space=pltpu.SMEM)
    hbm = pl.BlockSpec(memory_space=pltpu.HBM)

    first = lax.ppermute(cells[:FIRST], "inst", swap)
    payload, top, bottom = pl.pallas_call(
        pick_kernel,
        out_shape=[
            jax.ShapeDtypeStruct((SLOT, ROWS), F32),
            jax.ShapeDtypeStruct((CH, 16, LO), F32),
            jax.ShapeDtypeStruct((CH, 16, LO), F32),
        ],
        in_specs=[smem] + [hbm] * 5,
        out_specs=[vmem] * 3,
        scratch_shapes=[
            pltpu.VMEM((CH, HI, LO), F32),
            pltpu.VMEM((1, ROWS), jnp.int32),
            pltpu.VMEM((1, ROWS), jnp.int32),
            pltpu.VMEM((8, ROWS), jnp.int32),
            pltpu.VMEM((8, ROWS), F32),
            pltpu.SemaphoreType.DMA((FIELDS,)),
            pltpu.SemaphoreType.DMA((4,)),
        ],
        compiler_params=pltpu.CompilerParams(vmem_limit_bytes=56 * 2**20),
        cost_estimate=takes(5),
        name="pick",
    )(
        block_count.reshape(8),
        cells,
        receptor_cell.reshape(1, ROWS),
        donor_owner.reshape(1, ROWS),
        donor_cell.reshape(8, ROWS),
        donor_weight.reshape(8, ROWS),
    )
    got = lax.ppermute(payload, "xl", swap)
    rest, got, first = lax.optimization_barrier((cells[FIRST:], got, first))
    rest = lax.ppermute(rest, "inst", swap)

    message = pl.pallas_call(
        pack_kernel,
        out_shape=jax.ShapeDtypeStruct((NEAR * 2 * PIECE, LO), F32),
        in_specs=[smem, vmem, vmem],
        out_specs=vmem,
        compiler_params=pltpu.CompilerParams(vmem_limit_bytes=32 * 2**20),
        cost_estimate=takes(3),
        name="pack",
    )(lax.axis_index("xl").astype(jnp.int32).reshape(1), payload, got)
    message, gradient, top, bottom = lax.optimization_barrier((message, gradient, top, bottom))
    arrived = lax.all_to_all(
        message.reshape(-1), ("sys", "zc"), split_axis=0, concat_axis=0, tiled=True
    )
    before = lax.ppermute(top, ("xl", "zc"), [(i, i + 1) for i in range(blocks - 1)])
    after = lax.ppermute(bottom, ("xl", "zc"), [(i + 1, i) for i in range(blocks - 1)])

    steps = 2
    wide = 16 // steps
    partial, edge = pl.pallas_call(
        local_kernel,
        grid=(steps,),
        out_shape=[
            jax.ShapeDtypeStruct((CH, 16, 16, LO), F32),
            jax.ShapeDtypeStruct((2, 16, LO), F32),
        ],
        in_specs=[
            pl.BlockSpec((CH, wide, 16, LO), lambda i: (0, i, 0, 0)),
            pl.BlockSpec((CH, 1, 16, LO), lambda i: (0, jnp.maximum(wide * i - 1, 0), 0, 0)),
            pl.BlockSpec((CH, 1, 16, LO), lambda i: (0, jnp.minimum(wide * i + wide, 15), 0, 0)),
            pl.BlockSpec((CH, wide, 16, LO), lambda i: (0, i, 0, 0)),
            pl.BlockSpec((FIELDS, FIELDS, wide, 16, LO), lambda i: (0, 0, i, 0, 0)),
            pl.BlockSpec((6, wide, 16, LO), lambda i: (0, i, 0, 0)),
            pl.BlockSpec((wide, 16, LO), lambda i: (i, 0, 0)),
        ],
        out_specs=[
            pl.BlockSpec((CH, wide, 16, LO), lambda i: (0, i, 0, 0)),
            pl.BlockSpec((2, 16, LO), lambda i: (0, 0, 0)),
        ],
        compiler_params=pltpu.CompilerParams(vmem_limit_bytes=56 * 2**20),
        cost_estimate=takes(6),
        name="local",
    )(
        planes,
        planes,
        planes,
        gradient.reshape(CH, 16, 16, LO),
        jacobian.reshape(FIELDS, FIELDS, 16, 16, LO),
        coupling.reshape(6, 16, 16, LO),
        pseudo_step.reshape(16, 16, LO),
    )

    arrived, partial = lax.optimization_barrier((arrived, partial))
    tau = pseudo_step.reshape(HI, LO)
    partial = pl.pallas_call(
        fringe_kernel,
        out_shape=jax.ShapeDtypeStruct((CH, HI, LO), F32),
        in_specs=[vmem, hbm, vmem],
        out_specs=vmem,
        scratch_shapes=[pltpu.VMEM((8192, LO), F32)] * ACCS
        + [
            pltpu.VMEM((CAP * SLOT, LO), F32),
            pltpu.VMEM((LO, 9 * LO), BF16),
            pltpu.VMEM((LO, LO), jnp.int32),
            pltpu.VMEM((LO + 8, LO), jnp.int32),
            pltpu.SMEM((LO + 8, LO), jnp.int32),
            pltpu.VMEM((8, CAP * LO, LO), F32),
            pltpu.VMEM((CH, HI, LO), F32),
            pltpu.SemaphoreType.DMA,
            pltpu.SemaphoreType.DMA,
        ],
        compiler_params=pltpu.CompilerParams(vmem_limit_bytes=50 * 2**20),
        cost_estimate=takes(25),
        name="fringe",
    )(arrived.reshape(128 * PIECE, LO), partial.reshape(CH, HI, LO), tau)

    result = pl.pallas_call(
        final_kernel,
        out_shape=jax.ShapeDtypeStruct((CH, HI, LO), F32),
        in_specs=[vmem] * 7,
        out_specs=pl.BlockSpec(memory_space=pl.ANY),
        scratch_shapes=[pltpu.VMEM((CH, HI, LO), F32), pltpu.SemaphoreType.DMA((8,))],
        compiler_params=pltpu.CompilerParams(vmem_limit_bytes=40 * 2**20),
        cost_estimate=takes(2),
        name="final",
    )(partial, first, rest, tau, before, after, edge)
    return result.reshape(adjoint.shape)


def solution(mesh):
    fine = Mesh(mesh.devices.reshape(4, 2, 16, 2), ("sys", "xl", "zc", "inst"))
    blk = ("xl", "zc")
    return jax.shard_map(
        shards,
        mesh=fine,
        in_specs=(
            P("sys", "inst", None, blk, None, None),
            P("sys", "inst", None, blk, None, None),
            P("sys", None, None, blk, None, None),
            P("sys", None, blk, None, None),
            P("sys", blk, None, None),
            P("sys", blk, None),
            P("sys", blk, None, None),
            P("sys", blk, None, None),
            P("sys", blk, None, None),
            P("sys", blk, None),
        ),
        out_specs=P("sys", "inst", None, blk, None, None),
        check_vma=False,
    )
```

```python
import math

import jax
import jax.numpy as jnp
from jax import lax
from jax.experimental import pallas as pl
from jax.experimental.pallas import tpu as pltpu
from jax.sharding import Mesh, PartitionSpec as P

ROTOR_RATE = 0.6
F32 = jnp.float32
BF16 = jnp.bfloat16

FIELDS = 5
INSTANCES = 8
LOCAL = 4
CH = LOCAL * FIELDS
HI = 256
LO = 128
ROWS = 1024
CAP = 16
SLOT = 40
NEAR = 64
PIECE = CAP * SLOT // LO
FIRST = 3
ACCS = 8
SPARE = 16


def spectra_entry(offset):
    offset %= INSTANCES
    if offset == 0:
        return 0.0
    angle = math.pi * offset / INSTANCES
    return 0.5 * (-1.0) ** offset * math.cos(angle) / math.sin(angle)


def iota(shape, dim):
    return lax.broadcasted_iota(jnp.int32, shape, dim)


def split(x):
    head = x.astype(BF16)
    return head, (x - head.astype(F32)).astype(BF16)


def takes(microseconds):
    return pl.CostEstimate(flops=0, bytes_accessed=microseconds * 3_700_000, transcendentals=0)


def nt_dot(a, b):
    return lax.dot_general(a, b, (((1,), (1,)), ((), ())), preferred_element_type=F32)


def pick_kernel(counts, *refs):
    (cells, *small), (payload, top, bottom) = refs[:5], refs[5:8]
    adj, cell, owner, donor, weight, sem, small_sem = refs[8:]

    def chunk_copy(i):
        here = pl.ds(i * LOCAL, LOCAL)
        return pltpu.make_async_copy(cells.at[here], adj.at[here], sem.at[i])

    copies = [
        pltpu.make_async_copy(operand, place, small_sem.at[i])
        for i, (operand, place) in enumerate(zip(small, (cell, owner, donor, weight)))
    ]
    for copy in copies:
        copy.start()
    for i in range(FIELDS):
        chunk_copy(i).start()
    for copy in copies:
        copy.wait()
    for i in range(FIELDS):
        chunk_copy(i).wait()
    spot = cell[...]
    high = (spot >> 7) & 127
    low = ((spot >> 14) << 7) | (spot & 127)
    lefts = []
    for channel in range(CH):
        whole = adj[channel]
        head, tail = split(jnp.concatenate([whole[:LO], whole[LO:]], axis=1))
        lefts.append(jnp.concatenate([head, tail], axis=1))
    left = jnp.concatenate(lefts, axis=0)
    wide = 256
    for part in range(ROWS // wide):
        cols = slice(part * wide, (part + 1) * wide)
        lows = jnp.where(iota((2 * LO, wide), 0) == low[:, cols], 1.0, 0.0).astype(BF16)
        lows = jnp.concatenate([lows, lows], axis=0)
        here = iota((LO, wide), 0) == high[:, cols]
        found = jnp.dot(left, lows, preferred_element_type=F32)
        for channel in range(CH):
            payload[channel : channel + 1, cols] = jnp.sum(
                jnp.where(here, found[channel * LO : (channel + 1) * LO], 0.0),
                axis=0,
                keepdims=True,
            )
    for group in range(ROWS // LO):
        lanes = slice(group * LO, (group + 1) * LO)
        living = iota((1, LO), 1) < counts[group]
        payload[CH : CH + 1, lanes] = jnp.where(living, owner[:, lanes], -1).astype(F32)
    payload[CH + 1 : 24, :] = jnp.zeros((23 - CH, ROWS), F32)
    payload[24:32, :] = weight[...]
    payload[32:40, :] = donor[...].astype(F32)
    for channel in range(CH):
        top[channel] = adj[channel, HI - 16 :, :]
        bottom[channel] = adj[channel, :16, :]


def pack_kernel(position, own, got, message, spread):
    upto = jnp.where(iota((LO, LO), 0) <= iota((LO, LO), 1), 1.0, 0.0).astype(BF16)
    ones = jnp.ones((LO, LO), BF16)
    for half, payload in enumerate((own, got)):
        rows = payload[...]
        name = rows[CH : CH + 1].astype(jnp.int32)
        near = ((name >> 4) & 1) == position[0]
        name = jnp.where((name >= 0) & near, ((name >> 5) << 4) | (name & 15), -1)
        before = jnp.zeros((NEAR, LO), F32)
        chosen, ranks = [], []
        for group in range(ROWS // LO):
            lanes = slice(group * LO, (group + 1) * LO)
            hit = jnp.where(iota((NEAR, LO), 0) == name[:, lanes], 1.0, 0.0)
            hit16 = hit.astype(BF16)
            count = jnp.dot(hit16, upto, preferred_element_type=F32) + before
            before = before + jnp.dot(hit16, ones, preferred_element_type=F32)
            ranks.append(jnp.sum(hit * count, axis=0, keepdims=True) - 1.0)
            chosen.append(hit16)
        chosen = jnp.concatenate(chosen, axis=1)
        rank = jnp.concatenate(ranks, axis=1)
        placed = jnp.concatenate(
            [jnp.where(rank == float(slot), rows, 0.0) for slot in range(CAP)], axis=0
        )
        head, tail = split(placed)
        table = nt_dot(head, chosen) + nt_dot(tail, chosen)
        for piece in range(PIECE):
            block = table[piece * LO : (piece + 1) * LO].T
            spread[pl.ds(half * PIECE + piece, NEAR, stride=2 * PIECE), :] = block
    message[...] = spread[: NEAR * 2 * PIECE, :]


def local_kernel(adj, below, above, gradient, jacobian, coupling, step, out, edge):
    planes = step.shape[0]
    rows = planes * 16
    index = pl.program_id(0)
    last = pl.num_programs(0) - 1
    y = iota((rows, LO), 0) % 16
    z = iota((rows, LO), 1)
    faces = [coupling[d].reshape(rows, LO) for d in range(6)]
    faces[2] = jnp.where(y == 15, 0.0, faces[2])
    faces[3] = jnp.where(y == 0, 0.0, faces[3])
    faces[4] = jnp.where(z == LO - 1, 0.0, faces[4])
    faces[5] = jnp.where(z == 0, 0.0, faces[5])
    tau = step[...].reshape(rows, LO)

    @pl.when(index == 0)
    def _():
        edge[0] = (tau * faces[1])[:16]

    @pl.when(index == last)
    def _():
        edge[1] = (tau * faces[0])[-16:]

    for field in range(FIELDS):
        blocks = [jacobian[g, field].reshape(rows, LO) for g in range(FIELDS)]
        mine = [
            adj[t * FIELDS + field].reshape(rows, LO) for t in range(LOCAL)
        ]
        for t in range(LOCAL):
            channel = t * FIELDS + field
            own = mine[t]
            total = -gradient[channel].reshape(rows, LO)
            for g in range(FIELDS):
                total = total + blocks[g] * adj[t * FIELDS + g].reshape(rows, LO)
            next_plane = jnp.where(index == last, 0.0, above[channel, 0])
            past_plane = jnp.where(index == 0, 0.0, below[channel, 0])
            total = total - faces[0] * jnp.concatenate([own[16:], next_plane], axis=0)
            total = total - faces[1] * jnp.concatenate([past_plane, own[:-16]], axis=0)
            total = total - faces[2] * pltpu.roll(own, rows - 1, 0)
            total = total - faces[3] * pltpu.roll(own, 1, 0)
            total = total - faces[4] * pltpu.roll(own, LO - 1, 1)
            total = total - faces[5] * pltpu.roll(own, 1, 1)
            for s in range(LOCAL):
                if s != t:
                    total = total + (ROTOR_RATE * spectra_entry(s - t)) * mine[s]
            out[channel] = (own - tau * total).reshape(planes, 16, LO)


def fringe_kernel(rows, partial, step, out, *scratch):
    accs = scratch[:ACCS]
    spread, flat, expand, order, places, indices, products, held, sem, held_sem = scratch[ACCS:]
    fetch = pltpu.make_async_copy(partial, held, held_sem)
    fetch.start()
    spread[: LO * PIECE, :] = rows[...]
    for piece in range(PIECE):
        flat[pl.ds(piece * LO, LO), :] = spread[pl.ds(piece, LO, stride=PIECE), :].T

    weights = jnp.concatenate(
        [flat[slot * SLOT + 24 : slot * SLOT + 32, :] for slot in range(CAP)], axis=0
    )
    alive = jnp.where(weights > 0.0, 1.0, 0.0)
    upto = jnp.where(iota((LO, LO), 0) <= iota((LO, LO), 1), 1.0, 0.0).astype(BF16)
    rank = jnp.dot(alive.astype(BF16), upto, preferred_element_type=F32) * alive - 1.0
    order[...] = rank.astype(jnp.int32)
    places[LO : LO + 8, :] = nt_dot(jnp.ones((8, LO), BF16), alive.astype(BF16)).astype(jnp.int32)

    def move_of(slot):
        target = order[pl.ds(pl.multiple_of(slot * 8, 8), 1), :]
        return jnp.where(iota((LO, LO), 0) == target, 1.0, 0.0).astype(BF16)

    @pl.loop(0, CAP // 4)
    def _(four):
        for i in range(4):
            slot = four * 4 + i
            spot = flat[pl.ds(pl.multiple_of(slot * SLOT, 8) + 32, 8), :]
            head = spot.astype(BF16).astype(F32)
            both = jnp.concatenate([head, spot - head], axis=0).astype(BF16)
            both = nt_dot(both, move_of(slot))
            spot = (both[:8] + both[8:]).astype(jnp.int32)
            places[pl.ds(pl.multiple_of(slot * 8, 8), 8), :] = ((spot >> 9) << 7) | (spot & 127)

    copy = pltpu.make_async_copy(places, indices, sem)
    copy.start()

    row = iota((LO, LO), 0)
    lane = iota((LO, LO), 1)
    value_row = jnp.where(row < 24, row, row - 24)
    hit = (row < 48) & (value_row == lane // 4)
    expand[:, 0:LO] = jnp.where(hit, 1.0, 0.0).astype(BF16)
    weight_row = jnp.where(row < 80, row - 48, row - 80)
    for k in range(8):
        hit = (row >= 48) & (row < 112) & (weight_row == (lane % 4) * 8 + k)
        expand[:, (k + 1) * LO : (k + 2) * LO] = jnp.where(hit, 1.0, 0.0).astype(BF16)

    @pl.loop(0, CAP // 4)
    def _(four):
        for i in range(4):
            slot = four * 4 + i
            base = pl.multiple_of(slot * SLOT, 8)
            values = flat[pl.ds(base, 24), :]
            weights = flat[pl.ds(base + 24, 8), :]
            quarter = (flat[pl.ds(base + 32, 8), :].astype(jnp.int32) >> 7) & 3
            weights = jnp.concatenate(
                [jnp.where(quarter == q, weights, 0.0) for q in range(4)], axis=0
            )
            values_head = values.astype(BF16).astype(F32)
            weights_head = weights.astype(BF16).astype(F32)
            left = jnp.concatenate(
                [
                    values_head,
                    values - values_head,
                    weights_head,
                    weights - weights_head,
                    jnp.zeros((16, LO), F32),
                ],
                axis=0,
            )
            turned = nt_dot(move_of(slot), left.astype(BF16)).astype(BF16)
            both = jnp.dot(turned, expand[...], preferred_element_type=F32)
            here = pl.ds(pl.multiple_of(slot * LO, LO), LO)
            for k in range(8):
                products[k, here, :] = both[:, 0:LO] * both[:, (k + 1) * LO : (k + 2) * LO]

    zeros = jnp.zeros((64, LO), F32)

    @pl.loop(0, 8192 // 64)
    def _(i):
        for acc in accs:
            acc[pl.ds(pl.multiple_of(i * 64, 64), 64), :] = zeros

    copy.wait()
    listed = indices.reshape((LO + 8) * LO)

    @pl.loop(0, CAP)
    def _(slot):
        unroll = 8

        @pl.loop(0, (listed[LO * LO + slot * 8] + (unroll - 1)) // unroll)
        def _(chunk):
            for u in range(unroll):
                source = chunk * unroll + u
                for k in range(8):
                    acc = accs[k % ACCS]
                    place = listed[slot * 8 * LO + chunk * unroll + (k * LO + u)]
                    acc[pl.ds(place, 1), :] = (
                        acc[pl.ds(place, 1), :] + products[k, pl.ds(slot * LO + source, 1), :]
                    )

    fetch.wait()

    @pl.loop(0, HI // 8, unroll=4)
    def _(i):
        turned = []
        for half in range(2):
            begin = pl.multiple_of(i * 256 + half * LO, LO)
            total = accs[0][pl.ds(begin, LO), :]
            for acc in accs[1:]:
                total = total + acc[pl.ds(begin, LO), :]
            turned.append(total.T)
        here = pl.ds(pl.multiple_of(i * 8, 8), 8)
        tau = step[here, :]
        for channel in range(CH):
            cells = slice(channel * 4, channel * 4 + 4)
            gained = jnp.concatenate([turned[0][cells], turned[1][cells]], axis=0)
            out[channel, here, :] = held[channel, here, :] - tau * gained


def final_kernel(partial, first, rest, step, before, after, edge, out, ready, sem):
    steps = 8
    wide = HI // steps

    def copy_of(i):
        here = pl.ds(pl.multiple_of(i * wide, wide), wide)
        return pltpu.make_async_copy(ready.at[:, here, :], out.at[:, here, :], sem.at[i])

    def block(i):
        here = pl.ds(pl.multiple_of(i * wide, wide), wide)
        tau = step[here, :]
        for field in range(FIELDS):
            channels = [s * FIELDS + field for s in range(LOCAL)]
            others = [
                first[c, here, :] if c < FIRST else rest[c - FIRST, here, :] for c in channels
            ]
            for t in range(LOCAL):
                total = None
                for s in range(LOCAL):
                    if s == t:
                        continue
                    term = (ROTOR_RATE * spectra_entry(s - t + LOCAL)) * others[s]
                    total = term if total is None else total + term
                channel = channels[t]
                ready[channel, here, :] = partial[channel, here, :] - tau * total

    @pl.loop(0, steps)
    def _(i):
        block(i)

        @pl.when(i == 0)
        def _():
            for channel in range(CH):
                ready[channel, :16, :] += edge[0] * before[channel]

        @pl.when(i == steps - 1)
        def _():
            for channel in range(CH):
                ready[channel, HI - 16 :, :] += edge[1] * after[channel]

        copy_of(i).start()

    for i in range(steps):
        copy_of(i).wait()


def shards(
    adjoint,
    gradient,
    jacobian,
    coupling,
    pseudo_step,
    receptor_cell,
    donor_owner,
    donor_cell,
    donor_weight,
    block_count,
):
    swap = [(0, 1), (1, 0)]
    blocks = lax.axis_size("xl") * lax.axis_size("zc")
    cells = adjoint.reshape(CH, HI, LO)
    planes = adjoint.reshape(CH, 16, 16, LO)
    vmem = pl.BlockSpec(memory_space=pltpu.VMEM)
    smem = pl.BlockSpec(memory_space=pltpu.SMEM)
    hbm = pl.BlockSpec(memory_space=pltpu.HBM)

    first = lax.ppermute(cells[:FIRST], "inst", swap)
    payload, top, bottom = pl.pallas_call(
        pick_kernel,
        out_shape=[
            jax.ShapeDtypeStruct((SLOT, ROWS), F32),
            jax.ShapeDtypeStruct((CH, 16, LO), F32),
            jax.ShapeDtypeStruct((CH, 16, LO), F32),
        ],
        in_specs=[smem] + [hbm] * 5,
        out_specs=[vmem] * 3,
        scratch_shapes=[
            pltpu.VMEM((CH, HI, LO), F32),
            pltpu.VMEM((1, ROWS), jnp.int32),
            pltpu.VMEM((1, ROWS), jnp.int32),
            pltpu.VMEM((8, ROWS), jnp.int32),
            pltpu.VMEM((8, ROWS), F32),
            pltpu.SemaphoreType.DMA((FIELDS,)),
            pltpu.SemaphoreType.DMA((4,)),
        ],
        compiler_params=pltpu.CompilerParams(vmem_limit_bytes=56 * 2**20),
        cost_estimate=takes(5),
        name="pick",
    )(
        block_count.reshape(8),
        cells,
        receptor_cell.reshape(1, ROWS),
        donor_owner.reshape(1, ROWS),
        donor_cell.reshape(8, ROWS),
        donor_weight.reshape(8, ROWS),
    )
    got = lax.ppermute(payload, "xl", swap)
    rest, got, first = lax.optimization_barrier((cells[FIRST:], got, first))
    rest = lax.ppermute(rest, "inst", swap)

    message = pl.pallas_call(
        pack_kernel,
        out_shape=jax.ShapeDtypeStruct((NEAR * 2 * PIECE, LO), F32),
        in_specs=[smem, vmem, vmem],
        out_specs=vmem,
        scratch_shapes=[pltpu.VMEM((NEAR * 2 * PIECE + SPARE, LO), F32)],
        compiler_params=pltpu.CompilerParams(vmem_limit_bytes=32 * 2**20),
        cost_estimate=takes(3),
        name="pack",
    )(lax.axis_index("xl").astype(jnp.int32).reshape(1), payload, got)
    message, gradient, top, bottom = lax.optimization_barrier((message, gradient, top, bottom))
    arrived = lax.all_to_all(
        message.reshape(-1), ("sys", "zc"), split_axis=0, concat_axis=0, tiled=True
    )
    before = lax.ppermute(top, ("xl", "zc"), [(i, i + 1) for i in range(blocks - 1)])
    after = lax.ppermute(bottom, ("xl", "zc"), [(i + 1, i) for i in range(blocks - 1)])

    steps = 4
    wide = 16 // steps
    partial, edge = pl.pallas_call(
        local_kernel,
        grid=(steps,),
        out_shape=[
            jax.ShapeDtypeStruct((CH, 16, 16, LO), F32),
            jax.ShapeDtypeStruct((2, 16, LO), F32),
        ],
        in_specs=[
            pl.BlockSpec((CH, wide, 16, LO), lambda i: (0, i, 0, 0)),
            pl.BlockSpec((CH, 1, 16, LO), lambda i: (0, jnp.maximum(wide * i - 1, 0), 0, 0)),
            pl.BlockSpec((CH, 1, 16, LO), lambda i: (0, jnp.minimum(wide * i + wide, 15), 0, 0)),
            pl.BlockSpec((CH, wide, 16, LO), lambda i: (0, i, 0, 0)),
            pl.BlockSpec((FIELDS, FIELDS, wide, 16, LO), lambda i: (0, 0, i, 0, 0)),
            pl.BlockSpec((6, wide, 16, LO), lambda i: (0, i, 0, 0)),
            pl.BlockSpec((wide, 16, LO), lambda i: (i, 0, 0)),
        ],
        out_specs=[
            pl.BlockSpec((CH, wide, 16, LO), lambda i: (0, i, 0, 0)),
            pl.BlockSpec((2, 16, LO), lambda i: (0, 0, 0)),
        ],
        compiler_params=pltpu.CompilerParams(vmem_limit_bytes=56 * 2**20),
        cost_estimate=takes(6),
        name="local",
    )(
        planes,
        planes,
        planes,
        gradient.reshape(CH, 16, 16, LO),
        jacobian.reshape(FIELDS, FIELDS, 16, 16, LO),
        coupling.reshape(6, 16, 16, LO),
        pseudo_step.reshape(16, 16, LO),
    )

    arrived, partial = lax.optimization_barrier((arrived, partial))
    tau = pseudo_step.reshape(HI, LO)
    partial = pl.pallas_call(
        fringe_kernel,
        out_shape=jax.ShapeDtypeStruct((CH, HI, LO), F32),
        in_specs=[vmem, hbm, vmem],
        out_specs=vmem,
        scratch_shapes=[pltpu.VMEM((8192 + SPARE, LO), F32)] * ACCS
        + [
            pltpu.VMEM((LO * PIECE + SPARE, LO), F32),
            pltpu.VMEM((CAP * SLOT, LO), F32),
            pltpu.VMEM((LO, 9 * LO), BF16),
            pltpu.VMEM((LO, LO), jnp.int32),
            pltpu.VMEM((LO + 8, LO), jnp.int32),
            pltpu.SMEM((LO + 8, LO), jnp.int32),
            pltpu.VMEM((8, CAP * LO + SPARE, LO), F32),
            pltpu.VMEM((CH, HI, LO), F32),
            pltpu.SemaphoreType.DMA,
            pltpu.SemaphoreType.DMA,
        ],
        compiler_params=pltpu.CompilerParams(vmem_limit_bytes=50 * 2**20),
        cost_estimate=takes(25),
        name="fringe",
    )(arrived.reshape(128 * PIECE, LO), partial.reshape(CH, HI, LO), tau)

    result = pl.pallas_call(
        final_kernel,
        out_shape=jax.ShapeDtypeStruct((CH, HI, LO), F32),
        in_specs=[vmem] * 7,
        out_specs=pl.BlockSpec(memory_space=pl.ANY),
        scratch_shapes=[pltpu.VMEM((CH, HI, LO), F32), pltpu.SemaphoreType.DMA((8,))],
        compiler_params=pltpu.CompilerParams(vmem_limit_bytes=40 * 2**20),
        cost_estimate=takes(2),
        name="final",
    )(partial, first, rest, tau, before, after, edge)
    return result.reshape(adjoint.shape)


def solution(mesh):
    fine = Mesh(mesh.devices.reshape(4, 2, 16, 2), ("sys", "xl", "zc", "inst"))
    blk = ("xl", "zc")
    return jax.shard_map(
        shards,
        mesh=fine,
        in_specs=(
            P("sys", "inst", None, blk, None, None),
            P("sys", "inst", None, blk, None, None),
            P("sys", None, None, blk, None, None),
            P("sys", None, blk, None, None),
            P("sys", blk, None, None),
            P("sys", blk, None),
            P("sys", blk, None, None),
            P("sys", blk, None, None),
            P("sys", blk, None, None),
            P("sys", blk, None),
        ),
        out_specs=P("sys", "inst", None, blk, None, None),
        check_vma=False,
    )
```

```python
import math

import jax
import jax.numpy as jnp
from jax import lax
from jax.experimental import pallas as pl
from jax.experimental.pallas import tpu as pltpu
from jax.sharding import Mesh, PartitionSpec as P

ROTOR_RATE = 0.6
F32 = jnp.float32
BF16 = jnp.bfloat16

FIELDS = 5
INSTANCES = 8
LOCAL = 4
CH = LOCAL * FIELDS
HI = 256
LO = 128
ROWS = 1024
CAP = 16
SLOT = 40
NEAR = 64
PIECE = CAP * SLOT // LO
FIRST = 3
ACCS = 8
SPARE = 16


def spectra_entry(offset):
    offset %= INSTANCES
    if offset == 0:
        return 0.0
    angle = math.pi * offset / INSTANCES
    return 0.5 * (-1.0) ** offset * math.cos(angle) / math.sin(angle)


def iota(shape, dim):
    return lax.broadcasted_iota(jnp.int32, shape, dim)


def split(x):
    head = x.astype(BF16)
    return head, (x - head.astype(F32)).astype(BF16)


def takes(microseconds):
    return pl.CostEstimate(flops=0, bytes_accessed=microseconds * 3_700_000, transcendentals=0)


def nt_dot(a, b):
    return lax.dot_general(a, b, (((1,), (1,)), ((), ())), preferred_element_type=F32)


def pick_kernel(counts, *refs):
    (cells, *small), (payload, top, bottom) = refs[:5], refs[5:8]
    adj, cell, owner, donor, weight, sem, small_sem = refs[8:]

    def chunk_copy(i):
        here = pl.ds(i * LOCAL, LOCAL)
        return pltpu.make_async_copy(cells.at[here], adj.at[here], sem.at[i])

    copies = [
        pltpu.make_async_copy(operand, place, small_sem.at[i])
        for i, (operand, place) in enumerate(zip(small, (cell, owner, donor, weight)))
    ]
    for copy in copies:
        copy.start()
    for i in range(FIELDS):
        chunk_copy(i).start()
    for copy in copies:
        copy.wait()
    for i in range(FIELDS):
        chunk_copy(i).wait()
    spot = cell[...]
    high = (spot >> 7) & 127
    low = ((spot >> 14) << 7) | (spot & 127)
    lefts = []
    for channel in range(CH):
        whole = adj[channel]
        head, tail = split(jnp.concatenate([whole[:LO], whole[LO:]], axis=1))
        lefts.append(jnp.concatenate([head, tail], axis=1))
    left = jnp.concatenate(lefts, axis=0)
    wide = 256
    for part in range(ROWS // wide):
        cols = slice(part * wide, (part + 1) * wide)
        lows = jnp.where(iota((2 * LO, wide), 0) == low[:, cols], 1.0, 0.0).astype(BF16)
        lows = jnp.concatenate([lows, lows], axis=0)
        here = iota((LO, wide), 0) == high[:, cols]
        found = jnp.dot(left, lows, preferred_element_type=F32)
        for channel in range(CH):
            payload[channel : channel + 1, cols] = jnp.sum(
                jnp.where(here, found[channel * LO : (channel + 1) * LO], 0.0),
                axis=0,
                keepdims=True,
            )
    for group in range(ROWS // LO):
        lanes = slice(group * LO, (group + 1) * LO)
        living = iota((1, LO), 1) < counts[group]
        payload[CH : CH + 1, lanes] = jnp.where(living, owner[:, lanes], -1).astype(F32)
    payload[CH + 1 : 24, :] = jnp.zeros((23 - CH, ROWS), F32)
    payload[24:32, :] = weight[...]
    payload[32:40, :] = donor[...].astype(F32)
    for channel in range(CH):
        top[channel] = adj[channel, HI - 16 :, :]
        bottom[channel] = adj[channel, :16, :]


def pack_kernel(position, own, got, message, spread):
    upto = jnp.where(iota((LO, LO), 0) <= iota((LO, LO), 1), 1.0, 0.0).astype(BF16)
    ones = jnp.ones((LO, LO), BF16)
    for half, payload in enumerate((own, got)):
        rows = payload[...]
        name = rows[CH : CH + 1].astype(jnp.int32)
        near = ((name >> 4) & 1) == position[0]
        name = jnp.where((name >= 0) & near, ((name >> 5) << 4) | (name & 15), -1)
        before = jnp.zeros((NEAR, LO), F32)
        chosen, ranks = [], []
        for group in range(ROWS // LO):
            lanes = slice(group * LO, (group + 1) * LO)
            hit = jnp.where(iota((NEAR, LO), 0) == name[:, lanes], 1.0, 0.0)
            hit16 = hit.astype(BF16)
            count = jnp.dot(hit16, upto, preferred_element_type=F32) + before
            before = before + jnp.dot(hit16, ones, preferred_element_type=F32)
            ranks.append(jnp.sum(hit * count, axis=0, keepdims=True) - 1.0)
            chosen.append(hit16)
        chosen = jnp.concatenate(chosen, axis=1)
        rank = jnp.concatenate(ranks, axis=1)
        placed = jnp.concatenate(
            [jnp.where(rank == float(slot), rows, 0.0) for slot in range(CAP)], axis=0
        )
        head, tail = split(placed)
        table = nt_dot(head, chosen) + nt_dot(tail, chosen)
        for piece in range(PIECE):
            block = table[piece * LO : (piece + 1) * LO].T
            spread[pl.ds(half * PIECE + piece, NEAR, stride=2 * PIECE), :] = block
    message[...] = spread[: NEAR * 2 * PIECE, :]


def local_kernel(adj, below, above, gradient, jacobian, coupling, step, out, edge):
    planes = step.shape[0]
    rows = planes * 16
    index = pl.program_id(0)
    last = pl.num_programs(0) - 1
    y = iota((rows, LO), 0) % 16
    z = iota((rows, LO), 1)
    faces = [coupling[d].reshape(rows, LO) for d in range(6)]
    faces[2] = jnp.where(y == 15, 0.0, faces[2])
    faces[3] = jnp.where(y == 0, 0.0, faces[3])
    faces[4] = jnp.where(z == LO - 1, 0.0, faces[4])
    faces[5] = jnp.where(z == 0, 0.0, faces[5])
    tau = step[...].reshape(rows, LO)

    @pl.when(index == 0)
    def _():
        edge[0] = (tau * faces[1])[:16]

    @pl.when(index == last)
    def _():
        edge[1] = (tau * faces[0])[-16:]

    for field in range(FIELDS):
        blocks = [jacobian[g, field].reshape(rows, LO) for g in range(FIELDS)]
        mine = [
            adj[t * FIELDS + field].reshape(rows, LO) for t in range(LOCAL)
        ]
        for t in range(LOCAL):
            channel = t * FIELDS + field
            own = mine[t]
            total = -gradient[channel].reshape(rows, LO)
            for g in range(FIELDS):
                total = total + blocks[g] * adj[t * FIELDS + g].reshape(rows, LO)
            next_plane = jnp.where(index == last, 0.0, above[channel, 0])
            past_plane = jnp.where(index == 0, 0.0, below[channel, 0])
            total = total - faces[0] * jnp.concatenate([own[16:], next_plane], axis=0)
            total = total - faces[1] * jnp.concatenate([past_plane, own[:-16]], axis=0)
            total = total - faces[2] * pltpu.roll(own, rows - 1, 0)
            total = total - faces[3] * pltpu.roll(own, 1, 0)
            total = total - faces[4] * pltpu.roll(own, LO - 1, 1)
            total = total - faces[5] * pltpu.roll(own, 1, 1)
            for s in range(LOCAL):
                if s != t:
                    total = total + (ROTOR_RATE * spectra_entry(s - t)) * mine[s]
            out[channel] = (own - tau * total).reshape(planes, 16, LO)


def fringe_kernel(rows, partial, step, out, *scratch):
    accs = scratch[:ACCS]
    spread, flat, expand, order, places, indices, products, held, sem, held_sem = scratch[ACCS:]
    fetch = pltpu.make_async_copy(partial, held, held_sem)
    fetch.start()
    spread[: LO * PIECE, :] = rows[...]
    for piece in range(PIECE):
        flat[pl.ds(piece * LO, LO), :] = spread[pl.ds(piece, LO, stride=PIECE), :].T

    weights = jnp.concatenate(
        [flat[slot * SLOT + 24 : slot * SLOT + 32, :] for slot in range(CAP)], axis=0
    )
    alive = jnp.where(weights > 0.0, 1.0, 0.0)
    upto = jnp.where(iota((LO, LO), 0) <= iota((LO, LO), 1), 1.0, 0.0).astype(BF16)
    rank = jnp.dot(alive.astype(BF16), upto, preferred_element_type=F32) * alive - 1.0
    order[...] = rank.astype(jnp.int32)
    places[LO : LO + 8, :] = nt_dot(jnp.ones((8, LO), BF16), alive.astype(BF16)).astype(jnp.int32)

    def move_of(slot):
        target = order[pl.ds(pl.multiple_of(slot * 8, 8), 1), :]
        return jnp.where(iota((LO, LO), 0) == target, 1.0, 0.0).astype(BF16)

    @pl.loop(0, CAP // 4)
    def _(four):
        for i in range(4):
            slot = four * 4 + i
            spot = flat[pl.ds(pl.multiple_of(slot * SLOT, 8) + 32, 8), :]
            head = spot.astype(BF16).astype(F32)
            both = jnp.concatenate([head, spot - head], axis=0).astype(BF16)
            both = nt_dot(both, move_of(slot))
            spot = (both[:8] + both[8:]).astype(jnp.int32)
            places[pl.ds(pl.multiple_of(slot * 8, 8), 8), :] = ((spot >> 9) << 7) | (spot & 127)

    copy = pltpu.make_async_copy(places, indices, sem)
    copy.start()

    row = iota((LO, LO), 0)
    lane = iota((LO, LO), 1)
    value_row = jnp.where(row < 24, row, row - 24)
    hit = (row < 48) & (value_row == lane // 4)
    expand[:, 0:LO] = jnp.where(hit, 1.0, 0.0).astype(BF16)
    weight_row = jnp.where(row < 80, row - 48, row - 80)
    for k in range(8):
        hit = (row >= 48) & (row < 112) & (weight_row == (lane % 4) * 8 + k)
        expand[:, (k + 1) * LO : (k + 2) * LO] = jnp.where(hit, 1.0, 0.0).astype(BF16)

    @pl.loop(0, CAP // 4)
    def _(four):
        for i in range(4):
            slot = four * 4 + i
            base = pl.multiple_of(slot * SLOT, 8)
            values = flat[pl.ds(base, 24), :]
            weights = flat[pl.ds(base + 24, 8), :]
            quarter = (flat[pl.ds(base + 32, 8), :].astype(jnp.int32) >> 7) & 3
            weights = jnp.concatenate(
                [jnp.where(quarter == q, weights, 0.0) for q in range(4)], axis=0
            )
            values_head = values.astype(BF16).astype(F32)
            weights_head = weights.astype(BF16).astype(F32)
            left = jnp.concatenate(
                [
                    values_head,
                    values - values_head,
                    weights_head,
                    weights - weights_head,
                    jnp.zeros((16, LO), F32),
                ],
                axis=0,
            )
            turned = nt_dot(move_of(slot), left.astype(BF16)).astype(BF16)
            both = jnp.dot(turned, expand[...], preferred_element_type=F32)
            here = pl.ds(pl.multiple_of(slot * LO, LO), LO)
            for k in range(8):
                products[k, here, :] = both[:, 0:LO] * both[:, (k + 1) * LO : (k + 2) * LO]

    zeros = jnp.zeros((64, LO), F32)

    @pl.loop(0, 8192 // 64)
    def _(i):
        for acc in accs:
            acc[pl.ds(pl.multiple_of(i * 64, 64), 64), :] = zeros

    copy.wait()
    listed = indices.reshape((LO + 8) * LO)

    @pl.loop(0, CAP)
    def _(slot):
        unroll = 8

        @pl.loop(0, (listed[LO * LO + slot * 8] + (unroll - 1)) // unroll)
        def _(chunk):
            for u in range(unroll):
                source = chunk * unroll + u
                for k in range(8):
                    acc = accs[k % ACCS]
                    place = listed[slot * 8 * LO + chunk * unroll + (k * LO + u)]
                    acc[pl.ds(place, 1), :] = (
                        acc[pl.ds(place, 1), :] + products[k, pl.ds(slot * LO + source, 1), :]
                    )

    fetch.wait()

    @pl.loop(0, HI // 8, unroll=4)
    def _(i):
        turned = []
        for half in range(2):
            begin = pl.multiple_of(i * 256 + half * LO, LO)
            total = accs[0][pl.ds(begin, LO), :]
            for acc in accs[1:]:
                total = total + acc[pl.ds(begin, LO), :]
            turned.append(total.T)
        here = pl.ds(pl.multiple_of(i * 8, 8), 8)
        tau = step[here, :]
        for channel in range(CH):
            cells = slice(channel * 4, channel * 4 + 4)
            gained = jnp.concatenate([turned[0][cells], turned[1][cells]], axis=0)
            out[channel, here, :] = held[channel, here, :] - tau * gained


def final_kernel(partial, first, rest, step, before, after, edge, out, ready, sem):
    steps = 16
    wide = HI // steps

    def copy_of(i):
        here = pl.ds(pl.multiple_of(i * wide, wide), wide)
        return pltpu.make_async_copy(ready.at[:, here, :], out.at[:, here, :], sem.at[i])

    def block(i):
        here = pl.ds(pl.multiple_of(i * wide, wide), wide)
        tau = step[here, :]
        for field in range(FIELDS):
            channels = [s * FIELDS + field for s in range(LOCAL)]
            others = [
                first[c, here, :] if c < FIRST else rest[c - FIRST, here, :] for c in channels
            ]
            for t in range(LOCAL):
                total = None
                for s in range(LOCAL):
                    if s == t:
                        continue
                    term = (ROTOR_RATE * spectra_entry(s - t + LOCAL)) * others[s]
                    total = term if total is None else total + term
                channel = channels[t]
                ready[channel, here, :] = partial[channel, here, :] - tau * total

    @pl.loop(0, steps)
    def _(i):
        block(i)

        @pl.when(i == 0)
        def _():
            for channel in range(CH):
                ready[channel, :16, :] += edge[0] * before[channel]

        @pl.when(i == steps - 1)
        def _():
            for channel in range(CH):
                ready[channel, HI - 16 :, :] += edge[1] * after[channel]

        copy_of(i).start()

    for i in range(steps):
        copy_of(i).wait()


def shards(
    adjoint,
    gradient,
    jacobian,
    coupling,
    pseudo_step,
    receptor_cell,
    donor_owner,
    donor_cell,
    donor_weight,
    block_count,
):
    swap = [(0, 1), (1, 0)]
    blocks = lax.axis_size("xl") * lax.axis_size("zc")
    cells = adjoint.reshape(CH, HI, LO)
    planes = adjoint.reshape(CH, 16, 16, LO)
    vmem = pl.BlockSpec(memory_space=pltpu.VMEM)
    smem = pl.BlockSpec(memory_space=pltpu.SMEM)
    hbm = pl.BlockSpec(memory_space=pltpu.HBM)

    first = lax.ppermute(cells[:FIRST], "inst", swap)
    payload, top, bottom = pl.pallas_call(
        pick_kernel,
        out_shape=[
            jax.ShapeDtypeStruct((SLOT, ROWS), F32),
            jax.ShapeDtypeStruct((CH, 16, LO), F32),
            jax.ShapeDtypeStruct((CH, 16, LO), F32),
        ],
        in_specs=[smem] + [hbm] * 5,
        out_specs=[vmem] * 3,
        scratch_shapes=[
            pltpu.VMEM((CH, HI, LO), F32),
            pltpu.VMEM((1, ROWS), jnp.int32),
            pltpu.VMEM((1, ROWS), jnp.int32),
            pltpu.VMEM((8, ROWS), jnp.int32),
            pltpu.VMEM((8, ROWS), F32),
            pltpu.SemaphoreType.DMA((FIELDS,)),
            pltpu.SemaphoreType.DMA((4,)),
        ],
        compiler_params=pltpu.CompilerParams(vmem_limit_bytes=56 * 2**20),
        cost_estimate=takes(5),
        name="pick",
    )(
        block_count.reshape(8),
        cells,
        receptor_cell.reshape(1, ROWS),
        donor_owner.reshape(1, ROWS),
        donor_cell.reshape(8, ROWS),
        donor_weight.reshape(8, ROWS),
    )
    got = lax.ppermute(payload, "xl", swap)
    rest, got, first = lax.optimization_barrier((cells[FIRST:], got, first))
    rest = lax.ppermute(rest, "inst", swap)

    message = pl.pallas_call(
        pack_kernel,
        out_shape=jax.ShapeDtypeStruct((NEAR * 2 * PIECE, LO), F32),
        in_specs=[smem, vmem, vmem],
        out_specs=vmem,
        scratch_shapes=[pltpu.VMEM((NEAR * 2 * PIECE + SPARE, LO), F32)],
        compiler_params=pltpu.CompilerParams(vmem_limit_bytes=32 * 2**20),
        cost_estimate=takes(3),
        name="pack",
    )(lax.axis_index("xl").astype(jnp.int32).reshape(1), payload, got)
    message, gradient, top, bottom = lax.optimization_barrier((message, gradient, top, bottom))
    arrived = lax.all_to_all(
        message.reshape(-1), ("sys", "zc"), split_axis=0, concat_axis=0, tiled=True
    )
    before = lax.ppermute(top, ("xl", "zc"), [(i, i + 1) for i in range(blocks - 1)])
    after = lax.ppermute(bottom, ("xl", "zc"), [(i + 1, i) for i in range(blocks - 1)])

    steps = 4
    wide = 16 // steps
    partial, edge = pl.pallas_call(
        local_kernel,
        grid=(steps,),
        out_shape=[
            jax.ShapeDtypeStruct((CH, 16, 16, LO), F32),
            jax.ShapeDtypeStruct((2, 16, LO), F32),
        ],
        in_specs=[
            pl.BlockSpec((CH, wide, 16, LO), lambda i: (0, i, 0, 0)),
            pl.BlockSpec((CH, 1, 16, LO), lambda i: (0, jnp.maximum(wide * i - 1, 0), 0, 0)),
            pl.BlockSpec((CH, 1, 16, LO), lambda i: (0, jnp.minimum(wide * i + wide, 15), 0, 0)),
            pl.BlockSpec((CH, wide, 16, LO), lambda i: (0, i, 0, 0)),
            pl.BlockSpec((FIELDS, FIELDS, wide, 16, LO), lambda i: (0, 0, i, 0, 0)),
            pl.BlockSpec((6, wide, 16, LO), lambda i: (0, i, 0, 0)),
            pl.BlockSpec((wide, 16, LO), lambda i: (i, 0, 0)),
        ],
        out_specs=[
            pl.BlockSpec((CH, wide, 16, LO), lambda i: (0, i, 0, 0)),
            pl.BlockSpec((2, 16, LO), lambda i: (0, 0, 0)),
        ],
        compiler_params=pltpu.CompilerParams(vmem_limit_bytes=56 * 2**20),
        cost_estimate=takes(6),
        name="local",
    )(
        planes,
        planes,
        planes,
        gradient.reshape(CH, 16, 16, LO),
        jacobian.reshape(FIELDS, FIELDS, 16, 16, LO),
        coupling.reshape(6, 16, 16, LO),
        pseudo_step.reshape(16, 16, LO),
    )

    arrived, partial = lax.optimization_barrier((arrived, partial))
    tau = pseudo_step.reshape(HI, LO)
    partial = pl.pallas_call(
        fringe_kernel,
        out_shape=jax.ShapeDtypeStruct((CH, HI, LO), F32),
        in_specs=[vmem, hbm, vmem],
        out_specs=vmem,
        scratch_shapes=[pltpu.VMEM((8192 + SPARE, LO), F32)] * ACCS
        + [
            pltpu.VMEM((LO * PIECE + SPARE, LO), F32),
            pltpu.VMEM((CAP * SLOT, LO), F32),
            pltpu.VMEM((LO, 9 * LO), BF16),
            pltpu.VMEM((LO, LO), jnp.int32),
            pltpu.VMEM((LO + 8, LO), jnp.int32),
            pltpu.SMEM((LO + 8, LO), jnp.int32),
            pltpu.VMEM((8, CAP * LO + SPARE, LO), F32),
            pltpu.VMEM((CH, HI, LO), F32),
            pltpu.SemaphoreType.DMA,
            pltpu.SemaphoreType.DMA,
        ],
        compiler_params=pltpu.CompilerParams(vmem_limit_bytes=50 * 2**20),
        cost_estimate=takes(25),
        name="fringe",
    )(arrived.reshape(128 * PIECE, LO), partial.reshape(CH, HI, LO), tau)

    result = pl.pallas_call(
        final_kernel,
        out_shape=jax.ShapeDtypeStruct((CH, HI, LO), F32),
        in_specs=[vmem] * 7,
        out_specs=pl.BlockSpec(memory_space=pl.ANY),
        scratch_shapes=[pltpu.VMEM((CH, HI, LO), F32), pltpu.SemaphoreType.DMA((16,))],
        compiler_params=pltpu.CompilerParams(vmem_limit_bytes=40 * 2**20),
        cost_estimate=takes(2),
        name="final",
    )(partial, first, rest, tau, before, after, edge)
    return result.reshape(adjoint.shape)


def solution(mesh):
    fine = Mesh(mesh.devices.reshape(4, 2, 16, 2), ("sys", "xl", "zc", "inst"))
    blk = ("xl", "zc")
    return jax.shard_map(
        shards,
        mesh=fine,
        in_specs=(
            P("sys", "inst", None, blk, None, None),
            P("sys", "inst", None, blk, None, None),
            P("sys", None, None, blk, None, None),
            P("sys", None, blk, None, None),
            P("sys", blk, None, None),
            P("sys", blk, None),
            P("sys", blk, None, None),
            P("sys", blk, None, None),
            P("sys", blk, None, None),
            P("sys", blk, None),
        ),
        out_specs=P("sys", "inst", None, blk, None, None),
        check_vma=False,
    )
```

```python
import math

import jax
import jax.numpy as jnp
from jax import lax
from jax.experimental import pallas as pl
from jax.experimental.pallas import tpu as pltpu
from jax.sharding import Mesh, PartitionSpec as P

ROTOR_RATE = 0.6
F32 = jnp.float32
BF16 = jnp.bfloat16

FIELDS = 5
INSTANCES = 8
LOCAL = 4
CH = LOCAL * FIELDS
HI = 256
LO = 128
ROWS = 1024
CAP = 16
SLOT = 40
NEAR = 64
PIECE = CAP * SLOT // LO
FIRST = 3
ACCS = 8
SPARE = 16


def spectra_entry(offset):
    offset %= INSTANCES
    if offset == 0:
        return 0.0
    angle = math.pi * offset / INSTANCES
    return 0.5 * (-1.0) ** offset * math.cos(angle) / math.sin(angle)


def iota(shape, dim):
    return lax.broadcasted_iota(jnp.int32, shape, dim)


def split(x):
    head = x.astype(BF16)
    return head, (x - head.astype(F32)).astype(BF16)


def takes(microseconds):
    return pl.CostEstimate(flops=0, bytes_accessed=microseconds * 3_700_000, transcendentals=0)


def nt_dot(a, b):
    return lax.dot_general(a, b, (((1,), (1,)), ((), ())), preferred_element_type=F32)


def pick_kernel(counts, *refs):
    (cells, *small), (payload, top, bottom) = refs[:5], refs[5:8]
    adj, cell, owner, donor, weight, sem, small_sem = refs[8:]

    def chunk_copy(i):
        here = pl.ds(i * LOCAL, LOCAL)
        return pltpu.make_async_copy(cells.at[here], adj.at[here], sem.at[i])

    copies = [
        pltpu.make_async_copy(operand, place, small_sem.at[i])
        for i, (operand, place) in enumerate(zip(small, (cell, owner, donor, weight)))
    ]
    for copy in copies:
        copy.start()
    for i in range(FIELDS):
        chunk_copy(i).start()
    for copy in copies:
        copy.wait()
    for i in range(FIELDS):
        chunk_copy(i).wait()
    spot = cell[...]
    high = (spot >> 7) & 127
    low = ((spot >> 14) << 7) | (spot & 127)
    lefts = []
    for channel in range(CH):
        whole = adj[channel]
        head, tail = split(jnp.concatenate([whole[:LO], whole[LO:]], axis=1))
        lefts.append(jnp.concatenate([head, tail], axis=1))
    left = jnp.concatenate(lefts, axis=0)
    wide = 256
    for part in range(ROWS // wide):
        cols = slice(part * wide, (part + 1) * wide)
        lows = jnp.where(iota((2 * LO, wide), 0) == low[:, cols], 1.0, 0.0).astype(BF16)
        lows = jnp.concatenate([lows, lows], axis=0)
        here = iota((LO, wide), 0) == high[:, cols]
        found = jnp.dot(left, lows, preferred_element_type=F32)
        for channel in range(CH):
            payload[channel : channel + 1, cols] = jnp.sum(
                jnp.where(here, found[channel * LO : (channel + 1) * LO], 0.0),
                axis=0,
                keepdims=True,
            )
    for group in range(ROWS // LO):
        lanes = slice(group * LO, (group + 1) * LO)
        living = iota((1, LO), 1) < counts[group]
        payload[CH : CH + 1, lanes] = jnp.where(living, owner[:, lanes], -1).astype(F32)
    payload[CH + 1 : 24, :] = jnp.zeros((23 - CH, ROWS), F32)
    payload[24:32, :] = weight[...]
    payload[32:40, :] = donor[...].astype(F32)
    for channel in range(CH):
        top[channel] = adj[channel, HI - 16 :, :]
        bottom[channel] = adj[channel, :16, :]


def pack_kernel(position, own, got, message, spread):
    upto = jnp.where(iota((LO, LO), 0) <= iota((LO, LO), 1), 1.0, 0.0).astype(BF16)
    ones = jnp.ones((LO, LO), BF16)
    for half, payload in enumerate((own, got)):
        rows = payload[...]
        name = rows[CH : CH + 1].astype(jnp.int32)
        near = ((name >> 4) & 1) == position[0]
        name = jnp.where((name >= 0) & near, ((name >> 5) << 4) | (name & 15), -1)
        before = jnp.zeros((NEAR, LO), F32)
        chosen, ranks = [], []
        for group in range(ROWS // LO):
            lanes = slice(group * LO, (group + 1) * LO)
            hit = jnp.where(iota((NEAR, LO), 0) == name[:, lanes], 1.0, 0.0)
            hit16 = hit.astype(BF16)
            count = jnp.dot(hit16, upto, preferred_element_type=F32) + before
            before = before + jnp.dot(hit16, ones, preferred_element_type=F32)
            ranks.append(jnp.sum(hit * count, axis=0, keepdims=True) - 1.0)
            chosen.append(hit16)
        chosen = jnp.concatenate(chosen, axis=1)
        rank = jnp.concatenate(ranks, axis=1)
        placed = jnp.concatenate(
            [jnp.where(rank == float(slot), rows, 0.0) for slot in range(CAP)], axis=0
        )
        head, tail = split(placed)
        table = nt_dot(head, chosen) + nt_dot(tail, chosen)
        for piece in range(PIECE):
            block = table[piece * LO : (piece + 1) * LO].T
            spread[pl.ds(half * PIECE + piece, NEAR, stride=2 * PIECE), :] = block
    message[...] = spread[: NEAR * 2 * PIECE, :]


def local_kernel(adj, below, above, gradient, jacobian, coupling, step, out, edge):
    planes = step.shape[0]
    rows = planes * 16
    index = pl.program_id(0)
    last = pl.num_programs(0) - 1
    y = iota((rows, LO), 0) % 16
    z = iota((rows, LO), 1)
    faces = [coupling[d].reshape(rows, LO) for d in range(6)]
    faces[2] = jnp.where(y == 15, 0.0, faces[2])
    faces[3] = jnp.where(y == 0, 0.0, faces[3])
    faces[4] = jnp.where(z == LO - 1, 0.0, faces[4])
    faces[5] = jnp.where(z == 0, 0.0, faces[5])
    tau = step[...].reshape(rows, LO)

    @pl.when(index == 0)
    def _():
        edge[0] = (tau * faces[1])[:16]

    @pl.when(index == last)
    def _():
        edge[1] = (tau * faces[0])[-16:]

    for field in range(FIELDS):
        blocks = [jacobian[g, field].reshape(rows, LO) for g in range(FIELDS)]
        mine = [
            adj[t * FIELDS + field].reshape(rows, LO) for t in range(LOCAL)
        ]
        for t in range(LOCAL):
            channel = t * FIELDS + field
            own = mine[t]
            total = -gradient[channel].reshape(rows, LO)
            for g in range(FIELDS):
                total = total + blocks[g] * adj[t * FIELDS + g].reshape(rows, LO)
            next_plane = jnp.where(index == last, 0.0, above[channel, 0])
            past_plane = jnp.where(index == 0, 0.0, below[channel, 0])
            total = total - faces[0] * jnp.concatenate([own[16:], next_plane], axis=0)
            total = total - faces[1] * jnp.concatenate([past_plane, own[:-16]], axis=0)
            total = total - faces[2] * pltpu.roll(own, rows - 1, 0)
            total = total - faces[3] * pltpu.roll(own, 1, 0)
            total = total - faces[4] * pltpu.roll(own, LO - 1, 1)
            total = total - faces[5] * pltpu.roll(own, 1, 1)
            for s in range(LOCAL):
                if s != t:
                    total = total + (ROTOR_RATE * spectra_entry(s - t)) * mine[s]
            out[channel] = (own - tau * total).reshape(planes, 16, LO)


def fringe_kernel(rows, partial, step, out, *scratch):
    accs = scratch[:ACCS]
    spread, flat, expand, order, places, indices, products, held, sem, held_sem = scratch[ACCS:]
    fetch = pltpu.make_async_copy(partial, held, held_sem)
    fetch.start()
    spread[: LO * PIECE, :] = rows[...]
    for piece in range(PIECE):
        flat[pl.ds(piece * LO, LO), :] = spread[pl.ds(piece, LO, stride=PIECE), :].T

    weights = jnp.concatenate(
        [flat[slot * SLOT + 24 : slot * SLOT + 32, :] for slot in range(CAP)], axis=0
    )
    alive = jnp.where(weights > 0.0, 1.0, 0.0)
    upto = jnp.where(iota((LO, LO), 0) <= iota((LO, LO), 1), 1.0, 0.0).astype(BF16)
    rank = jnp.dot(alive.astype(BF16), upto, preferred_element_type=F32) * alive - 1.0
    order[...] = rank.astype(jnp.int32)
    places[LO : LO + 8, :] = nt_dot(jnp.ones((8, LO), BF16), alive.astype(BF16)).astype(jnp.int32)

    def move_of(slot):
        target = order[pl.ds(pl.multiple_of(slot * 8, 8), 1), :]
        return jnp.where(iota((LO, LO), 0) == target, 1.0, 0.0).astype(BF16)

    @pl.loop(0, CAP // 4)
    def _(four):
        for i in range(4):
            slot = four * 4 + i
            spot = flat[pl.ds(pl.multiple_of(slot * SLOT, 8) + 32, 8), :]
            head = spot.astype(BF16).astype(F32)
            both = jnp.concatenate([head, spot - head], axis=0).astype(BF16)
            both = nt_dot(both, move_of(slot))
            spot = (both[:8] + both[8:]).astype(jnp.int32)
            places[pl.ds(pl.multiple_of(slot * 8, 8), 8), :] = ((spot >> 9) << 7) | (spot & 127)

    copy = pltpu.make_async_copy(places, indices, sem)
    copy.start()

    row = iota((LO, LO), 0)
    lane = iota((LO, LO), 1)
    value_row = jnp.where(row < 24, row, row - 24)
    hit = (row < 48) & (value_row == lane // 4)
    expand[:, 0:LO] = jnp.where(hit, 1.0, 0.0).astype(BF16)
    weight_row = jnp.where(row < 80, row - 48, row - 80)
    for k in range(8):
        hit = (row >= 48) & (row < 112) & (weight_row == (lane % 4) * 8 + k)
        expand[:, (k + 1) * LO : (k + 2) * LO] = jnp.where(hit, 1.0, 0.0).astype(BF16)

    @pl.loop(0, CAP // 4)
    def _(four):
        for i in range(4):
            slot = four * 4 + i
            base = pl.multiple_of(slot * SLOT, 8)
            values = flat[pl.ds(base, 24), :]
            weights = flat[pl.ds(base + 24, 8), :]
            quarter = (flat[pl.ds(base + 32, 8), :].astype(jnp.int32) >> 7) & 3
            weights = jnp.concatenate(
                [jnp.where(quarter == q, weights, 0.0) for q in range(4)], axis=0
            )
            values_head = values.astype(BF16).astype(F32)
            weights_head = weights.astype(BF16).astype(F32)
            left = jnp.concatenate(
                [
                    values_head,
                    values - values_head,
                    weights_head,
                    weights - weights_head,
                    jnp.zeros((16, LO), F32),
                ],
                axis=0,
            )
            turned = nt_dot(move_of(slot), left.astype(BF16)).astype(BF16)
            both = jnp.dot(turned, expand[...], preferred_element_type=F32)
            here = pl.ds(pl.multiple_of(slot * LO, LO), LO)
            for k in range(8):
                products[k, here, :] = both[:, 0:LO] * both[:, (k + 1) * LO : (k + 2) * LO]

    zeros = jnp.zeros((64, LO), F32)

    @pl.loop(0, 8192 // 64)
    def _(i):
        for acc in accs:
            acc[pl.ds(pl.multiple_of(i * 64, 64), 64), :] = zeros

    copy.wait()
    listed = indices.reshape((LO + 8) * LO)

    @pl.loop(0, CAP)
    def _(slot):
        unroll = 8

        @pl.loop(0, (listed[LO * LO + slot * 8] + (unroll - 1)) // unroll)
        def _(chunk):
            for u in range(unroll):
                source = chunk * unroll + u
                for k in range(8):
                    acc = accs[k % ACCS]
                    place = listed[slot * 8 * LO + chunk * unroll + (k * LO + u)]
                    acc[pl.ds(place, 1), :] = (
                        acc[pl.ds(place, 1), :] + products[k, pl.ds(slot * LO + source, 1), :]
                    )

    fetch.wait()

    @pl.loop(0, HI // 8, unroll=4)
    def _(i):
        turned = []
        for half in range(2):
            begin = pl.multiple_of(i * 256 + half * LO, LO)
            total = accs[0][pl.ds(begin, LO), :]
            for acc in accs[1:]:
                total = total + acc[pl.ds(begin, LO), :]
            turned.append(total.T)
        here = pl.ds(pl.multiple_of(i * 8, 8), 8)
        tau = step[here, :]
        for channel in range(CH):
            cells = slice(channel * 4, channel * 4 + 4)
            gained = jnp.concatenate([turned[0][cells], turned[1][cells]], axis=0)
            out[channel, here, :] = held[channel, here, :] - tau * gained


def final_kernel(partial, first, rest, step, before, after, edge, out, ready, sem):
    steps = 4
    wide = HI // steps

    def copy_of(i):
        here = pl.ds(pl.multiple_of(i * wide, wide), wide)
        return pltpu.make_async_copy(ready.at[:, here, :], out.at[:, here, :], sem.at[i])

    def block(i):
        here = pl.ds(pl.multiple_of(i * wide, wide), wide)
        tau = step[here, :]
        for field in range(FIELDS):
            channels = [s * FIELDS + field for s in range(LOCAL)]
            others = [
                first[c, here, :] if c < FIRST else rest[c - FIRST, here, :] for c in channels
            ]
            for t in range(LOCAL):
                total = None
                for s in range(LOCAL):
                    if s == t:
                        continue
                    term = (ROTOR_RATE * spectra_entry(s - t + LOCAL)) * others[s]
                    total = term if total is None else total + term
                channel = channels[t]
                ready[channel, here, :] = partial[channel, here, :] - tau * total

    @pl.loop(0, steps)
    def _(i):
        block(i)

        @pl.when(i == 0)
        def _():
            for channel in range(CH):
                ready[channel, :16, :] += edge[0] * before[channel]

        @pl.when(i == steps - 1)
        def _():
            for channel in range(CH):
                ready[channel, HI - 16 :, :] += edge[1] * after[channel]

        copy_of(i).start()

    for i in range(steps):
        copy_of(i).wait()


def shards(
    adjoint,
    gradient,
    jacobian,
    coupling,
    pseudo_step,
    receptor_cell,
    donor_owner,
    donor_cell,
    donor_weight,
    block_count,
):
    swap = [(0, 1), (1, 0)]
    blocks = lax.axis_size("xl") * lax.axis_size("zc")
    cells = adjoint.reshape(CH, HI, LO)
    planes = adjoint.reshape(CH, 16, 16, LO)
    vmem = pl.BlockSpec(memory_space=pltpu.VMEM)
    smem = pl.BlockSpec(memory_space=pltpu.SMEM)
    hbm = pl.BlockSpec(memory_space=pltpu.HBM)

    first = lax.ppermute(cells[:FIRST], "inst", swap)
    payload, top, bottom = pl.pallas_call(
        pick_kernel,
        out_shape=[
            jax.ShapeDtypeStruct((SLOT, ROWS), F32),
            jax.ShapeDtypeStruct((CH, 16, LO), F32),
            jax.ShapeDtypeStruct((CH, 16, LO), F32),
        ],
        in_specs=[smem] + [hbm] * 5,
        out_specs=[vmem] * 3,
        scratch_shapes=[
            pltpu.VMEM((CH, HI, LO), F32),
            pltpu.VMEM((1, ROWS), jnp.int32),
            pltpu.VMEM((1, ROWS), jnp.int32),
            pltpu.VMEM((8, ROWS), jnp.int32),
            pltpu.VMEM((8, ROWS), F32),
            pltpu.SemaphoreType.DMA((FIELDS,)),
            pltpu.SemaphoreType.DMA((4,)),
        ],
        compiler_params=pltpu.CompilerParams(vmem_limit_bytes=56 * 2**20),
        cost_estimate=takes(5),
        name="pick",
    )(
        block_count.reshape(8),
        cells,
        receptor_cell.reshape(1, ROWS),
        donor_owner.reshape(1, ROWS),
        donor_cell.reshape(8, ROWS),
        donor_weight.reshape(8, ROWS),
    )
    got = lax.ppermute(payload, "xl", swap)
    rest, got, first = lax.optimization_barrier((cells[FIRST:], got, first))
    rest = lax.ppermute(rest, "inst", swap)

    message = pl.pallas_call(
        pack_kernel,
        out_shape=jax.ShapeDtypeStruct((NEAR * 2 * PIECE, LO), F32),
        in_specs=[smem, vmem, vmem],
        out_specs=vmem,
        scratch_shapes=[pltpu.VMEM((NEAR * 2 * PIECE + SPARE, LO), F32)],
        compiler_params=pltpu.CompilerParams(vmem_limit_bytes=32 * 2**20),
        cost_estimate=takes(3),
        name="pack",
    )(lax.axis_index("xl").astype(jnp.int32).reshape(1), payload, got)
    message, gradient, top, bottom = lax.optimization_barrier((message, gradient, top, bottom))
    arrived = lax.all_to_all(
        message.reshape(-1), ("sys", "zc"), split_axis=0, concat_axis=0, tiled=True
    )
    before = lax.ppermute(top, ("xl", "zc"), [(i, i + 1) for i in range(blocks - 1)])
    after = lax.ppermute(bottom, ("xl", "zc"), [(i + 1, i) for i in range(blocks - 1)])

    steps = 4
    wide = 16 // steps
    partial, edge = pl.pallas_call(
        local_kernel,
        grid=(steps,),
        out_shape=[
            jax.ShapeDtypeStruct((CH, 16, 16, LO), F32),
            jax.ShapeDtypeStruct((2, 16, LO), F32),
        ],
        in_specs=[
            pl.BlockSpec((CH, wide, 16, LO), lambda i: (0, i, 0, 0)),
            pl.BlockSpec((CH, 1, 16, LO), lambda i: (0, jnp.maximum(wide * i - 1, 0), 0, 0)),
            pl.BlockSpec((CH, 1, 16, LO), lambda i: (0, jnp.minimum(wide * i + wide, 15), 0, 0)),
            pl.BlockSpec((CH, wide, 16, LO), lambda i: (0, i, 0, 0)),
            pl.BlockSpec((FIELDS, FIELDS, wide, 16, LO), lambda i: (0, 0, i, 0, 0)),
            pl.BlockSpec((6, wide, 16, LO), lambda i: (0, i, 0, 0)),
            pl.BlockSpec((wide, 16, LO), lambda i: (i, 0, 0)),
        ],
        out_specs=[
            pl.BlockSpec((CH, wide, 16, LO), lambda i: (0, i, 0, 0)),
            pl.BlockSpec((2, 16, LO), lambda i: (0, 0, 0)),
        ],
        compiler_params=pltpu.CompilerParams(vmem_limit_bytes=56 * 2**20),
        cost_estimate=takes(6),
        name="local",
    )(
        planes,
        planes,
        planes,
        gradient.reshape(CH, 16, 16, LO),
        jacobian.reshape(FIELDS, FIELDS, 16, 16, LO),
        coupling.reshape(6, 16, 16, LO),
        pseudo_step.reshape(16, 16, LO),
    )

    arrived, partial = lax.optimization_barrier((arrived, partial))
    tau = pseudo_step.reshape(HI, LO)
    partial = pl.pallas_call(
        fringe_kernel,
        out_shape=jax.ShapeDtypeStruct((CH, HI, LO), F32),
        in_specs=[vmem, hbm, vmem],
        out_specs=vmem,
        scratch_shapes=[pltpu.VMEM((8192 + SPARE, LO), F32)] * ACCS
        + [
            pltpu.VMEM((LO * PIECE + SPARE, LO), F32),
            pltpu.VMEM((CAP * SLOT, LO), F32),
            pltpu.VMEM((LO, 9 * LO), BF16),
            pltpu.VMEM((LO, LO), jnp.int32),
            pltpu.VMEM((LO + 8, LO), jnp.int32),
            pltpu.SMEM((LO + 8, LO), jnp.int32),
            pltpu.VMEM((8, CAP * LO + SPARE, LO), F32),
            pltpu.VMEM((CH, HI, LO), F32),
            pltpu.SemaphoreType.DMA,
            pltpu.SemaphoreType.DMA,
        ],
        compiler_params=pltpu.CompilerParams(vmem_limit_bytes=50 * 2**20),
        cost_estimate=takes(25),
        name="fringe",
    )(arrived.reshape(128 * PIECE, LO), partial.reshape(CH, HI, LO), tau)

    result = pl.pallas_call(
        final_kernel,
        out_shape=jax.ShapeDtypeStruct((CH, HI, LO), F32),
        in_specs=[vmem] * 7,
        out_specs=pl.BlockSpec(memory_space=pl.ANY),
        scratch_shapes=[pltpu.VMEM((CH, HI, LO), F32), pltpu.SemaphoreType.DMA((8,))],
        compiler_params=pltpu.CompilerParams(vmem_limit_bytes=40 * 2**20),
        cost_estimate=takes(2),
        name="final",
    )(partial, first, rest, tau, before, after, edge)
    return result.reshape(adjoint.shape)


def solution(mesh):
    fine = Mesh(mesh.devices.reshape(4, 2, 16, 2), ("sys", "xl", "zc", "inst"))
    blk = ("xl", "zc")
    return jax.shard_map(
        shards,
        mesh=fine,
        in_specs=(
            P("sys", "inst", None, blk, None, None),
            P("sys", "inst", None, blk, None, None),
            P("sys", None, None, blk, None, None),
            P("sys", None, blk, None, None),
            P("sys", blk, None, None),
            P("sys", blk, None),
            P("sys", blk, None, None),
            P("sys", blk, None, None),
            P("sys", blk, None, None),
            P("sys", blk, None),
        ),
        out_specs=P("sys", "inst", None, blk, None, None),
        check_vma=False,
    )
```
